128 devices in a mesh: dp: 8 (over x, z_hi), seq: 16 (over z_lo, y, core).
Axes of the slice: x: 4, y: 4, z: 4 (z_hi: 2, z_lo: 2; z = z_hi * 2 + z_lo), core: 2. Of those that a mesh axis runs over, the one named last changes fastest.
Arguments:
- grad_seq: bfloat16 [8, 4096, 8192], P('dp', 'seq'), may hold values from -6 to 6
- features: bfloat16 [8, 1024, 5120], P('dp', 'seq'), may hold values from -6 to 6
- merger_norm_gain: float32 [1280], replicated, may hold values from 0.25 to 1.75
- w_in: bfloat16 [5120, 3072], P(None, 'dp'), may hold values from -0.078125 to 0.078125
- b_in: float32 [3072], P('dp'), may hold values from -3 to 3
- w_out: bfloat16 [3072, 8192], P('dp'), may hold values from -0.0625 to 0.0625
- image_counts: int32 [8, 64], P('dp'), may hold values from 1 to 16, as said below
- sample_owner: int32 [8, 64], P('dp'), may hold values from 0 to 15, as said below
- image_starts: int32 [8, 64], P('dp'), may hold values from 0 to 4095, as said below
Outputs:
- merger_input_gradient: bfloat16 [8, 1024, 5120], P('dp', 'seq')
- grad_w1: bfloat16 [5120, 3072], P('seq', 'dp')
- grad_w2: bfloat16 [3072, 8192], P('dp', 'seq')
The draws below stay inside these ranges and needn't reach their ends.
Inputs may be any that keep to these rules, and one draw needn't show every extreme that they name: `sample_owner`: in each group each owner has exactly 4 samples, no two of them in the same sequence shard. `image_counts`: in each group the counts of one owner's samples sum to at most 64, exactly 64 for some owner; the image tokens within one sequence shard of 256 tokens number at most 64, exactly 64 in some shard. `image_starts`: Samples' image tokens occupy disjoint ranges of the sequence in increasing sample order, each range inside one sequence shard of 256 tokens.
All inputs are finite; a program needn't handle non-finite values.
Results may differ from the reference program's by a relative error of at most 0.024.
Values may be sent and summed in bfloat16 or wider, within the bound.
A program may use at most 128 MiB of HBM per device.

```python
import jax
import jax.numpy as jnp
from jax import lax

D = 8192
VW = 1280
MERGER_WIDTH = 5120
HM = 3072
OWNER_SLOT_LIMIT = 64
TOK_DEV = 256
SPO = 4
SEQLEN = 4096
N_DP = 8
N_SEQ = 16


def layout(key):
    base = jax.random.fold_in(key, 11)
    quarter = OWNER_SLOT_LIMIT // 4

    def one_group(group_key):
        keys = jax.random.split(group_key, 5)
        order = jax.random.permutation(keys[0], N_SEQ).astype(jnp.int32)
        fullest = jax.random.randint(keys[1], (), 0, N_SEQ).astype(jnp.int32)
        picked_owner = jax.random.randint(keys[2], (), 0, N_SEQ).astype(jnp.int32)
        shard = jnp.arange(N_SEQ, dtype=jnp.int32)[:, None]
        column = jnp.arange(SPO, dtype=jnp.int32)[None, :]
        owners = order[(shard + column) % N_SEQ].astype(jnp.int32)
        counts = jax.random.randint(keys[3], (N_SEQ, SPO), 1, quarter + 1).astype(jnp.int32)
        counts = jnp.where((shard == fullest) | (owners == picked_owner), quarter, counts).astype(jnp.int32)
        weights = jax.random.randint(keys[4], (N_SEQ, SPO + 1), 1, 9).astype(jnp.int32)
        spare = TOK_DEV - jnp.sum(counts, axis=1)
        gaps = spare[:, None] * weights // jnp.sum(weights, axis=1, keepdims=True)
        starts = shard * TOK_DEV + jnp.cumsum(gaps[:, :SPO], axis=1) + jnp.cumsum(counts, axis=1) - counts
        return (counts.reshape(-1).astype(jnp.int32), owners.reshape(-1).astype(jnp.int32), starts.reshape(-1).astype(jnp.int32))
    return jax.vmap(one_group)(jax.random.split(base, N_DP))


def draw_image_counts(key, part):
    return layout(key)[0]


def draw_sample_owner(key, part):
    return layout(key)[1]


def draw_image_starts(key, part):
    return layout(key)[2]


def shard_levels(rng, dims, cuts, low, largest):
    gain, own = 1.0, jax.random.fold_in(rng, 6)
    for axis_at, blocks in cuts:
        heights = jnp.exp(jax.random.uniform(jax.random.fold_in(own, axis_at), (blocks,), jnp.float32, low / len(cuts), largest / len(cuts)))
        gain = gain * jnp.repeat(heights, dims[axis_at] // blocks).reshape([-1 if axis == axis_at else 1 for axis in range(len(dims))])
    return gain


def gaussian(own_key, shape, spread, most, pieces=(), kind=jnp.bfloat16):
    loudness = shard_levels(own_key, shape, pieces, -0.22, 0.18) if pieces else 1.0
    entries = jax.random.normal(own_key, shape, jnp.float32) * spread * loudness
    return jnp.minimum(jnp.maximum(entries, -most), most).astype(kind)


def setup_inputs(seed: int = 0) -> dict:
    key_of = jax.random.split(jax.random.key(seed), 10)
    return {
        "grad_seq": gaussian(key_of[0], (N_DP, SEQLEN, D), 1.0, 6.0, ((0, 8), (1, 16))),
        "features": gaussian(key_of[1], (N_DP, N_SEQ * OWNER_SLOT_LIMIT, MERGER_WIDTH), 1.0, 6.0, ((0, 8), (1, 16))),
        "merger_norm_gain": jnp.clip(1.0 + 0.15 * jax.random.normal(key_of[2], (VW,), jnp.float32), 0.25, 1.75),
        "w_in": gaussian(key_of[3], (MERGER_WIDTH, HM), MERGER_WIDTH ** -0.5, 0.078125, ((1, 8),)),
        "b_in": gaussian(key_of[4], (HM,), 0.7, 3.0, ((0, 8),), jnp.float32),
        "w_out": gaussian(key_of[5], (HM, D), D ** -0.5, 0.0625, ((0, 8),)),
        "image_counts": draw_image_counts(jax.random.fold_in(key_of[9], 71), 0),
        "sample_owner": draw_sample_owner(jax.random.fold_in(key_of[9], 71), 0),
        "image_starts": draw_image_starts(jax.random.fold_in(key_of[9], 71), 0),
    }


EPS = 1e-06

def slot_positions(counts_row, owner_row, starts_row, owners, capacity):
    chosen = owner_row[None, :] == jnp.arange(owners, dtype=jnp.int32)[:, None]
    taken = jnp.where(chosen, counts_row[None, :], 0).astype(jnp.int32)
    before = (jnp.cumsum(taken, axis=1) - taken).astype(jnp.int32)
    slots = jnp.arange(capacity, dtype=jnp.int32)
    inside = chosen[:, None, :] & (slots[None, :, None] >= before[:, None, :]) & (slots[None, :, None] < (before + taken)[:, None, :])
    located = jnp.where(inside, starts_row[None, None, :] + slots[None, :, None] - before[:, None, :], 0)
    return jnp.where(jnp.any(inside, axis=2), lax.optimization_barrier(jnp.sum(located, axis=2)), -1).astype(jnp.int32)

def normal_cdf(value):
    return 0.5 * (1.0 + jax.scipy.special.erf(value * 0.7071067811865476))

def normal_pdf(value):
    return jnp.exp(-0.5 * value * value) * 0.3989422804014327

def layer_normalize(rows, gain_vector):
    feature_count = rows.shape[0]
    vectors = rows.astype(jnp.float32).reshape(feature_count, 4, -1)
    subtract_mean = vectors - lax.optimization_barrier(jnp.mean(vectors, axis=2, keepdims=True))
    inverse_deviation = lax.rsqrt(lax.optimization_barrier(jnp.mean(subtract_mean * subtract_mean, axis=2, keepdims=True)) + EPS)
    standardized_input = subtract_mean * inverse_deviation
    normalized_rows = (standardized_input * gain_vector).reshape(feature_count, -1).astype(jnp.bfloat16)
    return (normalized_rows, standardized_input, inverse_deviation)

def apply_norm_gain(normalized_gradient, standardized_input, inverse_deviation, gain_vector):
    feature_count = normalized_gradient.shape[0]
    gain_scaled = normalized_gradient.reshape(feature_count, 4, -1) * gain_vector
    mean_removed = gain_scaled - lax.optimization_barrier(jnp.mean(gain_scaled, axis=2, keepdims=True)) - standardized_input * lax.optimization_barrier(jnp.mean(gain_scaled * standardized_input, axis=2, keepdims=True))
    return (mean_removed * inverse_deviation).reshape(feature_count, -1)

def pick_rows(sequence, index):
    return jnp.take(sequence, index, axis=0)

def reference(grad_seq, features, merger_norm_gain, w_in, b_in, w_out, image_counts, sample_owner, image_starts):

    def positions_of(counts_row, owner_row, starts_row):
        return slot_positions(counts_row, owner_row, starts_row, N_SEQ, OWNER_SLOT_LIMIT)
    positions = jax.vmap(positions_of)(image_counts, sample_owner, image_starts).reshape(N_DP, N_SEQ * OWNER_SLOT_LIMIT)
    picked = jax.vmap(pick_rows)(grad_seq, jnp.maximum(positions, 0))
    returned = jnp.where(positions[:, :, None] >= 0, picked, jnp.zeros((), jnp.bfloat16)).astype(jnp.bfloat16)
    returned = returned.reshape(N_DP * N_SEQ * OWNER_SLOT_LIMIT, D)
    normalized_rows, standardized_input, inverse_deviation = layer_normalize(features.reshape(N_DP * N_SEQ * OWNER_SLOT_LIMIT, MERGER_WIDTH), merger_norm_gain)
    pre = jnp.dot(normalized_rows, w_in, preferred_element_type=jnp.float32) + b_in
    activated = (pre * normal_cdf(pre)).astype(jnp.bfloat16)
    slope = normal_cdf(pre) + pre * normal_pdf(pre)
    grad_hidden = jnp.dot(returned, w_out.T, preferred_element_type=jnp.float32)
    grad_pre = (grad_hidden * slope).astype(jnp.bfloat16)
    normalized_gradient = jnp.dot(grad_pre, w_in.T, preferred_element_type=jnp.float32)
    merger_input_gradient = apply_norm_gain(normalized_gradient, standardized_input, inverse_deviation, merger_norm_gain).astype(jnp.bfloat16)
    grad_w1 = jnp.dot(normalized_rows.T, grad_pre, preferred_element_type=jnp.float32).astype(jnp.bfloat16)
    grad_w2 = jnp.dot(activated.T, returned, preferred_element_type=jnp.float32).astype(jnp.bfloat16)
    return (merger_input_gradient.reshape(N_DP, N_SEQ * OWNER_SLOT_LIMIT, MERGER_WIDTH), grad_w1, grad_w2)
```

```python
import functools

import jax
import jax.numpy as jnp
from jax import lax
from jax.experimental import pallas as pl
from jax.experimental.pallas import tpu as pltpu
from jax.sharding import PartitionSpec as P

EPS = 1e-06
MESH = pl.DeviceIdType.MESH
BF = jnp.bfloat16
F32 = jnp.float32
D = 8192
MW = 5120
VW = 1280
HID = 384
SLOTS = 64
TOK = 256
HALF = 32
CW = 2048
NT_DIMS = (((1,), (1,)), ((), ()))
TN_DIMS = (((0,), (0,)), ((), ()))


def slot_positions(counts_row, owner_row, starts_row, owners, capacity):
    chosen = owner_row[None, :] == jnp.arange(owners, dtype=jnp.int32)[:, None]
    taken = jnp.where(chosen, counts_row[None, :], 0)
    before = jnp.cumsum(taken, axis=1) - taken
    slots = jnp.arange(capacity, dtype=jnp.int32)
    inside = (
        chosen[:, None, :]
        & (slots[None, :, None] >= before[:, None, :])
        & (slots[None, :, None] < (before + taken)[:, None, :])
    )
    located = jnp.where(
        inside, starts_row[None, None, :] + slots[None, :, None] - before[:, None, :], 0
    )
    return jnp.where(jnp.any(inside, axis=2), jnp.sum(located, axis=2), -1)


def normal_cdf(value):
    return 0.5 * (1.0 + lax.erf(value * 0.7071067811865476))


def normal_pdf(value):
    return jnp.exp(-0.5 * value * value) * 0.3989422804014327


class Place:
    def __init__(self):
        d = lax.axis_index("dp")
        s = lax.axis_index("seq")
        self.x, self.zh = lax.div(d, 2), lax.rem(d, 2)
        self.zl, self.y, self.c = lax.div(s, 8), lax.rem(lax.div(s, 2), 4), lax.rem(s, 2)
        self.XP = self.dev(x=self.xs(1))
        self.XM = self.dev(x=self.xs(3))
        self.YP = self.dev(y=self.ys(1))
        self.YM = self.dev(y=self.ys(3))
        self.ZX = self.dev(zh=1 - self.zh, zl=1 - self.zl)
        self.ZL = self.dev(zl=1 - self.zl)
        self.CO = self.dev(c=1 - self.c)

    def xs(self, k):
        return lax.rem(self.x + k, 4)

    def ys(self, k):
        return lax.rem(self.y + k, 4)

    def dev(self, **kw):
        g = lambda n: kw.get(n, getattr(self, n))
        return (g("x") * 2 + g("zh"), g("zl") * 8 + g("y") * 2 + g("c"))

    def barrier(self):
        bar = pltpu.get_barrier_semaphore()
        everyone = (self.XP, self.XM, self.YP, self.YM, self.ZX, self.ZL, self.CO)
        for to in everyone:
            pl.semaphore_signal(bar, inc=1, device_id=to, device_id_type=MESH)
        pl.semaphore_wait(bar, len(everyone))


class Copies:
    def __init__(self, send, recv):
        self.send, self.recv, self.all = send, recv, []

    def __call__(self, src, dst, to):
        i = len(self.all)
        cp = pltpu.make_async_remote_copy(
            src_ref=src, dst_ref=dst, send_sem=self.send.at[i], recv_sem=self.recv.at[i],
            device_id=to, device_id_type=MESH,
        )
        cp.start()
        self.all.append(cp)
        return cp

    def finish(self):
        for cp in self.all:
            cp.wait_send()


class Gather:
    def __init__(self, pc, copy, buf, lo, w, z_first):
        self.pc, self.copy, self.buf, self.z_first = pc, copy, buf, z_first
        self.cols = pl.ds(lo, w)

    def blk(self, k, z, r=slice(None)):
        return self.buf.at[self.pc.xs(k) * 2 + z, r, self.cols]

    def to(self, ref, where):
        return self.copy(ref, ref, where)

    def s1(self):
        pc = self.pc
        own = self.blk(0, pc.zh)
        if self.z_first:
            self.z = self.to(own, pc.ZX)
        self.p, self.m = self.to(own, pc.XP), self.to(own, pc.XM)
        if not self.z_first:
            self.z = self.to(own, pc.ZX)

    def relay(self, z):
        pc = self.pc
        return [
            self.to(self.blk(3, z, pl.ds(0, HALF)), pc.XP),
            self.to(self.blk(1, z, pl.ds(HALF, HALF)), pc.XM),
        ]

    def s2(self):
        pc = self.pc
        if self.z_first:
            self.z.wait_recv()
            other = self.blk(0, 1 - pc.zh)
            self.zp, self.zm = self.to(other, pc.XP), self.to(other, pc.XM)
        else:
            self.p.wait_recv()
            self.m.wait_recv()
            self.r = self.relay(pc.zh)
            self.f = [self.to(self.blk(3, pc.zh), pc.ZX), self.to(self.blk(1, pc.zh), pc.ZX)]

    def s3(self):
        pc = self.pc
        if self.z_first:
            self.p.wait_recv()
            self.m.wait_recv()
            self.r = self.relay(pc.zh)
        else:
            for cp in self.r:
                cp.wait_recv()
            self.f.append(self.to(self.blk(2, pc.zh), pc.ZX))

    def s4(self):
        if self.z_first:
            self.zp.wait_recv()
            self.zm.wait_recv()
            self.r += self.relay(1 - self.pc.zh)

    def s5(self):
        for cp in self.r if self.z_first else [self.z] + self.f:
            cp.wait_recv()


def gather_kernel(
    pack_ref, route_ref, gain_ref, b_ref, gs_hbm, feat_hbm, win_hbm, wout_hbm,
    rt_hbm, nt_hbm, act_ref, gp_ref,
    gs, feat, win, wout, g, hb, hc, hz, rt, nt, pre, gh,
    send, recv, lsem,
):
    pc = Place()
    copy = Copies(send, recv)
    nc = D // CW
    cut = lambda i: pl.ds(i * CW, CW)
    loads = [
        pltpu.make_async_copy(gs_hbm.at[:, cut(i)], gs.at[:, cut(i)], lsem.at[i]) for i in range(nc)
    ]
    load_feat = pltpu.make_async_copy(feat_hbm, feat, lsem.at[nc])
    load_win = pltpu.make_async_copy(win_hbm, win, lsem.at[nc + 1])
    load_wout = pltpu.make_async_copy(wout_hbm, wout, lsem.at[nc + 2])
    loads[0].start()
    load_feat.start()
    for i in range(1, nc):
        loads[i].start()
    load_win.start()
    load_wout.start()
    stores = []

    def store(src, dst):
        cp = pltpu.make_async_copy(src, dst, lsem.at[nc + 3 + len(stores)])
        cp.start()
        stores.append(cp)

    me = pc.x * 2 + pc.zh
    pc.barrier()
    yp, ym, rp, rm, co, zl = ([None] * nc for _ in range(6))

    def pack(i):
        loads[i].wait()
        g[pc.y, :, cut(i)] = jnp.dot(
            pack_ref[...], gs[:, cut(i)], preferred_element_type=F32
        ).astype(BF)
        own = g.at[pc.y, :, cut(i)]
        yp[i] = copy(own, own, pc.YP)
        ym[i] = copy(own, own, pc.YM)

    def ring(i):
        yp[i].wait_recv()
        up = g.at[pc.ys(3), pl.ds(0, HALF), cut(i)]
        rp[i] = copy(up, up, pc.YP)
        ym[i].wait_recv()
        down = g.at[pc.ys(1), pl.ds(HALF, HALF), cut(i)]
        rm[i] = copy(down, down, pc.YM)

    def route(i):
        rp[i].wait_recv()
        rm[i].wait_recv()
        for j in range(CW // 512):
            cols = pl.ds(i * CW + j * 512, 512)
            hb[:, cols] = jnp.dot(
                route_ref[...], g[:, :, cols].reshape(4 * SLOTS, 512), preferred_element_type=F32
            ).astype(BF)
        co[i] = copy(hb.at[pl.ds(128, 128), cut(i)], hc.at[:, cut(i)], pc.CO)

    def across(i):
        co[i].wait_recv()
        hb[0:128, cut(i)] = hb[0:128, cut(i)] + hc[:, cut(i)]
        zl[i] = copy(hb.at[pl.ds(64, 64), cut(i)], hz.at[:, cut(i)], pc.ZL)

    def arrive(i):
        zl[i].wait_recv()
        rt[me, :, cut(i)] = hb[0:64, cut(i)] + hz[:, cut(i)]
        cs[i].s1()

    ns = [
        Gather(pc, copy, nt, 0, 3072, True),
        Gather(pc, copy, nt, 3072, 2048, False),
    ]
    cs = [Gather(pc, copy, rt, i * CW, CW, i % 2 == 0) for i in range(nc)]

    def normalize():
        load_feat.wait()
        for p in range(4):
            cols = slice(p * VW, (p + 1) * VW)
            v = feat[:, cols].astype(F32)
            d = v - jnp.mean(v, axis=1, keepdims=True)
            inv = lax.rsqrt(jnp.mean(d * d, axis=1, keepdims=True) + EPS)
            nt[me, :, cols] = (d * inv * gain_ref[...]).astype(BF)

    def contract(total, rows, weights, lo, w, dims, by):
        def step(k, _):
            cols = pl.ds(pl.multiple_of(lo + k * by, by), by)
            a = rows[:, :, cols].reshape(8 * SLOTS, by)
            b = weights[:, cols] if dims is NT_DIMS else weights[cols, :]
            if dims is NT_DIMS:
                total[...] += lax.dot_general(a, b, NT_DIMS, preferred_element_type=F32)
            else:
                total[...] += jnp.dot(a, b, preferred_element_type=F32)
            return 0

        lax.fori_loop(0, w // by, step, 0)

    def hidden(i):
        cs[i].s5()
        store(rt.at[:, :, cut(i)], rt_hbm.at[:, :, cut(i)])
        contract(gh, rt, wout, i * CW, CW, NT_DIMS, 1024)

    pack(0)
    pack(1)
    normalize()
    ns[0].s1()
    ns[1].s1()
    ring(0)
    pack(2)
    ring(1)
    route(0)
    pack(3)
    ns[0].s2()
    across(0)
    ring(2)
    route(1)
    arrive(0)
    across(1)
    ns[1].s2()
    ring(3)
    route(2)
    arrive(1)
    across(2)
    ns[0].s3()
    cs[0].s2()
    route(3)
    arrive(2)
    across(3)
    ns[1].s3()
    ns[0].s4()
    arrive(3)
    cs[1].s2()
    cs[0].s3()
    cs[2].s2()
    ns[0].s5()
    ns[1].s5()
    store(nt, nt_hbm)
    cs[0].s4()
    cs[1].s3()
    load_win.wait()
    pre[...] = jnp.broadcast_to(b_ref[...], pre.shape)
    gh[...] = jnp.zeros_like(gh)
    contract(pre, nt, win, 0, MW, None, 512)
    load_wout.wait()
    hidden(0)
    cs[2].s3()
    cs[3].s2()

    def activate(k, _):
        rows = pl.ds(pl.multiple_of(k * 64, 64), 64)
        v = pre[rows, :]
        cdf = normal_cdf(v)
        act_ref[rows, :] = (v * cdf).astype(BF)
        pre[rows, :] = cdf + v * normal_pdf(v)
        return 0

    lax.fori_loop(0, 8, activate, 0)
    hidden(1)
    cs[2].s4()
    cs[3].s3()
    hidden(2)
    hidden(3)

    def finish(k, _):
        rows = pl.ds(pl.multiple_of(k * 64, 64), 64)
        gp_ref[rows, :] = (gh[rows, :] * pre[rows, :]).astype(BF)
        return 0

    lax.fori_loop(0, 8, finish, 0)
    copy.finish()
    for cp in stores:
        cp.wait()


K1_COPIES = 100


def gather_call(pack, route, gain, bias, gs, feat, win, wout):
    vm = pl.BlockSpec(memory_space=pltpu.VMEM)
    hb = pl.BlockSpec(memory_space=pl.ANY)
    return pl.pallas_call(
        gather_kernel,
        out_shape=(
            jax.ShapeDtypeStruct((8, SLOTS, D), BF),
            jax.ShapeDtypeStruct((8, SLOTS, MW), BF),
            jax.ShapeDtypeStruct((8 * SLOTS, HID), BF),
            jax.ShapeDtypeStruct((8 * SLOTS, HID), BF),
        ),
        in_specs=[vm, vm, vm, vm, hb, hb, hb, hb],
        out_specs=(hb, hb, vm, vm),
        scratch_shapes=[
            pltpu.VMEM((TOK, D), BF),
            pltpu.VMEM((SLOTS, MW), BF),
            pltpu.VMEM((MW, HID), BF),
            pltpu.VMEM((HID, D), BF),
            pltpu.VMEM((4, SLOTS, D), BF),
            pltpu.VMEM((4 * SLOTS, D), BF),
            pltpu.VMEM((2 * SLOTS, D), BF),
            pltpu.VMEM((SLOTS, D), BF),
            pltpu.VMEM((8, SLOTS, D), BF),
            pltpu.VMEM((8, SLOTS, MW), BF),
            pltpu.VMEM((8 * SLOTS, HID), F32),
            pltpu.VMEM((8 * SLOTS, HID), F32),
            pltpu.SemaphoreType.DMA((K1_COPIES,)),
            pltpu.SemaphoreType.DMA((K1_COPIES,)),
            pltpu.SemaphoreType.DMA((16,)),
        ],
        compiler_params=pltpu.CompilerParams(
            collective_id=0, has_side_effects=True, vmem_limit_bytes=60 * 2**20
        ),
        cost_estimate=pl.CostEstimate(
            flops=2 * 512 * 384 * 13312, bytes_accessed=30 * 2**20, transcendentals=400000
        ),
        name="gather_rows",
    )(pack, route, gain, bias, gs, feat, win, wout)


class InputScatter:
    def __init__(self, pc, copy, gn, xa, xb, zr, fin, lo, w, x_first):
        self.pc, self.copy, self.gn, self.xa, self.xb, self.zr, self.fin = pc, copy, gn, xa, xb, zr, fin
        self.cols, self.x_first = pl.ds(lo, w), x_first
        self.zs = pl.ds(0, 2) if x_first else pl.ds(pc.zh, 1)

    def s1(self):
        pc, c, gn = self.pc, self.cols, self.gn
        if self.x_first:
            self.first()
        else:
            self.z = self.copy(gn.at[:, 1 - pc.zh, :, c], self.zr.at[:, :, c], pc.ZX)

    def first(self):
        pc, c, gn = self.pc, self.cols, self.gn
        far = pc.xs(2)
        self.a = [
            self.copy(gn.at[far, self.zs, pl.ds(0, HALF), c], self.xa.at[0, self.zs, :, c], pc.XP),
            self.copy(gn.at[far, self.zs, pl.ds(HALF, HALF), c], self.xa.at[1, self.zs, :, c], pc.XM),
        ]

    def second(self):
        pc, c, gn = self.pc, self.cols, self.gn
        self.b = []
        for d, (k, to) in enumerate(((1, pc.XP), (3, pc.XM))):
            self.a[d].wait_recv()
            rows = pl.ds(d * HALF, HALF)
            gn[pc.xs(k), self.zs, rows, c] = gn[pc.xs(k), self.zs, rows, c] + self.xa[d, self.zs, :, c]
            self.b.append(self.copy(gn.at[pc.xs(k), self.zs, :, c], self.xb.at[d, self.zs, :, c], to))

    def s2(self):
        pc, c, gn = self.pc, self.cols, self.gn
        if self.x_first:
            self.second()
        else:
            self.z.wait_recv()
            for k in (2, 1, 3, 0):
                gn[pc.xs(k), pc.zh, :, c] = gn[pc.xs(k), pc.zh, :, c] + self.zr[pc.xs(k), :, c]
                if k == 2:
                    self.first()

    def total(self, z):
        c = self.cols
        return (
            self.gn[self.pc.x, z, :, c].astype(F32)
            + self.xb[0, z, :, c].astype(F32)
            + self.xb[1, z, :, c].astype(F32)
        )

    def s3(self):
        pc, c, gn = self.pc, self.cols, self.gn
        if self.x_first:
            for cp in self.b:
                cp.wait_recv()
            gn[pc.x, 1 - pc.zh, :, c] = self.total(1 - pc.zh).astype(BF)
            self.z = self.copy(gn.at[pc.x, 1 - pc.zh, :, c], self.zr.at[0, :, c], pc.ZX)
        else:
            self.second()

    def s4(self):
        c = self.cols
        if self.x_first:
            self.z.wait_recv()
            self.fin[:, c] = self.total(self.pc.zh) + self.zr[0, :, c].astype(F32)
        else:
            for cp in self.b:
                cp.wait_recv()
            self.fin[:, c] = self.total(self.pc.zh)


class WeightScatter:
    def __init__(self, pc, copy, w, cr, ya, yb, zr, out):
        self.pc, self.copy, self.w, self.cr, self.ya, self.yb, self.zr, self.out = (
            pc, copy, w, cr, ya, yb, zr, out
        )
        self.half = w.shape[3] // 2
        self.co = {}

    def to_core(self, k):
        pc = self.pc
        y = pc.ys(k)
        self.co[k] = self.copy(self.w.at[1 - pc.c, y], self.cr.at[y], pc.CO)

    def add_core(self, k):
        pc = self.pc
        y = pc.ys(k)
        self.co[k].wait_recv()
        for z in range(2):
            self.w[pc.c, y, z] = self.w[pc.c, y, z] + self.cr[y, z]

    def first(self):
        pc, h = self.pc, self.half
        self.add_core(2)
        far = self.w.at[pc.c, pc.ys(2)]
        self.a = [
            self.copy(far.at[:, pl.ds(0, h)], self.ya.at[0], pc.YP),
            self.copy(far.at[:, pl.ds(h, h)], self.ya.at[1], pc.YM),
        ]

    def second(self):
        pc, h = self.pc, self.half
        self.b = []
        for d, (k, to) in enumerate(((1, pc.YP), (3, pc.YM))):
            y = pc.ys(k)
            rows = pl.ds(d * h, h)
            self.add_core(k)
            self.a[d].wait_recv()
            for z in range(2):
                self.w[pc.c, y, z, rows] = self.w[pc.c, y, z, rows] + self.ya[d, z]
            self.b.append(self.copy(self.w.at[pc.c, y], self.yb.at[d], to))

    def total(self, z):
        pc = self.pc
        return (
            self.w[pc.c, pc.y, z].astype(F32)
            + self.yb[0, z].astype(F32)
            + self.yb[1, z].astype(F32)
        )

    def third(self):
        pc = self.pc
        self.add_core(0)
        for cp in self.b:
            cp.wait_recv()
        self.w[pc.c, pc.y, 1 - pc.zl] = self.total(1 - pc.zl).astype(BF)
        self.z = self.copy(self.w.at[pc.c, pc.y, 1 - pc.zl], self.zr, pc.ZL)

    def last(self):
        self.z.wait_recv()
        self.out[...] = (self.total(self.pc.zl) + self.zr[...].astype(F32)).astype(BF)


def scatter_kernel(
    gain_ref, act_ref, gp_ref, rt_hbm, nt_hbm, win_hbm, feat_hbm,
    mig_ref, gw1_ref, gw2_ref,
    rt, nt, win, feat, act_t, gn, xa, xb, zr, fin,
    w2, cr2, ya2, yb2, zr2, w1, cr1, ya1, yb1, zr1,
    send, recv, lsem,
):
    pc = Place()
    copy = Copies(send, recv)
    load_win = pltpu.make_async_copy(win_hbm, win, lsem.at[0])
    load_rt = pltpu.make_async_copy(rt_hbm, rt, lsem.at[1])
    load_nt = pltpu.make_async_copy(nt_hbm, nt, lsem.at[2])
    load_feat = pltpu.make_async_copy(feat_hbm, feat, lsem.at[3])
    for cp in (load_win, load_rt, load_nt, load_feat):
        cp.start()
    pc.barrier()

    gw = 1024
    gs = [
        InputScatter(pc, copy, gn, xa, xb, zr, fin, j * gw, gw, j % 2 == 0) for j in range(MW // gw)
    ]
    load_win.wait()
    for j in (1, 0, 3, 2, 4):
        def tile(k, _, j=j):
            at = pl.multiple_of(j * gw + k * 512, 512)
            gn[:, :, :, pl.ds(at, 512)] = (
                lax.dot_general(gp_ref[...], win[pl.ds(at, 512), :], NT_DIMS, preferred_element_type=F32)
                .astype(BF).reshape(4, 2, SLOTS, 512)
            )
            return 0

        lax.fori_loop(0, gw // 512, tile, 0)
        gs[j].s1()

    s2 = WeightScatter(pc, copy, w2, cr2, ya2, yb2, zr2, gw2_ref)
    s1 = WeightScatter(pc, copy, w1, cr1, ya1, yb1, zr1, gw1_ref)
    act_t[...] = act_ref[...].T
    load_rt.wait()

    def grad2(c, k):
        y = pc.ys(k)

        def tile(z, _):
            cols = pl.ds(pl.multiple_of((z * 8 + y * 2 + c) * 512, 512), 512)
            w2[c, y, z] = jnp.dot(
                act_t[...], rt[:, :, cols].reshape(8 * SLOTS, 512), preferred_element_type=F32
            ).astype(BF)
            return 0

        lax.fori_loop(0, 2, tile, 0)

    def grad1(k):
        y = pc.ys(k)

        def tile(z, _):
            cols = pl.ds(pl.multiple_of((z * 4 + y) * 640, 128), 640)
            part = lax.dot_general(
                nt[:, :, cols].reshape(8 * SLOTS, 640), gp_ref[...], TN_DIMS, preferred_element_type=F32
            ).astype(BF)
            w1[0, y, z] = part[0:320]
            w1[1, y, z] = part[320:640]
            return 0

        lax.fori_loop(0, 2, tile, 0)

    for k in (2, 1, 3, 0):
        grad2(1 - pc.c, k)
        s2.to_core(k)
        if k == 1:
            gs[0].s2()
            gs[1].s2()
    grad2(pc.c, 2)
    s2.first()
    gs[3].s2()
    gs[2].s2()
    grad2(pc.c, 1)
    grad2(pc.c, 3)
    grad2(pc.c, 0)
    gs[1].s3()
    gs[0].s3()
    gs[4].s2()
    load_nt.wait()
    for k in (2, 1):
        grad1(k)
        s1.to_core(k)
    s2.second()
    gs[3].s3()
    gs[2].s3()
    s1.first()
    for k in (3, 0):
        grad1(k)
        s1.to_core(k)
    gs[4].s3()
    s1.second()
    gs[0].s4()
    gs[1].s4()
    s2.third()
    gs[3].s4()
    gs[2].s4()
    gs[4].s4()
    load_feat.wait()
    for p in range(4):
        cols = slice(p * VW, (p + 1) * VW)
        v = feat[:, cols].astype(F32)
        d = v - jnp.mean(v, axis=1, keepdims=True)
        inv = lax.rsqrt(jnp.mean(d * d, axis=1, keepdims=True) + EPS)
        xhat = d * inv
        t = fin[:, cols] * gain_ref[...]
        mig_ref[:, cols] = (
            (t - jnp.mean(t, axis=1, keepdims=True) - xhat * jnp.mean(t * xhat, axis=1, keepdims=True)) * inv
        ).astype(BF)
    s1.third()
    s2.last()
    s1.last()
    copy.finish()


K2_COPIES = 60


def scatter_call(gain, act, gp, rt, nt, win, feat):
    vm = pl.BlockSpec(memory_space=pltpu.VMEM)
    hb = pl.BlockSpec(memory_space=pl.ANY)
    return pl.pallas_call(
        scatter_kernel,
        out_shape=(
            jax.ShapeDtypeStruct((SLOTS, MW), BF),
            jax.ShapeDtypeStruct((320, HID), BF),
            jax.ShapeDtypeStruct((HID, 512), BF),
        ),
        in_specs=[vm, vm, vm, hb, hb, hb, hb],
        out_specs=(vm, vm, vm),
        scratch_shapes=[
            pltpu.VMEM((8, SLOTS, D), BF),
            pltpu.VMEM((8, SLOTS, MW), BF),
            pltpu.VMEM((MW, HID), BF),
            pltpu.VMEM((SLOTS, MW), BF),
            pltpu.VMEM((HID, 8 * SLOTS), BF),
            pltpu.VMEM((4, 2, SLOTS, MW), BF),
            pltpu.VMEM((2, 2, HALF, MW), BF),
            pltpu.VMEM((2, 2, SLOTS, MW), BF),
            pltpu.VMEM((4, SLOTS, MW), BF),
            pltpu.VMEM((SLOTS, MW), F32),
            pltpu.VMEM((2, 4, 2, HID, 512), BF),
            pltpu.VMEM((4, 2, HID, 512), BF),
            pltpu.VMEM((2, 2, HID // 2, 512), BF),
            pltpu.VMEM((2, 2, HID, 512), BF),
            pltpu.VMEM((HID, 512), BF),
            pltpu.VMEM((2, 4, 2, 320, HID), BF),
            pltpu.VMEM((4, 2, 320, HID), BF),
            pltpu.VMEM((2, 2, 160, HID), BF),
            pltpu.VMEM((2, 2, 320, HID), BF),
            pltpu.VMEM((320, HID), BF),
            pltpu.SemaphoreType.DMA((K2_COPIES,)),
            pltpu.SemaphoreType.DMA((K2_COPIES,)),
            pltpu.SemaphoreType.DMA((4,)),
        ],
        compiler_params=pltpu.CompilerParams(
            collective_id=1, has_side_effects=True, vmem_limit_bytes=62 * 2**20
        ),
        cost_estimate=pl.CostEstimate(
            flops=2 * 512 * 384 * 18432, bytes_accessed=30 * 2**20, transcendentals=400
        ),
        name="scatter_sums",
    )(gain, act, gp, rt, nt, win, feat)


def local(
    grad_seq, features, merger_norm_gain, w_in, b_in, w_out, image_counts, sample_owner, image_starts
):
    seq_index = lax.axis_index("seq")
    zl, y, c = seq_index // 8, (seq_index // 2) % 4, seq_index % 2
    counts, owner, starts = image_counts[0], sample_owner[0], image_starts[0]
    wanted = slot_positions(counts, owner, starts, 16, SLOTS)
    packing = slot_positions(counts, starts // TOK, starts, 16, SLOTS)
    mine = lax.dynamic_index_in_dim(packing, seq_index, 0, False)
    places = seq_index * TOK + jnp.arange(TOK, dtype=jnp.int32)
    pack = (mine[:, None] == places[None, :]).astype(BF)
    want = lax.dynamic_index_in_dim(wanted.reshape(2, 4, 2, SLOTS), y, 1, False)
    pair = lambda a, i: jnp.concatenate(
        [lax.dynamic_index_in_dim(a, i, 0), lax.dynamic_index_in_dim(a, 1 - i, 0)], axis=0
    )
    want = pair(pair(want, zl).transpose(1, 0, 2), c).reshape(-1)
    held = lax.dynamic_index_in_dim(packing.reshape(2, 4, 2, SLOTS), zl, 0, False)
    held = lax.dynamic_index_in_dim(held, c, 1, False).reshape(-1)
    route = ((want[:, None] == held[None, :]) & (want >= 0)[:, None]).astype(BF)
    gain = merger_norm_gain[None, :]
    feat = features[0]
    rt, nt, act, gp = gather_call(pack, route, gain, b_in[None, :], grad_seq[0], feat, w_in, w_out)
    mig, gw1, gw2 = scatter_call(gain, act, gp, rt, nt, w_in, feat)
    return (mig[None], gw1, gw2)


def solution(mesh):
    in_specs = (
        P("dp", "seq", None),
        P("dp", "seq", None),
        P(),
        P(None, "dp"),
        P("dp"),
        P("dp", None),
        P("dp", None),
        P("dp", None),
        P("dp", None),
    )
    out_specs = (P("dp", "seq", None), P("seq", "dp"), P("dp", "seq"))
    return jax.shard_map(local, mesh=mesh, in_specs=in_specs, out_specs=out_specs, check_vma=False)
```

```python
import jax
import jax.numpy as jnp
from jax import lax
from jax.experimental import pallas as pl
from jax.experimental.pallas import tpu as pltpu
from jax.sharding import PartitionSpec as P

EPS = 1e-06
MESH = pl.DeviceIdType.MESH
BF = jnp.bfloat16
F32 = jnp.float32
I32 = jnp.int32
D = 8192
MW = 5120
VW = 1280
HID = 384
HH = HID // 2
SLOTS = 64
TOK = 256
ROWS = 512
HALF = 32
BW = 512
CW = 1024
GW = 640
NT_DIMS = (((1,), (1,)), ((), ()))
TN_DIMS = (((0,), (0,)), ((), ()))
N_KINDS = "ABAA"
C_KINDS = "BABABABA"
G_KINDS = "ABAABABA"
ORDER = (
    ("norm", 0), ("norm", 1), ("norm", 2), ("norm", 3), ("pack", 0), ("pack", 1), ("pack", 2), ("N3", 0),
    ("N2", 0), ("ring", 0), ("pack", 3), ("N2", 1), ("ring", 1), ("pack", 4), ("N3", 2), ("N2", 2),
    ("ring", 2), ("pack", 5), ("route", 0), ("N3", 3), ("N2", 3), ("across", 0), ("ring", 3), ("pack", 6),
    ("route", 1), ("across", 1), ("arrive", 0), ("N4", 0), ("ring", 4), ("pack", 7), ("N3", 1), ("route", 2),
    ("across", 2), ("arrive", 1), ("ring", 5), ("route", 3), ("N4", 2), ("across", 3), ("arrive", 2),
    ("N5", 1), ("pre", 1), ("ring", 6), ("route", 4), ("C2", 1), ("across", 4), ("arrive", 3), ("N4", 3),
    ("ring", 7), ("route", 5), ("C2", 0), ("route", 6), ("arrive", 4), ("C2", 3), ("N5", 0), ("pre", 0),
    ("route", 7), ("across", 5), ("C3", 1), ("across", 6), ("across", 7), ("N5", 2), ("pre", 2),
    ("arrive", 5), ("C2", 2), ("arrive", 6), ("C4", 1), ("C2", 5), ("arrive", 7), ("C3", 3), ("N5", 3),
    ("pre", 3), ("act", 0), ("C3", 0), ("C2", 4), ("C4", 3), ("C2", 7), ("C5", 0), ("hid", 0), ("C3", 5),
    ("C3", 2), ("C2", 6), ("C5", 1), ("w2", 0), ("hid", 1), ("C4", 5), ("C5", 2), ("hid", 2), ("w2a", 0),
    ("C3", 7), ("C3", 4), ("w2b", 0), ("C5", 3), ("w2", 1), ("hid", 3), ("C4", 7), ("C5", 4), ("hid", 4),
    ("w2a", 1), ("w2c", 0), ("C3", 6), ("C5", 5), ("w2", 2), ("w2b", 1), ("hid", 5), ("w2a", 2), ("C5", 7),
    ("hid", 7), ("C5", 6), ("hid", 6), ("gp", 0), ("gn", 0), ("w2c", 1), ("w2z", 0), ("w2", 3), ("w2b", 2),
    ("g2", 0), ("gn", 1), ("gn", 2), ("w2a", 3), ("gn", 3), ("g1", 2), ("w2s", 0), ("gn", 4), ("gn", 5),
    ("f1", 0), ("w2c", 2), ("g1", 1), ("g2", 2), ("g2", 3), ("w2b", 3), ("g2", 1), ("g1", 3), ("g2", 5),
    ("gn", 6), ("g3", 0), ("gn", 7), ("f2", 0), ("g1", 0), ("g3", 2), ("g2", 4), ("w2c", 3), ("w2z", 1),
    ("g3", 3), ("g3", 1), ("g3", 5), ("w2s", 1), ("g2", 7), ("g2", 6), ("w2o", 0), ("g3", 4), ("g4", 0),
    ("w2f", 0), ("g4", 1), ("mig", 0), ("g4", 2), ("f3", 0), ("g4", 3), ("mig", 1), ("g3", 7), ("g4", 5),
    ("g3", 6), ("g4", 4), ("mig", 2), ("g4", 7), ("g4", 6), ("mig", 3), ("f4", 0),
)
MAX_COPIES = 256


def normal_cdf(value):
    return 0.5 * (1.0 + lax.erf(value * 0.7071067811865476))


def normal_pdf(value):
    return jnp.exp(-0.5 * value * value) * 0.3989422804014327


def dot(a, b):
    return jnp.dot(a, b, preferred_element_type=F32)


class Place:
    def __init__(self):
        d = lax.axis_index("dp")
        s = lax.axis_index("seq")
        self.seq = s
        self.x, self.zh = lax.div(d, 2), lax.rem(d, 2)
        self.zl, self.y, self.c = lax.div(s, 8), lax.rem(lax.div(s, 2), 4), lax.rem(s, 2)
        self.XP = self.dev(x=self.xs(1))
        self.XM = self.dev(x=self.xs(3))
        self.YP = self.dev(y=self.ys(1))
        self.YM = self.dev(y=self.ys(3))
        self.ZX = self.dev(zh=1 - self.zh, zl=1 - self.zl)
        self.ZL = self.dev(zl=1 - self.zl)
        self.CO = self.dev(c=1 - self.c)

    def xs(self, k):
        return lax.rem(self.x + k, 4)

    def ys(self, k):
        return lax.rem(self.y + k, 4)

    def dev(self, **kw):
        g = lambda n: kw.get(n, getattr(self, n))
        return (g("x") * 2 + g("zh"), g("zl") * 8 + g("y") * 2 + g("c"))

    def barrier(self):
        bar = pltpu.get_barrier_semaphore()
        everyone = (self.XP, self.XM, self.YP, self.YM, self.ZX, self.ZL, self.CO)
        for to in everyone:
            pl.semaphore_signal(bar, inc=1, device_id=to, device_id_type=MESH)
        pl.semaphore_wait(bar, len(everyone))


class Copies:
    def __init__(self, send, recv):
        self.send, self.recv, self.all, self.sent = send, recv, [], set()

    def __call__(self, src, dst, to):
        i = len(self.all)
        cp = pltpu.make_async_remote_copy(
            src_ref=src, dst_ref=dst, send_sem=self.send.at[i], recv_sem=self.recv.at[i],
            device_id=to, device_id_type=MESH,
        )
        cp.start()
        self.all.append(cp)
        return cp

    def leave(self, copies):
        for cp in copies:
            if id(cp) not in self.sent:
                self.sent.add(id(cp))
                cp.wait_send()

    def finish(self):
        self.leave(self.all)


class Gather:
    def __init__(self, pc, copy, buf, lo, w, z_first):
        self.pc, self.copy, self.buf, self.z_first = pc, copy, buf, z_first
        self.cols = pl.ds(lo, w)

    def blk(self, k, z, r=slice(None)):
        return self.buf.at[self.pc.xs(k) * 2 + z, r, self.cols]

    def to(self, ref, where):
        return self.copy(ref, ref, where)

    def s1(self):
        pc = self.pc
        own = self.blk(0, pc.zh)
        if self.z_first:
            self.z = self.to(own, pc.ZX)
        self.p, self.m = self.to(own, pc.XP), self.to(own, pc.XM)
        if not self.z_first:
            self.z = self.to(own, pc.ZX)

    def relay(self, z):
        pc = self.pc
        return [
            self.to(self.blk(3, z, pl.ds(0, HALF)), pc.XP),
            self.to(self.blk(1, z, pl.ds(HALF, HALF)), pc.XM),
        ]

    def s2(self):
        pc = self.pc
        if self.z_first:
            self.z.wait_recv()
            other = self.blk(0, 1 - pc.zh)
            self.zp, self.zm = self.to(other, pc.XP), self.to(other, pc.XM)
        else:
            self.p.wait_recv()
            self.m.wait_recv()
            self.r = self.relay(pc.zh)
            self.f = [self.to(self.blk(3, pc.zh), pc.ZX), self.to(self.blk(1, pc.zh), pc.ZX)]

    def s3(self):
        pc = self.pc
        if self.z_first:
            self.p.wait_recv()
            self.m.wait_recv()
            self.r = self.relay(pc.zh)
        else:
            for cp in self.r:
                cp.wait_recv()
            self.f.append(self.to(self.blk(2, pc.zh), pc.ZX))

    def s4(self):
        self.zp.wait_recv()
        self.zm.wait_recv()
        self.r += self.relay(1 - self.pc.zh)

    def s5(self):
        for cp in self.r if self.z_first else [self.z] + self.f:
            cp.wait_recv()


class InputScatter:
    def __init__(self, pc, copy, gn, xa, xb, zr, fin, lo, at, w, x_first):
        self.pc, self.copy, self.gn, self.xa, self.xb, self.zr, self.fin = pc, copy, gn, xa, xb, zr, fin
        self.cols, self.at, self.x_first = pl.ds(lo, w), pl.ds(at, w), x_first
        self.zs = pl.ds(0, 2) if x_first else pl.ds(pc.zh, 1)

    def s1(self):
        pc, c = self.pc, self.cols
        if self.x_first:
            self.first()
        else:
            self.z = self.copy(self.gn.at[:, 1 - pc.zh, :, c], self.zr.at[:, :, self.at], pc.ZX)

    def first(self):
        pc, c, gn, at = self.pc, self.cols, self.gn, self.at
        far = pc.xs(2)
        self.a = [
            self.copy(gn.at[far, self.zs, pl.ds(0, HALF), c], self.xa.at[0, :, :, at], pc.XP),
            self.copy(gn.at[far, self.zs, pl.ds(HALF, HALF), c], self.xa.at[1, :, :, at], pc.XM),
        ]

    def second(self):
        pc, c, gn, at = self.pc, self.cols, self.gn, self.at
        self.b = []
        for d, (k, to) in enumerate(((1, pc.XP), (3, pc.XM))):
            self.a[d].wait_recv()
            rows = pl.ds(d * HALF, HALF)
            gn[pc.xs(k), self.zs, rows, c] = gn[pc.xs(k), self.zs, rows, c] + self.xa[d, :, :, at]
            self.b.append(self.copy(gn.at[pc.xs(k), self.zs, :, c], self.xb.at[d, :, :, at], to))

    def s2(self):
        pc, c, gn = self.pc, self.cols, self.gn
        if self.x_first:
            self.second()
        else:
            self.z.wait_recv()
            for k in (2, 1, 3, 0):
                gn[pc.xs(k), pc.zh, :, c] = gn[pc.xs(k), pc.zh, :, c] + self.zr[pc.xs(k), :, self.at]
                if k == 2:
                    self.first()

    def total(self, z):
        i = z if self.x_first else 0
        return (
            self.gn[self.pc.x, z, :, self.cols].astype(F32)
            + self.xb[0, i, :, self.at].astype(F32)
            + self.xb[1, i, :, self.at].astype(F32)
        )

    def s3(self):
        pc, c, gn = self.pc, self.cols, self.gn
        if self.x_first:
            for cp in self.b:
                cp.wait_recv()
            gn[pc.x, 1 - pc.zh, :, c] = self.total(1 - pc.zh).astype(BF)
            self.z = self.copy(gn.at[pc.x, 1 - pc.zh, :, c], self.zr.at[:, self.at], pc.ZX)
        else:
            self.second()

    def s4(self):
        if self.x_first:
            self.z.wait_recv()
            self.fin[:, self.cols] = self.total(self.pc.zh) + self.zr[:, self.at].astype(F32)
        else:
            for cp in self.b:
                cp.wait_recv()
            self.fin[:, self.cols] = self.total(self.pc.zh)


def routing_tables(pc, cnt, own, st):
    iota = lambda shape, axis: lax.broadcasted_iota(I32, shape, axis)
    one = lambda m: jnp.where(m, 1.0, 0.0).astype(BF)
    i0, i1 = iota((64, 64), 0), iota((64, 64), 1)
    col = lambda r: jnp.sum(jnp.where(i0 == i1, r, 0), axis=1, keepdims=True)
    sh = lax.div(st, TOK)
    cnt_c, own_c, st_c, sh_c = col(cnt), col(own), col(st), col(sh)
    before_o = jnp.sum(jnp.where((own_c == own) & (i0 < i1), cnt_c, 0), axis=0, keepdims=True)
    before_h = jnp.sum(jnp.where((sh_c == sh) & (i1 < i0), cnt, 0), axis=1, keepdims=True)
    off = iota((64, TOK), 1) + pc.seq * TOK - st_c
    inside = (sh_c == pc.seq) & (off >= 0) & (off < cnt_c)
    rank = jnp.sum(jnp.where(inside, before_h + off + 1, 0), axis=0, keepdims=True) - 1
    pack = one(iota((64, TOK), 0) == rank)
    r = iota((256, 64), 0)
    q, k = lax.div(r, 64), lax.rem(r, 64)
    core = pc.c + lax.div(q, 2) * (1 - 2 * pc.c)
    zl = pc.zl + lax.rem(q, 2) * (1 - 2 * pc.zl)
    off = k - before_o
    inside = (own == zl * 8 + pc.y * 2 + core) & (off >= 0) & (off < cnt)
    want = jnp.sum(jnp.where(inside, st + off + 1, 0), axis=1, keepdims=True)
    r = iota((64, 256), 1)
    off = lax.rem(r, 64) - before_h
    inside = (sh_c == pc.zl * 8 + lax.div(r, 64) * 2 + pc.c) & (off >= 0) & (off < cnt_c)
    held = jnp.sum(jnp.where(inside, st_c + off + 1, 0), axis=0, keepdims=True)
    return pack, one((want == held) & (want > 0))


def merger_kernel(
    cnt_ref, own_ref, st_ref, gain_ref, b_ref, gs_hbm, feat_hbm, win_hbm, wout_hbm,
    mig_ref, gw1_ref, gw2_ref,
    pack_m, route_m, big, feat, win, wout, g, hc, hz, rt, nt, pre, gh, act_t, gp,
    w2, cr2, ya2, yb2, ss, zr2, o2, xaa, xba, zra, xab, xbb, zrb, fin, cr1, ya1, yb1, zr1,
    send, recv, lsem,
):
    pc = Place()
    copy = Copies(send, recv)
    me = pc.x * 2 + pc.zh
    nc = D // CW
    cut = lambda i: pl.ds(i * CW, CW)
    loads = []

    def load(src, dst):
        cp = pltpu.make_async_copy(src, dst, lsem.at[len(loads)])
        cp.start()
        loads.append(cp)
        return cp

    def piece(p):
        return pl.ds(((p // 4) % 2 * 8 + p % 4 * 2 + p // 8) * BW, BW)

    lf = load(feat_hbm, feat)
    lg = [load(gs_hbm.at[:, :, :, piece(p)], big.at[0:2, :, :, pl.ds(p * BW, BW)]) for p in range(16)]
    lw = load(win_hbm, win)
    lo = [load(wout_hbm.at[:, piece(p)], wout.at[p]) for p in range(16)]
    pack_m[...], route_m[...] = routing_tables(pc, cnt_ref[...], own_ref[...], st_ref[...])
    gain = gain_ref[...].reshape(1, VW)
    pc.barrier()

    yp, ym, rp, rm, co, zl = ({} for _ in range(6))

    def do_pack(i):
        lg[2 * i].wait()
        lg[2 * i + 1].wait()
        g[pc.y, :, cut(i)] = dot(pack_m[...], big[0:2, :, :, cut(i)].reshape(TOK, CW)).astype(BF)
        own = g.at[pc.y, :, cut(i)]
        yp[i] = copy(own, own, pc.YP)
        ym[i] = copy(own, own, pc.YM)

    def do_ring(i):
        yp[i].wait_recv()
        up = g.at[pc.ys(3), pl.ds(0, HALF), cut(i)]
        rp[i] = copy(up, up, pc.YP)
        ym[i].wait_recv()
        down = g.at[pc.ys(1), pl.ds(HALF, HALF), cut(i)]
        rm[i] = copy(down, down, pc.YM)

    def do_route(i):
        rp[i].wait_recv()
        rm[i].wait_recv()
        for j in range(CW // 512):
            cols = pl.ds(i * CW + j * 512, 512)
            big[2:4, :, :, cols] = (
                dot(route_m[...], g[:, :, cols].reshape(4 * SLOTS, 512)).astype(BF).reshape(2, 2, SLOTS, 512)
            )
        co[i] = copy(big.at[3, :, :, cut(i)], hc.at[:, :, cut(i)], pc.CO)

    def do_across(i):
        co[i].wait_recv()
        big[2, :, :, cut(i)] = big[2, :, :, cut(i)] + hc[:, :, cut(i)]
        zl[i] = copy(big.at[2, 1, :, cut(i)], hz.at[:, cut(i)], pc.ZL)

    cs = [Gather(pc, copy, rt, i * CW, CW, C_KINDS[i] == "A") for i in range(nc)]
    ns = [Gather(pc, copy, nt, n * VW, VW, N_KINDS[n] == "A") for n in range(4)]

    def do_arrive(i):
        zl[i].wait_recv()
        rt[me, :, cut(i)] = big[2, 0, :, cut(i)] + hz[:, cut(i)]
        cs[i].s1()

    def standardized(n):
        v = feat[:, n * VW:(n + 1) * VW].astype(F32)
        d = v - jnp.mean(v, axis=1, keepdims=True)
        inv = lax.rsqrt(jnp.mean(d * d, axis=1, keepdims=True) + EPS)
        return d * inv, inv

    def do_norm(n):
        if n == 0:
            lf.wait()
        nt[me, :, n * VW:(n + 1) * VW] = (standardized(n)[0] * gain).astype(BF)
        ns[n].s1()

    started = []

    def do_pre(n):
        if not started:
            lw.wait()
            pre[...] = jnp.broadcast_to(b_ref[...].reshape(1, HID), pre.shape)
            started.append(n)

        def tile(k, _):
            cols = pl.ds(pl.multiple_of(n * VW + k * 256, 256), 256)
            pre[...] += dot(nt[:, :, cols].reshape(ROWS, 256), win[cols, :])
            return 0

        lax.fori_loop(0, VW // 256, tile, 0)

    def do_act(_):
        def tile(k, _):
            rows = pl.ds(pl.multiple_of(k * 128, 128), 128)
            v = pre[rows, :]
            cdf = normal_cdf(v)
            act_t[:, rows] = (v * cdf).T.astype(BF)
            pre[rows, :] = cdf + v * normal_pdf(v)
            return 0

        lax.fori_loop(0, ROWS // 128, tile, 0)

    opened = []

    def do_hid(i):
        lo[2 * i].wait()
        lo[2 * i + 1].wait()
        for p in (2 * i, 2 * i + 1):
            part = lax.dot_general(
                rt[:, :, p * BW:(p + 1) * BW].reshape(ROWS, BW), wout[p], NT_DIMS, preferred_element_type=F32
            )
            if opened:
                gh[...] += part
            else:
                gh[...] = part
                opened.append(p)

    mine = pl.ds(pl.multiple_of(pc.c * HH, HH), HH)
    theirs = pl.ds(pl.multiple_of((1 - pc.c) * HH, HH), HH)
    wc, wa, wb, wz, wo = ({} for _ in range(5))

    def do_w2(k):
        b = k % 2
        if k >= 2:
            copy.leave([wc[k - 2]] + wa[k - 2] + wb[k - 2])

        def tile(y, _):
            cols = pl.ds(pl.multiple_of(k * 4 * BW + y * BW, BW), BW)
            w2[b, y] = dot(act_t[...], rt[:, :, cols].reshape(ROWS, BW)).astype(BF)
            return 0

        lax.fori_loop(0, 4, tile, 0)
        wc[k] = copy(w2.at[b, :, theirs], cr2.at[k], pc.CO)

    def do_w2a(k):
        b, y = k % 2, pc.ys(2)
        wc[k].wait_recv()
        w2[b, y, mine] = w2[b, y, mine] + cr2[k, y]
        wa[k] = []
        for d, to in enumerate((pc.YP, pc.YM)):
            rows = pl.ds(pl.multiple_of(pc.c * HH + d * HH // 2, HH // 2), HH // 2)
            wa[k].append(copy(w2.at[b, y, rows], ya2.at[k, d], to))

    def do_w2b(k):
        b = k % 2
        wb[k] = []
        for d, (r, to) in enumerate(((1, pc.YP), (3, pc.YM))):
            y = pc.ys(r)
            w2[b, y, mine] = w2[b, y, mine] + cr2[k, y]
            wa[k][d].wait_recv()
            rows = pl.ds(pl.multiple_of(pc.c * HH + d * HH // 2, HH // 2), HH // 2)
            w2[b, y, rows] = w2[b, y, rows] + ya2[k, d]
            wb[k].append(copy(w2.at[b, y, mine], yb2.at[k, d], to))

    def do_w2c(k):
        for cp in wb[k]:
            cp.wait_recv()
        ss[k] = (
            w2[k % 2, pc.y, mine].astype(F32) + cr2[k, pc.y].astype(F32)
            + yb2[k, 0].astype(F32) + yb2[k, 1].astype(F32)
        ).astype(BF)

    def do_w2z(q):
        wz[q] = copy(ss.at[1 - pc.zl + 2 * q], zr2.at[q], pc.ZL)

    def do_w2s(q):
        wz[q].wait_recv()
        ss[pc.zl + 2 * q] = ss[pc.zl + 2 * q] + zr2[q]

    def do_w2o(_):
        wo[0] = copy(ss.at[pc.zl + 2 * (1 - pc.c)], o2, pc.CO)

    def do_w2f(_):
        wo[0].wait_recv()
        gw2_ref[mine, :] = ss[pc.zl + 2 * pc.c]
        gw2_ref[theirs, :] = o2[...]

    def do_gp(_):
        def tile(k, _):
            rows = pl.ds(pl.multiple_of(k * 64, 64), 64)
            gp[rows, :] = (gh[rows, :] * pre[rows, :]).astype(BF)
            return 0

        lax.fori_loop(0, 8, tile, 0)
        copy.leave(list(co.values()) + list(zl.values()))

    gs, used = [], {"A": 0, "B": 0}
    for j, kind in enumerate(G_KINDS):
        xa, xb, zr = (xaa, xba, zra) if kind == "A" else (xab, xbb, zrb)
        gs.append(InputScatter(pc, copy, big, xa, xb, zr, fin, j * GW, used[kind], GW, kind == "A"))
        used[kind] += GW

    def do_gn(j):
        part = lax.dot_general(gp[...], win[j * GW:(j + 1) * GW, :], NT_DIMS, preferred_element_type=F32)
        big[:, :, :, j * GW:(j + 1) * GW] = part.astype(BF).reshape(4, 2, SLOTS, GW)
        gs[j].s1()

    def do_mig(n):
        xhat, inv = standardized(n)
        t = fin[:, n * VW:(n + 1) * VW] * gain
        mig_ref[:, n * VW:(n + 1) * VW] = (
            (t - jnp.mean(t, axis=1, keepdims=True) - xhat * jnp.mean(t * xhat, axis=1, keepdims=True)) * inv
        ).astype(BF)

    vc, va, vb, vz = {}, [], [], []

    def w1(c, y, z, lo=0, n=320):
        return wout.at[c * 8 + y * 2 + z, pl.ds(lo, n), pl.ds(0, HID)]

    def do_g1(k):
        y = pc.ys(k)

        def tile(z, _):
            cols = pl.ds(pl.multiple_of((z * 4 + y) * 640, 128), 640)
            part = lax.dot_general(
                nt[:, :, cols].reshape(ROWS, 640), gp[...], TN_DIMS, preferred_element_type=F32
            ).astype(BF)
            w1(0, y, z)[...] = part[0:320]
            w1(1, y, z)[...] = part[320:640]
            return 0

        lax.fori_loop(0, 2, tile, 0)
        at = pl.ds((1 - pc.c) * 8 + y * 2, 2)
        vc[k] = copy(wout.at[at, pl.ds(0, 320), pl.ds(0, HID)], cr1.at[y], pc.CO)

    def w1_pair(y, lo, n):
        return wout.at[pl.ds(pc.c * 8 + y * 2, 2), pl.ds(lo, n), pl.ds(0, HID)]

    def w1_core(k):
        y = pc.ys(k)
        vc[k].wait_recv()
        for z in range(2):
            w1(pc.c, y, z)[...] = w1(pc.c, y, z)[...] + cr1[y, z]

    def do_f1(_):
        w1_core(2)
        for d, to in enumerate((pc.YP, pc.YM)):
            va.append(copy(w1_pair(pc.ys(2), d * 160, 160), ya1.at[d], to))

    def do_f2(_):
        for d, (r, to) in enumerate(((1, pc.YP), (3, pc.YM))):
            y = pc.ys(r)
            w1_core(r)
            va[d].wait_recv()
            for z in range(2):
                part = w1(pc.c, y, z, d * 160, 160)
                part[...] = part[...] + ya1[d, z]
            vb.append(copy(w1_pair(y, 0, 320), yb1.at[d], to))

    def w1_total(z):
        return w1(pc.c, pc.y, z)[...].astype(F32) + yb1[0, z].astype(F32) + yb1[1, z].astype(F32)

    def do_f3(_):
        w1_core(0)
        for cp in vb:
            cp.wait_recv()
        there = w1(pc.c, pc.y, 1 - pc.zl)
        there[...] = w1_total(1 - pc.zl).astype(BF)
        vz.append(copy(there, zr1, pc.ZL))

    def do_f4(_):
        vz[0].wait_recv()
        gw1_ref[...] = (w1_total(pc.zl) + zr1[...].astype(F32)).astype(BF)

    stages = {
        "pack": do_pack, "ring": do_ring, "route": do_route, "across": do_across, "arrive": do_arrive,
        "norm": do_norm, "pre": do_pre, "act": do_act, "hid": do_hid, "gp": do_gp, "gn": do_gn, "mig": do_mig,
        "w2": do_w2, "w2a": do_w2a, "w2b": do_w2b, "w2c": do_w2c, "w2z": do_w2z, "w2s": do_w2s,
        "w2o": do_w2o, "w2f": do_w2f, "g1": do_g1, "f1": do_f1, "f2": do_f2, "f3": do_f3, "f4": do_f4,
    }
    for s in range(2, 6):
        stages["N%d" % s] = lambda i, s=s: getattr(ns[i], "s%d" % s)()
        stages["C%d" % s] = lambda i, s=s: getattr(cs[i], "s%d" % s)()
    for s in range(2, 5):
        stages["g%d" % s] = lambda i, s=s: getattr(gs[i], "s%d" % s)()
    for name, i in ORDER:
        stages[name](i)
    copy.finish()
    assert len(copy.all) <= MAX_COPIES


def merger_call(cnt, own, st, gain, bias, gs, feat, win, wout):
    vm = pl.BlockSpec(memory_space=pltpu.VMEM)
    hb = pl.BlockSpec(memory_space=pl.ANY)
    na, nb = G_KINDS.count("A") * GW, G_KINDS.count("B") * GW
    buf = lambda *shape: pltpu.VMEM(shape, BF)
    return pl.pallas_call(
        merger_kernel,
        out_shape=(
            jax.ShapeDtypeStruct((SLOTS, MW), BF),
            jax.ShapeDtypeStruct((320, HID), BF),
            jax.ShapeDtypeStruct((HID, BW), BF),
        ),
        in_specs=[vm, vm, vm, vm, vm, hb, hb, hb, hb],
        out_specs=(vm, vm, vm),
        scratch_shapes=[
            buf(SLOTS, TOK),
            buf(4 * SLOTS, 4 * SLOTS),
            buf(4, 2, SLOTS, D),
            buf(SLOTS, MW),
            buf(MW, HID),
            buf(16, HID, BW),
            buf(4, SLOTS, D),
            buf(2, SLOTS, D),
            buf(SLOTS, D),
            buf(8, SLOTS, D),
            buf(8, SLOTS, MW),
            pltpu.VMEM((ROWS, HID), F32),
            pltpu.VMEM((ROWS, HID), F32),
            buf(HID, ROWS),
            buf(ROWS, HID),
            buf(2, 4, HID, BW),
            buf(4, 4, HH, BW),
            buf(4, 2, HH // 2, BW),
            buf(4, 2, HH, BW),
            buf(4, HH, BW),
            buf(2, HH, BW),
            buf(HH, BW),
            buf(2, 2, HALF, na),
            buf(2, 2, SLOTS, na),
            buf(SLOTS, na),
            buf(2, 1, HALF, nb),
            buf(2, 1, SLOTS, nb),
            buf(4, SLOTS, nb),
            pltpu.VMEM((SLOTS, MW), F32),
            buf(4, 2, 320, HID),
            buf(2, 2, 160, HID),
            buf(2, 2, 320, HID),
            buf(320, HID),
            pltpu.SemaphoreType.DMA((MAX_COPIES,)),
            pltpu.SemaphoreType.DMA((MAX_COPIES,)),
            pltpu.SemaphoreType.DMA((40,)),
        ],
        compiler_params=pltpu.CompilerParams(
            collective_id=0, has_side_effects=True, vmem_limit_bytes=63 * 2**20
        ),
        cost_estimate=pl.CostEstimate(
            flops=2 * 512 * 384 * 31744, bytes_accessed=16 * 2**20, transcendentals=400000
        ),
        name="merger_backward",
    )(cnt, own, st, gain, bias, gs, feat, win, wout)


def local(
    grad_seq, features, merger_norm_gain, w_in, b_in, w_out, image_counts, sample_owner, image_starts
):
    mig, gw1, gw2 = merger_call(
        image_counts, sample_owner, image_starts, merger_norm_gain, b_in,
        grad_seq.reshape(2, 2, SLOTS, D), features[0], w_in, w_out,
    )
    return (mig[None], gw1, gw2)


def solution(mesh):
    in_specs = (
        P("dp", "seq", None),
        P("dp", "seq", None),
        P(),
        P(None, "dp"),
        P("dp"),
        P("dp", None),
        P("dp", None),
        P("dp", None),
        P("dp", None),
    )
    out_specs = (P("dp", "seq", None), P("seq", "dp"), P("dp", "seq"))
    return jax.shard_map(local, mesh=mesh, in_specs=in_specs, out_specs=out_specs, check_vma=False)
```

```python
import jax
import jax.numpy as jnp
from jax import lax
from jax.experimental import pallas as pl
from jax.experimental.pallas import tpu as pltpu
from jax.sharding import PartitionSpec as P

EPS = 1e-06
MESH = pl.DeviceIdType.MESH
BF = jnp.bfloat16
F32 = jnp.float32
I32 = jnp.int32
D = 8192
MW = 5120
VW = 1280
HID = 384
HH = HID // 2
SLOTS = 64
TOK = 256
ROWS = 512
HALF = 32
BW = 512
CW = 1024
KW = 2048
RB = 32
NT_DIMS = (((1,), (1,)), ((), ()))
TN_DIMS = (((0,), (0,)), ((), ()))
N_KINDS = "ABAB"
C_KINDS = "AABAABAB"
ORDER = (
    ("wi1", 0), ("norm", 0), ("norm", 1), ("pack", 0), ("pack", 1), ("ring", 0), ("norm", 2), ("pack", 2),
    ("ring", 1), ("pack", 3), ("norm", 3), ("route", 0), ("wi2", 0), ("ring", 2), ("N2", 0), ("route", 1),
    ("across", 0), ("N2", 3), ("pack", 4), ("N3", 2), ("ring", 3), ("route", 2), ("N2", 2), ("across", 1),
    ("ring", 4), ("across", 2), ("N2", 1), ("N3", 0), ("arrive", 0), ("pack", 5), ("N4", 2), ("N4", 0),
    ("route", 3), ("route", 4), ("across", 3), ("pack", 6), ("arrive", 2), ("arrive", 1), ("C1", 0),
    ("pack", 7), ("across", 4), ("C1", 4), ("N3", 3), ("arrive", 3), ("N5", 0), ("C1", 1), ("C1", 5),
    ("ring", 6), ("C2", 4), ("N5", 2), ("ring", 5), ("route", 6), ("N3", 1), ("ring", 7), ("C3", 4),
    ("C2", 5), ("route", 7), ("C2", 0), ("wi3", 0), ("route", 5), ("C3", 0), ("C4", 4), ("C3", 5),
    ("pre", 2), ("across", 5), ("across", 7), ("arrive", 4), ("C4", 0), ("C2", 1), ("arrive", 5), ("N5", 1),
    ("C1", 2), ("arrive", 7), ("C1", 6), ("N5", 3), ("C3", 1), ("across", 6), ("C5", 4), ("C5", 0),
    ("pre", 1), ("wi4", 0), ("C4", 1), ("pre", 0), ("C5", 5), ("pre", 3), ("C2", 2), ("arrive", 6),
    ("act", 0), ("C1", 3), ("w2", 0), ("C1", 7), ("w2a", 0), ("C5", 1), ("C3", 2), ("w2", 1), ("hid", 0),
    ("C2", 6), ("w2a", 1), ("wi5", 0), ("C2", 7), ("w2b", 0), ("C2", 3), ("hid", 5), ("C3", 6), ("w2b", 1),
    ("hid", 1), ("C4", 6), ("hid", 4), ("C3", 7), ("C4", 3), ("C5", 2), ("w2c", 0), ("C3", 3), ("hid", 2),
    ("C5", 6), ("w2", 2), ("hid", 6), ("w2c", 1), ("C5", 3), ("hid", 3), ("w2a", 2), ("C5", 7), ("w2", 3),
    ("gp", 0), ("hid", 7), ("w2a", 3), ("gp", 1), ("g1", 2), ("w2b", 2), ("w2z", 0), ("g1", 1), ("gy", 0),
    ("gn", 3), ("v0", 2), ("gn", 0), ("f1", 0), ("gn", 2), ("g1", 3), ("g1", 0), ("g2", 3), ("v0", 1),
    ("gy", 1), ("gn", 7), ("w2b", 3), ("w2c", 2), ("gn", 1), ("v0", 3), ("v0", 0), ("e1", 0), ("gn", 6),
    ("gn", 5), ("g2", 0), ("w2s", 0), ("f2", 0), ("g2", 1), ("w2c", 3), ("g2", 6), ("gn", 4), ("g3", 3),
    ("g2", 5), ("g2", 2), ("w2z", 1), ("g3", 0), ("g3", 1), ("e2", 0), ("g2", 7), ("g2", 4), ("f3", 0),
    ("e3", 0), ("g3", 6), ("w2s", 1), ("w2o", 0), ("g3", 2), ("w2f", 0), ("g3", 7), ("g3", 5), ("e4", 0),
    ("g3", 4), ("f4", 0),
)
MAX_COPIES = 256


def normal_cdf(value):
    return 0.5 * (1.0 + lax.erf(value * 0.7071067811865476))


def normal_pdf(value):
    return jnp.exp(-0.5 * value * value) * 0.3989422804014327


def dot(a, b):
    return jnp.dot(a, b, preferred_element_type=F32)


class Place:
    def __init__(self):
        d = lax.axis_index("dp")
        s = lax.axis_index("seq")
        self.seq = s
        self.x, self.zh = lax.div(d, 2), lax.rem(d, 2)
        self.zl, self.y, self.c = lax.div(s, 8), lax.rem(lax.div(s, 2), 4), lax.rem(s, 2)
        self.XP = self.dev(x=self.xs(1))
        self.XM = self.dev(x=self.xs(3))
        self.YP = self.dev(y=self.ys(1))
        self.YM = self.dev(y=self.ys(3))
        self.ZX = self.dev(zh=1 - self.zh, zl=1 - self.zl)
        self.ZL = self.dev(zl=1 - self.zl)
        self.CO = self.dev(c=1 - self.c)

    def xs(self, k):
        return lax.rem(self.x + k, 4)

    def ys(self, k):
        return lax.rem(self.y + k, 4)

    def dev(self, **kw):
        g = lambda n: kw.get(n, getattr(self, n))
        return (g("x") * 2 + g("zh"), g("zl") * 8 + g("y") * 2 + g("c"))

    def greet(self):
        for to in (self.XP, self.XM, self.YP, self.YM, self.ZX, self.ZL, self.CO):
            pl.semaphore_signal(pltpu.get_barrier_semaphore(), inc=1, device_id=to, device_id_type=MESH)

    def meet(self):
        pl.semaphore_wait(pltpu.get_barrier_semaphore(), 7)


class Copies:
    def __init__(self, send, recv):
        self.send, self.recv, self.all, self.sent = send, recv, [], set()

    def __call__(self, src, dst, to):
        i = len(self.all)
        cp = pltpu.make_async_remote_copy(
            src_ref=src, dst_ref=dst, send_sem=self.send.at[i], recv_sem=self.recv.at[i],
            device_id=to, device_id_type=MESH,
        )
        cp.start()
        self.all.append(cp)
        return cp

    def leave(self, copies):
        for cp in copies:
            if id(cp) not in self.sent:
                self.sent.add(id(cp))
                cp.wait_send()

    def finish(self):
        self.leave(self.all)


class Gather:
    def __init__(self, pc, copy, buf, row, rows, lo, w, z_first):
        self.pc, self.copy, self.buf, self.z_first = pc, copy, buf, z_first
        self.rows, self.lo, self.w, self.r = pl.ds(row, rows), lo, w, []

    def blk(self, k, z, part=0, parts=1):
        w = self.w // parts
        return self.buf.at[self.pc.xs(k) * 2 + z, self.rows, pl.ds(self.lo + part * w, w)]

    def to(self, ref, where):
        return self.copy(ref, ref, where)

    def s1(self):
        pc = self.pc
        own = self.blk(0, pc.zh)
        if self.z_first:
            self.z = self.to(own, pc.ZX)
        self.p, self.m = self.to(own, pc.XP), self.to(own, pc.XM)
        if not self.z_first:
            self.z = self.to(own, pc.ZX)

    def relay(self, z):
        pc = self.pc
        return [self.to(self.blk(3, z, 0, 2), pc.XP), self.to(self.blk(1, z, 1, 2), pc.XM)]

    def s2(self):
        pc = self.pc
        if self.z_first:
            self.z.wait_recv()
            other = self.blk(0, 1 - pc.zh)
            self.zp, self.zm = self.to(other, pc.XP), self.to(other, pc.XM)
        else:
            self.p.wait_recv()
            self.m.wait_recv()
            self.r += self.relay(pc.zh)
            self.f = [self.to(self.blk(3, pc.zh), pc.ZX), self.to(self.blk(1, pc.zh), pc.ZX)]

    def s3(self):
        pc = self.pc
        if self.z_first:
            self.p.wait_recv()
            self.m.wait_recv()
            self.r += self.relay(pc.zh)
        else:
            for cp in self.r:
                cp.wait_recv()
            self.f.append(self.to(self.blk(2, pc.zh), pc.ZX))

    def s4(self):
        self.zp.wait_recv()
        self.zm.wait_recv()
        self.r += self.relay(1 - self.pc.zh)

    def s5(self):
        for cp in self.r if self.z_first else [self.z] + self.f:
            cp.wait_recv()


def routing_tables(pc, cnt, own, st):
    iota = lambda shape, axis: lax.broadcasted_iota(I32, shape, axis)
    one = lambda m: jnp.where(m, 1.0, 0.0).astype(BF)
    i0, i1 = iota((64, 64), 0), iota((64, 64), 1)
    col = lambda r: jnp.sum(jnp.where(i0 == i1, r, 0), axis=1, keepdims=True)
    sh = lax.div(st, TOK)
    cnt_c, own_c, st_c, sh_c = col(cnt), col(own), col(st), col(sh)
    before_o = jnp.sum(jnp.where((own_c == own) & (i0 < i1), cnt_c, 0), axis=0, keepdims=True)
    before_h = jnp.sum(jnp.where((sh_c == sh) & (i1 < i0), cnt, 0), axis=1, keepdims=True)
    off = iota((64, TOK), 1) + pc.seq * TOK - st_c
    inside = (sh_c == pc.seq) & (off >= 0) & (off < cnt_c)
    rank = jnp.sum(jnp.where(inside, before_h + off + 1, 0), axis=0, keepdims=True) - 1
    pack = one(iota((64, TOK), 0) == rank)
    r = iota((256, 64), 0)
    q, k = lax.div(r, 64), lax.rem(r, 64)
    core = pc.c + lax.div(q, 2) * (1 - 2 * pc.c)
    zl = pc.zl + lax.rem(q, 2) * (1 - 2 * pc.zl)
    off = k - before_o
    inside = (own == zl * 8 + pc.y * 2 + core) & (off >= 0) & (off < cnt)
    want = jnp.sum(jnp.where(inside, st + off + 1, 0), axis=1, keepdims=True)
    r = iota((64, 256), 1)
    off = lax.rem(r, 64) - before_h
    inside = (sh_c == pc.zl * 8 + lax.div(r, 64) * 2 + pc.c) & (off >= 0) & (off < cnt_c)
    held = jnp.sum(jnp.where(inside, st_c + off + 1, 0), axis=0, keepdims=True)
    return pack, one((want == held) & (want > 0))


def merger_kernel(
    cnt_ref, own_ref, st_ref, gain_ref, b_ref, gs_hbm, feat_hbm, win_hbm, wout_hbm,
    mig_ref, gw1_ref, gw2_ref,
    pack_m, route_m, big, feat, win, win2, wout, g, hc, hz, rt, nt, pre, gh, act_t, gp, gp2,
    w2, cr2, ya2, yb2, ss, zr2, o2, xa, xb, cr1, ya1, yb1, zr1, eb1, ec1, ed1,
    send, recv, lsem,
):
    pc = Place()
    copy = Copies(send, recv)
    me = pc.x * 2 + pc.zh
    nc = D // CW
    cut = lambda i: pl.ds(i * CW, CW)
    loads = []

    def load(src, dst):
        cp = pltpu.make_async_copy(src, dst, lsem.at[len(loads)])
        cp.start()
        loads.append(cp)
        return cp

    def piece(p):
        return pl.ds(((p // 4) % 2 * 8 + p % 4 * 2 + p // 8) * BW, BW)

    lf = load(feat_hbm, feat)
    lg = [load(gs_hbm.at[:, :, :, piece(p)], big.at[0:2, :, :, pl.ds(p * BW, BW)]) for p in range(16)]
    lw = load(win_hbm, win)
    lo = [load(wout_hbm.at[:, piece(p)], wout.at[p // 8, p // 4 % 2, p % 4]) for p in range(16)]
    pc.greet()
    pack_m[...], route_m[...] = routing_tables(pc, cnt_ref[...], own_ref[...], st_ref[...])
    gain = gain_ref[...].reshape(1, VW)
    pc.meet()

    yp, ym, rp, rm, co, zl = ({} for _ in range(6))

    def do_pack(i):
        lg[2 * i].wait()
        lg[2 * i + 1].wait()
        g[pc.y, :, cut(i)] = dot(pack_m[...], big[0:2, :, :, cut(i)].reshape(TOK, CW)).astype(BF)
        own = g.at[pc.y, :, cut(i)]
        yp[i] = copy(own, own, pc.YP)
        ym[i] = copy(own, own, pc.YM)

    def do_ring(i):
        yp[i].wait_recv()
        up = g.at[pc.ys(3), pl.ds(0, HALF), cut(i)]
        rp[i] = copy(up, up, pc.YP)
        ym[i].wait_recv()
        down = g.at[pc.ys(1), pl.ds(HALF, HALF), cut(i)]
        rm[i] = copy(down, down, pc.YM)

    def do_route(i):
        rp[i].wait_recv()
        rm[i].wait_recv()
        for j in range(CW // 512):
            cols = pl.ds(i * CW + j * 512, 512)
            big[2:4, :, :, cols] = (
                dot(route_m[...], g[:, :, cols].reshape(4 * SLOTS, 512)).astype(BF).reshape(2, 2, SLOTS, 512)
            )
        co[i] = copy(big.at[3, :, :, cut(i)], hc.at[:, :, cut(i)], pc.CO)

    def do_across(i):
        co[i].wait_recv()
        big[2, :, :, cut(i)] = big[2, :, :, cut(i)] + hc[:, :, cut(i)]
        zl[i] = copy(big.at[2, 1, :, cut(i)], hz.at[:, cut(i)], pc.ZL)

    cs = [Gather(pc, copy, rt, i // 4 * RB, RB, i % 4 * KW, KW, C_KINDS[i] == "A") for i in range(8)]
    ns = [Gather(pc, copy, nt, 0, SLOTS, n * VW, VW, N_KINDS[n] == "A") for n in range(4)]

    def do_arrive(i):
        zl[i].wait_recv()
        rt[me, :, cut(i)] = big[2, 0, :, cut(i)] + hz[:, cut(i)]

    def standardized(n, row=0, rows=SLOTS):
        v = feat[row:row + rows, n * VW:(n + 1) * VW].astype(F32)
        d = v - jnp.mean(v, axis=1, keepdims=True)
        inv = lax.rsqrt(jnp.mean(d * d, axis=1, keepdims=True) + EPS)
        return d * inv, inv

    def do_norm(n):
        if n == 0:
            lf.wait()
        nt[me, :, n * VW:(n + 1) * VW] = (standardized(n)[0] * gain).astype(BF)
        ns[n].s1()

    def do_pre(n):
        part = dot(
            nt[:, :, n * VW:(n + 1) * VW].reshape(ROWS, VW), win[n * VW:(n + 1) * VW, :]
        ).reshape(8, SLOTS, HID)
        if started:
            pre[...] += part
        else:
            pre[...] = part + b_ref[...].reshape(1, 1, HID)
            started.append(n)

    started = []

    def do_act(_):
        def tile(k, _):
            at = pl.ds(k * 2, 2)
            v = pre[at].reshape(128, HID)
            cdf = normal_cdf(v)
            act_t[:, pl.ds(pl.multiple_of(k * 128, 128), 128)] = (v * cdf).T.astype(BF)
            pre[at] = (cdf + v * normal_pdf(v)).reshape(2, SLOTS, HID)
            return 0

        lax.fori_loop(0, 4, tile, 0)

    opened = set()

    def do_hid(i):
        b, k = i // 4, i % 4
        part = None
        for y in range(4):
            p = 4 * k + y
            if p not in ready:
                lo[p].wait()
                ready.add(p)
            one = lax.dot_general(
                rt[:, b * RB:(b + 1) * RB, p * BW:(p + 1) * BW].reshape(8 * RB, BW),
                wout[k // 2, k % 2, y], NT_DIMS, preferred_element_type=F32,
            )
            part = one if part is None else part + one
        if b in opened:
            gh[b] += part
        else:
            gh[b] = part
            opened.add(b)

    ready = set()

    mine = pl.ds(pl.multiple_of(pc.c * HH, HH), HH)
    theirs = pl.ds(pl.multiple_of((1 - pc.c) * HH, HH), HH)
    wc, wa, wb, wz, wo = ({} for _ in range(5))

    def do_w2(k):
        b = k % 2
        if k >= 2:
            copy.leave([wc[k - 2]] + wa[k - 2] + wb[k - 2])

        def tile(y, _):
            cols = pl.ds(pl.multiple_of(k * 4 * BW + y * BW, BW), BW)
            w2[b, y] = dot(act_t[...], rt[:, :, cols].reshape(ROWS, BW)).astype(BF)
            return 0

        lax.fori_loop(0, 4, tile, 0)
        wc[k] = copy(w2.at[b, :, theirs], cr2.at[k], pc.CO)

    def do_w2a(k):
        b, y = k % 2, pc.ys(2)
        wc[k].wait_recv()
        w2[b, y, mine] = w2[b, y, mine] + cr2[k, y]
        wa[k] = []
        for d, to in enumerate((pc.YP, pc.YM)):
            rows = pl.ds(pl.multiple_of(pc.c * HH + d * HH // 2, HH // 2), HH // 2)
            wa[k].append(copy(w2.at[b, y, rows], ya2.at[k, d], to))

    def do_w2b(k):
        b = k % 2
        wb[k] = []
        for d, (r, to) in enumerate(((1, pc.YP), (3, pc.YM))):
            y = pc.ys(r)
            w2[b, y, mine] = w2[b, y, mine] + cr2[k, y]
            wa[k][d].wait_recv()
            rows = pl.ds(pl.multiple_of(pc.c * HH + d * HH // 2, HH // 2), HH // 2)
            w2[b, y, rows] = w2[b, y, rows] + ya2[k, d]
            wb[k].append(copy(w2.at[b, y, mine], yb2.at[k, d], to))

    def do_w2c(k):
        for cp in wb[k]:
            cp.wait_recv()
        ss[k] = (
            w2[k % 2, pc.y, mine].astype(F32) + cr2[k, pc.y].astype(F32)
            + yb2[k, 0].astype(F32) + yb2[k, 1].astype(F32)
        ).astype(BF)

    def do_w2z(q):
        wz[q] = copy(ss.at[1 - pc.zl + 2 * q], zr2.at[q], pc.ZL)

    def do_w2s(q):
        wz[q].wait_recv()
        ss[pc.zl + 2 * q] = ss[pc.zl + 2 * q] + zr2[q]

    def do_w2o(_):
        wo[0] = copy(ss.at[pc.zl + 2 * (1 - pc.c)], o2, pc.CO)

    def do_w2f(_):
        wo[0].wait_recv()
        gw2_ref[mine, :] = ss[pc.zl + 2 * pc.c]
        gw2_ref[theirs, :] = o2[...]

    gx, ga, gb, wi = {}, {}, {}, {}

    def share(z, n=1):
        return pl.ds(pl.multiple_of((pc.c * 8 + pc.y * 2 + z) * 320, 320), n * 320)

    def do_wi1(_):
        lw.wait()
        wi[1] = [copy(win.at[share(1 - pc.zl)], win2.at[share(1 - pc.zl)], pc.ZX)]

    def pass_on(n, refs):
        for cp in wi[n - 1]:
            cp.wait_recv()
        wi[n] = [copy(win2.at[rows], win2.at[rows], to) for rows, to in refs]

    def do_wi2(_):
        pass_on(2, [(share(pc.zl), pc.ZL)])

    def do_wi3(_):
        pass_on(3, [(share(0, 2), pc.YP), (share(0, 2), pc.YM)])

    def do_wi4(_):
        at = lambda k, z: pl.ds(pl.multiple_of((pc.c * 8 + pc.ys(k) * 2 + z) * 320, 320), 320)
        pass_on(4, [(at(3, 0), pc.YP), (at(1, 1), pc.YM)])

    def do_wi5(_):
        pass_on(5, [(pl.ds(pl.multiple_of(pc.c * 2560, 2560), 2560), pc.CO)])

    def do_gp(b):
        rows = pl.ds(b * RB, RB)
        gp[:, :, rows, :] = (
            (gh[b].reshape(8, RB, HID) * pre[:, rows, :]).astype(BF).reshape(4, 2, RB, HID)
        )
        copy.leave(list(co.values()) + list(zl.values()))
        gx[b] = copy(gp.at[:, 1 - pc.zh, rows], gp2.at[:, rows], pc.ZX)

    def do_gy(b):
        for cp in wi.pop(5, []):
            cp.wait_recv()
        gx[b].wait_recv()

    def do_gn(i):
        b, j = i // 4, i % 4
        rows, at = pl.ds(b * RB, RB), slice(j * VW, (j + 1) * VW)
        part = lax.dot_general(
            gp[:, pc.zh, rows, :].reshape(4 * RB, HID), win[at, :], NT_DIMS, preferred_element_type=F32
        ) + lax.dot_general(
            gp2[:, rows, :].reshape(4 * RB, HID), win2[at, :], NT_DIMS, preferred_element_type=F32
        )
        big[:, 0, rows, at] = part.astype(BF).reshape(4, RB, VW)
        ga[i] = [
            copy(
                big.at[pc.xs(2), 0, rows, pl.ds(j * VW + d * VW // 2, VW // 2)],
                xa.at[d, rows, pl.ds(j * VW // 2, VW // 2)], to,
            )
            for d, to in enumerate((pc.XP, pc.XM))
        ]

    def do_g2(i):
        b, j = i // 4, i % 4
        rows, at = pl.ds(b * RB, RB), pl.ds(j * VW, VW)
        gb[i] = []
        for d, (k, to) in enumerate(((1, pc.XP), (3, pc.XM))):
            ga[i][d].wait_recv()
            half = pl.ds(j * VW + d * VW // 2, VW // 2)
            near = pc.xs(k)
            big[near, 0, rows, half] = big[near, 0, rows, half] + xa[d, rows, pl.ds(j * VW // 2, VW // 2)]
            gb[i].append(copy(big.at[near, 0, rows, at], xb.at[d, rows, at], to))

    def do_g3(i):
        b, j = i // 4, i % 4
        rows, at = pl.ds(b * RB, RB), pl.ds(j * VW, VW)
        for cp in gb[i]:
            cp.wait_recv()
        total = (
            big[pc.x, 0, rows, at].astype(F32) + xb[0, rows, at].astype(F32) + xb[1, rows, at].astype(F32)
        )
        xhat, inv = standardized(j, b * RB, RB)
        t = total * gain
        mig_ref[rows, at] = (
            (t - jnp.mean(t, axis=1, keepdims=True) - xhat * jnp.mean(t * xhat, axis=1, keepdims=True)) * inv
        ).astype(BF)

    vc, va, vb, vz, ve, vf, vg = {}, [], [], [], [], [], []
    col_a, col_b = pl.ds(0, 256), pl.ds(256, 128)

    def w1(z, y, cols, row=0, rows=320):
        return wout.at[pc.c, z, y, pl.ds(row, rows), cols]

    def do_g1(k):
        y = pc.ys(k)

        def tile(z, _):
            cols = pl.ds(pl.multiple_of((z * 4 + y) * 640, 128), 640)
            part = lax.dot_general(
                nt[:, :, cols].reshape(ROWS, 640), gp[...].reshape(ROWS, HID), TN_DIMS,
                preferred_element_type=F32,
            ).astype(BF)
            wout[0, z, y, 0:320, 0:HID] = part[0:320]
            wout[1, z, y, 0:320, 0:HID] = part[320:640]
            return 0

        lax.fori_loop(0, 2, tile, 0)
        vc[k] = copy(wout.at[1 - pc.c, :, y, pl.ds(0, 320), pl.ds(0, HID)], cr1.at[:, y], pc.CO)

    def do_v0(k):
        y = pc.ys(k)
        vc[k].wait_recv()
        for z in range(2):
            part = w1(z, y, pl.ds(0, HID))
            part[...] = part[...] + cr1[z, y]

    def do_f1(_):
        for d, to in enumerate((pc.YP, pc.YM)):
            va.append(copy(w1(slice(None), pc.ys(2), col_a, d * 160, 160), ya1.at[d], to))

    def do_f2(_):
        for d, (r, to) in enumerate(((1, pc.YP), (3, pc.YM))):
            y = pc.ys(r)
            va[d].wait_recv()
            for z in range(2):
                part = w1(z, y, col_a, d * 160, 160)
                part[...] = part[...] + ya1[d, z]
            vb.append(copy(w1(slice(None), y, col_a), yb1.at[d], to))

    def total_a(z):
        return w1(z, pc.y, col_a)[...].astype(F32) + yb1[0, z].astype(F32) + yb1[1, z].astype(F32)

    def do_f3(_):
        for cp in vb:
            cp.wait_recv()
        there = w1(1 - pc.zl, pc.y, col_a)
        there[...] = total_a(1 - pc.zl).astype(BF)
        vz.append(copy(there, zr1, pc.ZL))

    def do_f4(_):
        vz[0].wait_recv()
        gw1_ref[:, 0:256] = (total_a(pc.zl) + zr1[...].astype(F32)).astype(BF)

    def do_e1(_):
        ve.append(copy(w1(1 - pc.zl, slice(None), col_b), eb1, pc.ZL))

    def do_e2(_):
        ve[0].wait_recv()
        for k in (2, 1, 3, 0):
            y = pc.ys(k)
            part = w1(pc.zl, y, col_b)
            part[...] = part[...] + eb1[y]
            if k == 2:
                for d, to in enumerate((pc.YP, pc.YM)):
                    vf.append(copy(w1(pc.zl, y, col_b, d * 160, 160), ec1.at[d], to))

    def do_e3(_):
        for d, (r, to) in enumerate(((1, pc.YP), (3, pc.YM))):
            y = pc.ys(r)
            vf[d].wait_recv()
            part = w1(pc.zl, y, col_b, d * 160, 160)
            part[...] = part[...] + ec1[d]
            vg.append(copy(w1(pc.zl, y, col_b), ed1.at[d], to))

    def do_e4(_):
        for cp in vg:
            cp.wait_recv()
        gw1_ref[:, 256:384] = (
            w1(pc.zl, pc.y, col_b)[...].astype(F32) + ed1[0].astype(F32) + ed1[1].astype(F32)
        ).astype(BF)

    stages = {
        "pack": do_pack, "ring": do_ring, "route": do_route, "across": do_across, "arrive": do_arrive,
        "norm": do_norm, "pre": do_pre, "act": do_act, "hid": do_hid, "gp": do_gp, "gy": do_gy, "gn": do_gn,
        "g2": do_g2, "g3": do_g3, "wi1": do_wi1, "wi2": do_wi2, "wi3": do_wi3, "wi4": do_wi4, "wi5": do_wi5,
        "w2": do_w2, "w2a": do_w2a, "w2b": do_w2b, "w2c": do_w2c, "w2z": do_w2z, "w2s": do_w2s,
        "w2o": do_w2o, "w2f": do_w2f, "g1": do_g1, "v0": do_v0, "f1": do_f1, "f2": do_f2, "f3": do_f3, "f4": do_f4,
        "e1": do_e1, "e2": do_e2, "e3": do_e3, "e4": do_e4,
    }
    for s in range(1, 6):
        stages["N%d" % s] = lambda i, s=s: getattr(ns[i], "s%d" % s)()
        stages["C%d" % s] = lambda i, s=s: getattr(cs[i], "s%d" % s)()
    for name, i in ORDER:
        stages[name](i)
    copy.finish()
    assert len(copy.all) <= MAX_COPIES


def merger_call(cnt, own, st, gain, bias, gs, feat, win, wout):
    vm = pl.BlockSpec(memory_space=pltpu.VMEM)
    hb = pl.BlockSpec(memory_space=pl.ANY)
    buf = lambda *shape: pltpu.VMEM(shape, BF)
    return pl.pallas_call(
        merger_kernel,
        out_shape=(
            jax.ShapeDtypeStruct((SLOTS, MW), BF),
            jax.ShapeDtypeStruct((320, HID), BF),
            jax.ShapeDtypeStruct((HID, BW), BF),
        ),
        in_specs=[vm, vm, vm, vm, vm, hb, hb, hb, hb],
        out_specs=(vm, vm, vm),
        scratch_shapes=[
            buf(SLOTS, TOK),
            buf(4 * SLOTS, 4 * SLOTS),
            buf(4, 2, SLOTS, D),
            buf(SLOTS, MW),
            buf(MW, HID),
            buf(MW, HID),
            buf(2, 2, 4, HID, BW),
            buf(4, SLOTS, D),
            buf(2, SLOTS, D),
            buf(SLOTS, D),
            buf(8, SLOTS, D),
            buf(8, SLOTS, MW),
            pltpu.VMEM((8, SLOTS, HID), F32),
            pltpu.VMEM((2, 8 * RB, HID), F32),
            buf(HID, ROWS),
            buf(4, 2, SLOTS, HID),
            buf(4, SLOTS, HID),
            buf(2, 4, HID, BW),
            buf(4, 4, HH, BW),
            buf(4, 2, HH // 2, BW),
            buf(4, 2, HH, BW),
            buf(4, HH, BW),
            buf(2, HH, BW),
            buf(HH, BW),
            buf(2, SLOTS, MW // 2),
            buf(2, SLOTS, MW),
            buf(2, 4, 320, HID),
            buf(2, 2, 160, 256),
            buf(2, 2, 320, 256),
            buf(320, 256),
            buf(4, 320, 128),
            buf(2, 160, 128),
            buf(2, 320, 128),
            pltpu.SemaphoreType.DMA((MAX_COPIES,)),
            pltpu.SemaphoreType.DMA((MAX_COPIES,)),
            pltpu.SemaphoreType.DMA((40,)),
        ],
        compiler_params=pltpu.CompilerParams(
            collective_id=0, has_side_effects=True, vmem_limit_bytes=63 * 2**20
        ),
        cost_estimate=pl.CostEstimate(
            flops=2 * 512 * 384 * 31744, bytes_accessed=16 * 2**20, transcendentals=400000
        ),
        name="merger_backward",
    )(cnt, own, st, gain, bias, gs, feat, win, wout)


def finish_kernel(a, b, c, ao, bo, co):
    for i, o in ((a, ao), (b, bo), (c, co)):
        o[...] = i[...]


def finish_call(*arrays):
    vm = pl.BlockSpec(memory_space=pltpu.VMEM)
    return pl.pallas_call(
        finish_kernel,
        out_shape=tuple(jax.ShapeDtypeStruct(a.shape, a.dtype) for a in arrays),
        in_specs=[vm] * 3,
        out_specs=(vm, vm, vm),
        compiler_params=pltpu.CompilerParams(vmem_limit_bytes=63 * 2**20),
        name="write_results",
    )(*arrays)


def local(
    grad_seq, features, merger_norm_gain, w_in, b_in, w_out, image_counts, sample_owner, image_starts
):
    mig, gw1, gw2 = merger_call(
        image_counts, sample_owner, image_starts, merger_norm_gain, b_in,
        grad_seq.reshape(2, 2, SLOTS, D), features[0], w_in, w_out,
    )
    mig, gw1, gw2 = finish_call(mig, gw1, gw2)
    return (mig[None], gw1, gw2)


def solution(mesh):
    in_specs = (
        P("dp", "seq", None),
        P("dp", "seq", None),
        P(),
        P(None, "dp"),
        P("dp"),
        P("dp", None),
        P("dp", None),
        P("dp", None),
        P("dp", None),
    )
    out_specs = (P("dp", "seq", None), P("seq", "dp"), P("dp", "seq"))
    return jax.shard_map(local, mesh=mesh, in_specs=in_specs, out_specs=out_specs, check_vma=False)
```

```python
import jax
import jax.numpy as jnp
from jax import lax
from jax.experimental import pallas as pl
from jax.experimental.pallas import tpu as pltpu
from jax.sharding import PartitionSpec as P

EPS = 1e-06
MESH = pl.DeviceIdType.MESH
BF = jnp.bfloat16
F32 = jnp.float32
I32 = jnp.int32
D = 8192
MW = 5120
VW = 1280
HID = 384
HH = HID // 2
SLOTS = 64
TOK = 256
ROWS = 512
HALF = 32
BW = 512
CW = 1024
KW = 2048
RB = 32
NT_DIMS = (((1,), (1,)), ((), ()))
TN_DIMS = (((0,), (0,)), ((), ()))
N_KINDS = "ABAB"
C_KINDS = "AABAABAB"
ORDER = (
    ("norm", 0), ("pack", 0), ("pack", 1), ("pack", 2), ("norm", 1), ("norm", 2), ("N2", 1), ("N2", 0),
    ("ring", 0), ("ring", 1), ("ring", 2), ("route", 0), ("N3", 0), ("pack", 3), ("norm", 3), ("across", 0),
    ("pack", 4), ("pack", 5), ("route", 1), ("across", 1), ("route", 2), ("ring", 3), ("wi1", 0), ("N3", 2),
    ("pack", 6), ("arrive", 0), ("across", 2), ("N2", 2), ("arrive", 1), ("C1", 0), ("ring", 5), ("ring", 4),
    ("N4", 0), ("route", 3), ("N3", 1), ("across", 3), ("C1", 4), ("C2", 0), ("wi2", 0), ("pack", 7),
    ("arrive", 2), ("ring", 6), ("arrive", 3), ("route", 5), ("N2", 3), ("C1", 1), ("C3", 4), ("across", 5),
    ("N5", 1), ("ring", 7), ("N3", 3), ("C1", 5), ("route", 6), ("C2", 4), ("C4", 0), ("route", 7),
    ("C3", 0), ("pre", 1), ("across", 6), ("route", 4), ("across", 7), ("wi3", 0), ("across", 4), ("C2", 5),
    ("N5", 3), ("pre", 3), ("N4", 2), ("C2", 1), ("N5", 0), ("arrive", 7), ("arrive", 5), ("C3", 5),
    ("arrive", 4), ("C4", 4), ("C3", 1), ("N5", 2), ("C1", 2), ("C5", 0), ("wi4", 0), ("pre", 0), ("pre", 2),
    ("C1", 6), ("act", 0), ("C4", 1), ("C5", 4), ("w2", 0), ("C5", 5), ("w2a", 0), ("C2", 2), ("arrive", 6),
    ("C1", 3), ("C5", 1), ("C2", 6), ("C3", 2), ("w2b", 0), ("C1", 7), ("C3", 6), ("w2", 1), ("hid", 5),
    ("C4", 6), ("w2a", 1), ("wi5", 0), ("C2", 3), ("hid", 0), ("C2", 7), ("w2b", 1), ("w2c", 0), ("C5", 2),
    ("C3", 3), ("C5", 6), ("w2", 2), ("hid", 4), ("C4", 3), ("hid", 1), ("w2a", 2), ("C3", 7), ("hid", 6),
    ("w2c", 1), ("C5", 3), ("hid", 3), ("hid", 2), ("gp", 0), ("w2z", 0), ("w2b", 2), ("C5", 7), ("w2", 3),
    ("hid", 7), ("gp", 1), ("g1", 2), ("gy", 0), ("w2a", 3), ("gn", 2), ("gn", 0), ("v0", 2), ("gn", 1),
    ("f1", 0), ("g1", 1), ("f1", 1), ("g1", 3), ("g2", 2), ("g1", 0), ("w2b", 3), ("g2", 1), ("v0", 3),
    ("v0", 1), ("gn", 3), ("v0", 0), ("gy", 1), ("e1", 0), ("gn", 4), ("f2", 1), ("gn", 7), ("gn", 5),
    ("gn", 6), ("g3", 1), ("g3", 2), ("w2c", 2), ("g2", 0), ("g2", 3), ("w2c", 3), ("g2", 4), ("f2", 0),
    ("w2z", 1), ("g2", 7), ("f3", 1), ("e2", 0), ("g3", 3), ("g2", 6), ("w2s", 0), ("g2", 5), ("f3", 0),
    ("e3", 0), ("w2s", 1), ("g3", 7), ("w2o", 0), ("g3", 4), ("g3", 0), ("w2f", 0), ("f4", 1), ("g3", 6),
    ("f4", 0), ("e4", 0), ("g3", 5),
)
MAX_COPIES = 256


def normal_cdf(value):
    return 0.5 * (1.0 + lax.erf(value * 0.7071067811865476))


def normal_pdf(value):
    return jnp.exp(-0.5 * value * value) * 0.3989422804014327


def dot(a, b):
    return jnp.dot(a, b, preferred_element_type=F32)


class Place:
    def __init__(self):
        d = lax.axis_index("dp")
        s = lax.axis_index("seq")
        self.seq = s
        self.x, self.zh = lax.div(d, 2), lax.rem(d, 2)
        self.zl, self.y, self.c = lax.div(s, 8), lax.rem(lax.div(s, 2), 4), lax.rem(s, 2)
        self.XP = self.dev(x=self.xs(1))
        self.XM = self.dev(x=self.xs(3))
        self.YP = self.dev(y=self.ys(1))
        self.YM = self.dev(y=self.ys(3))
        self.ZX = self.dev(zh=1 - self.zh, zl=1 - self.zl)
        self.ZL = self.dev(zl=1 - self.zl)
        self.CO = self.dev(c=1 - self.c)

    def xs(self, k):
        return lax.rem(self.x + k, 4)

    def ys(self, k):
        return lax.rem(self.y + k, 4)

    def dev(self, **kw):
        g = lambda n: kw.get(n, getattr(self, n))
        return (g("x") * 2 + g("zh"), g("zl") * 8 + g("y") * 2 + g("c"))

    def greet(self):
        for to in (self.XP, self.XM, self.YP, self.YM, self.ZX, self.ZL, self.CO):
            pl.semaphore_signal(pltpu.get_barrier_semaphore(), inc=1, device_id=to, device_id_type=MESH)

    def meet(self):
        pl.semaphore_wait(pltpu.get_barrier_semaphore(), 7)


class Copies:
    def __init__(self, send, recv):
        self.send, self.recv, self.all, self.sent = send, recv, [], set()

    def __call__(self, src, dst, to):
        i = len(self.all)
        cp = pltpu.make_async_remote_copy(
            src_ref=src, dst_ref=dst, send_sem=self.send.at[i], recv_sem=self.recv.at[i],
            device_id=to, device_id_type=MESH,
        )
        cp.start()
        self.all.append(cp)
        return cp

    def leave(self, copies):
        for cp in copies:
            if id(cp) not in self.sent:
                self.sent.add(id(cp))
                cp.wait_send()

    def finish(self):
        self.leave(self.all)


class Gather:
    def __init__(self, pc, copy, buf, row, rows, lo, w, z_first):
        self.pc, self.copy, self.buf, self.z_first = pc, copy, buf, z_first
        self.rows, self.lo, self.w, self.r = pl.ds(row, rows), lo, w, []

    def blk(self, k, z, part=0, parts=1):
        w = self.w // parts
        return self.buf.at[self.pc.xs(k) * 2 + z, self.rows, pl.ds(self.lo + part * w, w)]

    def to(self, ref, where):
        return self.copy(ref, ref, where)

    def s1(self):
        pc = self.pc
        own = self.blk(0, pc.zh)
        if self.z_first:
            self.z = self.to(own, pc.ZX)
        self.p, self.m = self.to(own, pc.XP), self.to(own, pc.XM)
        if not self.z_first:
            self.z = self.to(own, pc.ZX)

    def relay(self, z):
        pc = self.pc
        return [self.to(self.blk(3, z, 0, 2), pc.XP), self.to(self.blk(1, z, 1, 2), pc.XM)]

    def s2(self):
        pc = self.pc
        if self.z_first:
            self.z.wait_recv()
            other = self.blk(0, 1 - pc.zh)
            self.zp, self.zm = self.to(other, pc.XP), self.to(other, pc.XM)
        else:
            self.p.wait_recv()
            self.m.wait_recv()
            self.r += self.relay(pc.zh)
            self.f = [self.to(self.blk(3, pc.zh), pc.ZX), self.to(self.blk(1, pc.zh), pc.ZX)]

    def s3(self):
        pc = self.pc
        if self.z_first:
            self.p.wait_recv()
            self.m.wait_recv()
            self.r += self.relay(pc.zh)
        else:
            for cp in self.r:
                cp.wait_recv()
            self.f.append(self.to(self.blk(2, pc.zh), pc.ZX))

    def s4(self):
        self.zp.wait_recv()
        self.zm.wait_recv()
        self.r += self.relay(1 - self.pc.zh)

    def s5(self):
        for cp in self.r if self.z_first else [self.z] + self.f:
            cp.wait_recv()


def routing_tables(pc, cnt, own, st):
    iota = lambda shape, axis: lax.broadcasted_iota(I32, shape, axis)
    one = lambda m: jnp.where(m, 1.0, 0.0).astype(BF)
    i0, i1 = iota((64, 64), 0), iota((64, 64), 1)
    col = lambda r: jnp.sum(jnp.where(i0 == i1, r, 0), axis=1, keepdims=True)
    sh = lax.div(st, TOK)
    cnt_c, own_c, st_c, sh_c = col(cnt), col(own), col(st), col(sh)
    before_o = jnp.sum(jnp.where((own_c == own) & (i0 < i1), cnt_c, 0), axis=0, keepdims=True)
    before_h = jnp.sum(jnp.where((sh_c == sh) & (i1 < i0), cnt, 0), axis=1, keepdims=True)
    off = iota((64, TOK), 1) + pc.seq * TOK - st_c
    inside = (sh_c == pc.seq) & (off >= 0) & (off < cnt_c)
    rank = jnp.sum(jnp.where(inside, before_h + off + 1, 0), axis=0, keepdims=True) - 1
    pack = one(iota((64, TOK), 0) == rank)
    r = iota((256, 64), 0)
    q, k = lax.div(r, 64), lax.rem(r, 64)
    core = pc.c + lax.div(q, 2) * (1 - 2 * pc.c)
    zl = pc.zl + lax.rem(q, 2) * (1 - 2 * pc.zl)
    off = k - before_o
    inside = (own == zl * 8 + pc.y * 2 + core) & (off >= 0) & (off < cnt)
    want = jnp.sum(jnp.where(inside, st + off + 1, 0), axis=1, keepdims=True)
    r = iota((64, 256), 1)
    off = lax.rem(r, 64) - before_h
    inside = (sh_c == pc.zl * 8 + lax.div(r, 64) * 2 + pc.c) & (off >= 0) & (off < cnt_c)
    held = jnp.sum(jnp.where(inside, st_c + off + 1, 0), axis=0, keepdims=True)
    return pack, one((want == held) & (want > 0))


def merger_kernel(
    cnt_ref, own_ref, st_ref, gain_ref, b_ref, gs_hbm, feat_hbm, win_hbm, wout_hbm,
    mig_ref, gw1_ref, gw2_ref,
    pack_m, route_m, big, feat, win, win2, wout, g, hc, hz, rt, nt, pre, gh, act_t, gp, gp2,
    w2, cr2, ya2, yb2, ss, zr2, o2, xa, xb, cr1, ya1, yb1, zr1, eb1, ec1, ed1,
    send, recv, lsem,
):
    pc = Place()
    copy = Copies(send, recv)
    me = pc.x * 2 + pc.zh
    nc = D // CW
    cut = lambda i: pl.ds(i * CW, CW)
    loads = []

    def load(src, dst):
        cp = pltpu.make_async_copy(src, dst, lsem.at[len(loads)])
        cp.start()
        loads.append(cp)
        return cp

    def piece(p):
        return pl.ds(((p // 4) % 2 * 8 + p % 4 * 2 + p // 8) * BW, BW)

    lf = load(feat_hbm, feat)
    lg = [load(gs_hbm.at[:, :, :, piece(p)], big.at[0:2, :, :, pl.ds(p * BW, BW)]) for p in range(16)]
    lw = load(win_hbm, win)
    lo = [load(wout_hbm.at[:, piece(p)], wout.at[p // 8, p // 4 % 2, p % 4]) for p in range(16)]
    pc.greet()
    pack_m[...], route_m[...] = routing_tables(pc, cnt_ref[...], own_ref[...], st_ref[...])
    gain = gain_ref[...].reshape(1, VW)
    pc.meet()

    yp, ym, rp, rm, co, zl = ({} for _ in range(6))

    def do_pack(i):
        lg[2 * i].wait()
        lg[2 * i + 1].wait()
        g[pc.y, :, cut(i)] = dot(pack_m[...], big[0:2, :, :, cut(i)].reshape(TOK, CW)).astype(BF)
        own = g.at[pc.y, :, cut(i)]
        yp[i] = copy(own, own, pc.YP)
        ym[i] = copy(own, own, pc.YM)

    def do_ring(i):
        yp[i].wait_recv()
        up = g.at[pc.ys(3), pl.ds(0, HALF), cut(i)]
        rp[i] = copy(up, up, pc.YP)
        ym[i].wait_recv()
        down = g.at[pc.ys(1), pl.ds(HALF, HALF), cut(i)]
        rm[i] = copy(down, down, pc.YM)

    def do_route(i):
        rp[i].wait_recv()
        rm[i].wait_recv()
        for j in range(CW // 512):
            cols = pl.ds(i * CW + j * 512, 512)
            big[2:4, :, :, cols] = (
                dot(route_m[...], g[:, :, cols].reshape(4 * SLOTS, 512)).astype(BF).reshape(2, 2, SLOTS, 512)
            )
        co[i] = copy(big.at[3, :, :, cut(i)], hc.at[:, :, cut(i)], pc.CO)

    def do_across(i):
        co[i].wait_recv()
        big[2, :, :, cut(i)] = big[2, :, :, cut(i)] + hc[:, :, cut(i)]
        zl[i] = copy(big.at[2, 1, :, cut(i)], hz.at[:, cut(i)], pc.ZL)

    cs = [Gather(pc, copy, rt, i // 4 * RB, RB, i % 4 * KW, KW, C_KINDS[i] == "A") for i in range(8)]
    ns = [Gather(pc, copy, nt, 0, SLOTS, n * VW, VW, N_KINDS[n] == "A") for n in range(4)]

    def do_arrive(i):
        zl[i].wait_recv()
        rt[me, :, cut(i)] = big[2, 0, :, cut(i)] + hz[:, cut(i)]

    def standardized(n, row=0, rows=SLOTS):
        v = feat[row:row + rows, n * VW:(n + 1) * VW].astype(F32)
        d = v - jnp.mean(v, axis=1, keepdims=True)
        inv = lax.rsqrt(jnp.mean(d * d, axis=1, keepdims=True) + EPS)
        return d * inv, inv

    def do_norm(n):
        if n == 0:
            lf.wait()
        nt[me, :, n * VW:(n + 1) * VW] = (standardized(n)[0] * gain).astype(BF)
        ns[n].s1()

    def do_pre(n):
        if not started:
            lw.wait()
        part = dot(
            nt[:, :, n * VW:(n + 1) * VW].reshape(ROWS, VW), win[n * VW:(n + 1) * VW, :]
        ).reshape(8, SLOTS, HID)
        if started:
            pre[...] += part
        else:
            pre[...] = part + b_ref[...].reshape(1, 1, HID)
            started.append(n)

    started = []

    def do_act(_):
        def tile(k, _):
            at = pl.ds(k * 2, 2)
            v = pre[at].reshape(128, HID)
            cdf = normal_cdf(v)
            act_t[:, pl.ds(pl.multiple_of(k * 128, 128), 128)] = (v * cdf).T.astype(BF)
            pre[at] = (cdf + v * normal_pdf(v)).reshape(2, SLOTS, HID)
            return 0

        lax.fori_loop(0, 4, tile, 0)

    opened = set()

    def do_hid(i):
        b, k = i // 4, i % 4
        part = None
        for y in range(4):
            p = 4 * k + y
            if p not in ready:
                lo[p].wait()
                ready.add(p)
            one = lax.dot_general(
                rt[:, b * RB:(b + 1) * RB, p * BW:(p + 1) * BW].reshape(8 * RB, BW),
                wout[k // 2, k % 2, y], NT_DIMS, preferred_element_type=F32,
            )
            part = one if part is None else part + one
        if b in opened:
            gh[b] += part
        else:
            gh[b] = part
            opened.add(b)

    ready = set()

    mine = pl.ds(pl.multiple_of(pc.c * HH, HH), HH)
    theirs = pl.ds(pl.multiple_of((1 - pc.c) * HH, HH), HH)
    wc, wa, wb, wz, wo = ({} for _ in range(5))

    def do_w2(k):
        b = k % 2
        if k >= 2:
            copy.leave([wc[k - 2]] + wa[k - 2] + wb[k - 2])

        def tile(y, _):
            cols = pl.ds(pl.multiple_of(k * 4 * BW + y * BW, BW), BW)
            w2[b, y] = dot(act_t[...], rt[:, :, cols].reshape(ROWS, BW)).astype(BF)
            return 0

        lax.fori_loop(0, 4, tile, 0)
        wc[k] = copy(w2.at[b, :, theirs], cr2.at[k], pc.CO)

    def do_w2a(k):
        b, y = k % 2, pc.ys(2)
        wc[k].wait_recv()
        w2[b, y, mine] = w2[b, y, mine] + cr2[k, y]
        wa[k] = []
        for d, to in enumerate((pc.YP, pc.YM)):
            rows = pl.ds(pl.multiple_of(pc.c * HH + d * HH // 2, HH // 2), HH // 2)
            wa[k].append(copy(w2.at[b, y, rows], ya2.at[k, d], to))

    def do_w2b(k):
        b = k % 2
        wb[k] = []
        for d, (r, to) in enumerate(((1, pc.YP), (3, pc.YM))):
            y = pc.ys(r)
            w2[b, y, mine] = w2[b, y, mine] + cr2[k, y]
            wa[k][d].wait_recv()
            rows = pl.ds(pl.multiple_of(pc.c * HH + d * HH // 2, HH // 2), HH // 2)
            w2[b, y, rows] = w2[b, y, rows] + ya2[k, d]
            wb[k].append(copy(w2.at[b, y, mine], yb2.at[k, d], to))

    def do_w2c(k):
        for cp in wb[k]:
            cp.wait_recv()
        ss[k] = (
            w2[k % 2, pc.y, mine].astype(F32) + cr2[k, pc.y].astype(F32)
            + yb2[k, 0].astype(F32) + yb2[k, 1].astype(F32)
        ).astype(BF)

    def do_w2z(q):
        wz[q] = copy(ss.at[1 - pc.zl + 2 * q], zr2.at[q], pc.ZL)

    def do_w2s(q):
        wz[q].wait_recv()
        ss[pc.zl + 2 * q] = ss[pc.zl + 2 * q] + zr2[q]

    def do_w2o(_):
        wo[0] = copy(ss.at[pc.zl + 2 * (1 - pc.c)], o2, pc.CO)

    def do_w2f(_):
        wo[0].wait_recv()
        gw2_ref[mine, :] = ss[pc.zl + 2 * pc.c]
        gw2_ref[theirs, :] = o2[...]

    gx, ga, gb, wi = {}, {}, {}, {}

    def share(z, n=1):
        return pl.ds(pl.multiple_of((pc.c * 8 + pc.y * 2 + z) * 320, 320), n * 320)

    def do_wi1(_):
        wi[1] = [copy(win_hbm.at[share(1 - pc.zl)], win2.at[share(1 - pc.zl)], pc.ZX)]

    def pass_on(n, refs):
        for cp in wi[n - 1]:
            cp.wait_recv()
        wi[n] = [copy(win2.at[rows], win2.at[rows], to) for rows, to in refs]

    def do_wi2(_):
        pass_on(2, [(share(pc.zl), pc.ZL)])

    def do_wi3(_):
        pass_on(3, [(share(0, 2), pc.YP), (share(0, 2), pc.YM)])

    def do_wi4(_):
        at = lambda k, z: pl.ds(pl.multiple_of((pc.c * 8 + pc.ys(k) * 2 + z) * 320, 320), 320)
        pass_on(4, [(at(3, 0), pc.YP), (at(1, 1), pc.YM)])

    def do_wi5(_):
        pass_on(5, [(pl.ds(pl.multiple_of(pc.c * 2560, 2560), 2560), pc.CO)])

    def do_gp(b):
        rows = pl.ds(b * RB, RB)
        gp[:, :, rows, :] = (
            (gh[b].reshape(8, RB, HID) * pre[:, rows, :]).astype(BF).reshape(4, 2, RB, HID)
        )
        copy.leave(list(co.values()) + list(zl.values()))
        gx[b] = copy(gp.at[:, 1 - pc.zh, rows], gp2.at[:, rows], pc.ZX)

    def do_gy(b):
        for cp in wi.pop(5, []):
            cp.wait_recv()
        gx[b].wait_recv()

    def do_gn(i):
        b, j = i // 4, i % 4
        rows, at = pl.ds(b * RB, RB), slice(j * VW, (j + 1) * VW)
        part = lax.dot_general(
            gp[:, pc.zh, rows, :].reshape(4 * RB, HID), win[at, :], NT_DIMS, preferred_element_type=F32
        ) + lax.dot_general(
            gp2[:, rows, :].reshape(4 * RB, HID), win2[at, :], NT_DIMS, preferred_element_type=F32
        )
        big[:, 0, rows, at] = part.astype(BF).reshape(4, RB, VW)
        ga[i] = [
            copy(
                big.at[pc.xs(2), 0, rows, pl.ds(j * VW + d * VW // 2, VW // 2)],
                xa.at[d, rows, pl.ds(j * VW // 2, VW // 2)], to,
            )
            for d, to in enumerate((pc.XP, pc.XM))
        ]

    def do_g2(i):
        b, j = i // 4, i % 4
        rows, at = pl.ds(b * RB, RB), pl.ds(j * VW, VW)
        gb[i] = []
        for d, (k, to) in enumerate(((1, pc.XP), (3, pc.XM))):
            ga[i][d].wait_recv()
            half = pl.ds(j * VW + d * VW // 2, VW // 2)
            near = pc.xs(k)
            big[near, 0, rows, half] = big[near, 0, rows, half] + xa[d, rows, pl.ds(j * VW // 2, VW // 2)]
            gb[i].append(copy(big.at[near, 0, rows, at], xb.at[d, rows, at], to))

    def do_g3(i):
        b, j = i // 4, i % 4
        rows, at = pl.ds(b * RB, RB), pl.ds(j * VW, VW)
        for cp in gb[i]:
            cp.wait_recv()
        total = (
            big[pc.x, 0, rows, at].astype(F32) + xb[0, rows, at].astype(F32) + xb[1, rows, at].astype(F32)
        )
        xhat, inv = standardized(j, b * RB, RB)
        t = total * gain
        mig_ref[rows, at] = (
            (t - jnp.mean(t, axis=1, keepdims=True) - xhat * jnp.mean(t * xhat, axis=1, keepdims=True)) * inv
        ).astype(BF)

    vc, va, vb, vz, ve, vf, vg = {}, {}, {}, {}, [], [], []
    col_a, col_b = (pl.ds(0, 128), pl.ds(128, 128)), pl.ds(256, 128)

    def w1(z, y, cols, row=0, rows=320):
        return wout.at[pc.c, z, y, pl.ds(row, rows), cols]

    def do_g1(k):
        y = pc.ys(k)

        def tile(z, _):
            cols = pl.ds(pl.multiple_of((z * 4 + y) * 640, 128), 640)
            part = lax.dot_general(
                nt[:, :, cols].reshape(ROWS, 640), gp[...].reshape(ROWS, HID), TN_DIMS,
                preferred_element_type=F32,
            ).astype(BF)
            wout[0, z, y, 0:320, 0:HID] = part[0:320]
            wout[1, z, y, 0:320, 0:HID] = part[320:640]
            return 0

        lax.fori_loop(0, 2, tile, 0)
        vc[k] = copy(wout.at[1 - pc.c, :, y, pl.ds(0, 320), pl.ds(0, HID)], cr1.at[:, y], pc.CO)

    def do_v0(k):
        y = pc.ys(k)
        vc[k].wait_recv()
        for z in range(2):
            part = w1(z, y, pl.ds(0, HID))
            part[...] = part[...] + cr1[z, y]

    def do_f1(p):
        va[p] = [
            copy(w1(slice(None), pc.ys(2), col_a[p], d * 160, 160), ya1.at[p, d], to)
            for d, to in enumerate((pc.YP, pc.YM))
        ]

    def do_f2(p):
        vb[p] = []
        for d, (r, to) in enumerate(((1, pc.YP), (3, pc.YM))):
            y = pc.ys(r)
            va[p][d].wait_recv()
            for z in range(2):
                part = w1(z, y, col_a[p], d * 160, 160)
                part[...] = part[...] + ya1[p, d, z]
            vb[p].append(copy(w1(slice(None), y, col_a[p]), yb1.at[p, d], to))

    def total_a(p, z):
        return (
            w1(z, pc.y, col_a[p])[...].astype(F32) + yb1[p, 0, z].astype(F32) + yb1[p, 1, z].astype(F32)
        )

    def do_f3(p):
        for cp in vb[p]:
            cp.wait_recv()
        there = w1(1 - pc.zl, pc.y, col_a[p])
        there[...] = total_a(p, 1 - pc.zl).astype(BF)
        vz[p] = copy(there, zr1.at[p], pc.ZL)

    def do_f4(p):
        vz[p].wait_recv()
        gw1_ref[:, p * 128:(p + 1) * 128] = (total_a(p, pc.zl) + zr1[p].astype(F32)).astype(BF)

    def do_e1(_):
        ve.append(copy(w1(1 - pc.zl, slice(None), col_b), eb1, pc.ZL))

    def do_e2(_):
        ve[0].wait_recv()
        for k in (2, 1, 3, 0):
            y = pc.ys(k)
            part = w1(pc.zl, y, col_b)
            part[...] = part[...] + eb1[y]
            if k == 2:
                for d, to in enumerate((pc.YP, pc.YM)):
                    vf.append(copy(w1(pc.zl, y, col_b, d * 160, 160), ec1.at[d], to))

    def do_e3(_):
        for d, (r, to) in enumerate(((1, pc.YP), (3, pc.YM))):
            y = pc.ys(r)
            vf[d].wait_recv()
            part = w1(pc.zl, y, col_b, d * 160, 160)
            part[...] = part[...] + ec1[d]
            vg.append(copy(w1(pc.zl, y, col_b), ed1.at[d], to))

    def do_e4(_):
        for cp in vg:
            cp.wait_recv()
        gw1_ref[:, 256:384] = (
            w1(pc.zl, pc.y, col_b)[...].astype(F32) + ed1[0].astype(F32) + ed1[1].astype(F32)
        ).astype(BF)

    stages = {
        "pack": do_pack, "ring": do_ring, "route": do_route, "across": do_across, "arrive": do_arrive,
        "norm": do_norm, "pre": do_pre, "act": do_act, "hid": do_hid, "gp": do_gp, "gy": do_gy, "gn": do_gn,
        "g2": do_g2, "g3": do_g3, "wi1": do_wi1, "wi2": do_wi2, "wi3": do_wi3, "wi4": do_wi4, "wi5": do_wi5,
        "w2": do_w2, "w2a": do_w2a, "w2b": do_w2b, "w2c": do_w2c, "w2z": do_w2z, "w2s": do_w2s,
        "w2o": do_w2o, "w2f": do_w2f, "g1": do_g1, "v0": do_v0, "f1": do_f1, "f2": do_f2, "f3": do_f3, "f4": do_f4,
        "e1": do_e1, "e2": do_e2, "e3": do_e3, "e4": do_e4,
    }
    for s in range(1, 6):
        stages["N%d" % s] = lambda i, s=s: getattr(ns[i], "s%d" % s)()
        stages["C%d" % s] = lambda i, s=s: getattr(cs[i], "s%d" % s)()
    for name, i in ORDER:
        stages[name](i)
    copy.finish()
    assert len(copy.all) <= MAX_COPIES


def merger_call(cnt, own, st, gain, bias, gs, feat, win, wout):
    vm = pl.BlockSpec(memory_space=pltpu.VMEM)
    hb = pl.BlockSpec(memory_space=pl.ANY)
    buf = lambda *shape: pltpu.VMEM(shape, BF)
    return pl.pallas_call(
        merger_kernel,
        out_shape=(
            jax.ShapeDtypeStruct((SLOTS, MW), BF),
            jax.ShapeDtypeStruct((320, HID), BF),
            jax.ShapeDtypeStruct((HID, BW), BF),
        ),
        in_specs=[vm, vm, vm, vm, vm, hb, hb, hb, hb],
        out_specs=(vm, vm, vm),
        scratch_shapes=[
            buf(SLOTS, TOK),
            buf(4 * SLOTS, 4 * SLOTS),
            buf(4, 2, SLOTS, D),
            buf(SLOTS, MW),
            buf(MW, HID),
            buf(MW, HID),
            buf(2, 2, 4, HID, BW),
            buf(4, SLOTS, D),
            buf(2, SLOTS, D),
            buf(SLOTS, D),
            buf(8, SLOTS, D),
            buf(8, SLOTS, MW),
            pltpu.VMEM((8, SLOTS, HID), F32),
            pltpu.VMEM((2, 8 * RB, HID), F32),
            buf(HID, ROWS),
            buf(4, 2, SLOTS, HID),
            buf(4, SLOTS, HID),
            buf(2, 4, HID, BW),
            buf(4, 4, HH, BW),
            buf(4, 2, HH // 2, BW),
            buf(4, 2, HH, BW),
            buf(4, HH, BW),
            buf(2, HH, BW),
            buf(HH, BW),
            buf(2, SLOTS, MW // 2),
            buf(2, SLOTS, MW),
            buf(2, 4, 320, HID),
            buf(2, 2, 2, 160, 128),
            buf(2, 2, 2, 320, 128),
            buf(2, 320, 128),
            buf(4, 320, 128),
            buf(2, 160, 128),
            buf(2, 320, 128),
            pltpu.SemaphoreType.DMA((MAX_COPIES,)),
            pltpu.SemaphoreType.DMA((MAX_COPIES,)),
            pltpu.SemaphoreType.DMA((40,)),
        ],
        compiler_params=pltpu.CompilerParams(
            collective_id=0, has_side_effects=True, vmem_limit_bytes=63 * 2**20
        ),
        cost_estimate=pl.CostEstimate(
            flops=2 * 512 * 384 * 31744, bytes_accessed=16 * 2**20, transcendentals=400000
        ),
        name="merger_backward",
    )(cnt, own, st, gain, bias, gs, feat, win, wout)


def finish_kernel(a, b, c, ao, bo, co):
    for i, o in ((a, ao), (b, bo), (c, co)):
        o[...] = i[...]


def finish_call(*arrays):
    vm = pl.BlockSpec(memory_space=pltpu.VMEM)
    return pl.pallas_call(
        finish_kernel,
        out_shape=tuple(jax.ShapeDtypeStruct(a.shape, a.dtype) for a in arrays),
        in_specs=[vm] * 3,
        out_specs=(vm, vm, vm),
        compiler_params=pltpu.CompilerParams(vmem_limit_bytes=63 * 2**20),
        name="write_results",
    )(*arrays)


def local(
    grad_seq, features, merger_norm_gain, w_in, b_in, w_out, image_counts, sample_owner, image_starts
):
    mig, gw1, gw2 = merger_call(
        image_counts, sample_owner, image_starts, merger_norm_gain, b_in,
        grad_seq.reshape(2, 2, SLOTS, D), features[0], w_in, w_out,
    )
    mig, gw1, gw2 = finish_call(mig, gw1, gw2)
    return (mig[None], gw1, gw2)


def solution(mesh):
    in_specs = (
        P("dp", "seq", None),
        P("dp", "seq", None),
        P(),
        P(None, "dp"),
        P("dp"),
        P("dp", None),
        P("dp", None),
        P("dp", None),
        P("dp", None),
    )
    out_specs = (P("dp", "seq", None), P("seq", "dp"), P("dp", "seq"))
    return jax.shard_map(local, mesh=mesh, in_specs=in_specs, out_specs=out_specs, check_vma=False)
```

```python
import jax
import jax.numpy as jnp
from jax import lax
from jax.experimental import pallas as pl
from jax.experimental.pallas import tpu as pltpu
from jax.sharding import PartitionSpec as P

EPS = 1e-06
MESH = pl.DeviceIdType.MESH
BF = jnp.bfloat16
F32 = jnp.float32
I32 = jnp.int32
D = 8192
MW = 5120
VW = 1280
HID = 384
HH = HID // 2
SLOTS = 64
TOK = 256
ROWS = 512
HALF = 32
BW = 512
CW = 1024
UW = BW // 2
CA = 128
RB = 32
NT_DIMS = (((1,), (1,)), ((), ()))
TN_DIMS = (((0,), (0,)), ((), ()))
N_KINDS = "ABAB"
C_KINDS = ("AABA", "ABABA")
CHUNKS = (((0, 2), (2, 2), (4, 2), (6, 2)), ((0, 2), (2, 2), (4, 2), (6, 1), (7, 1)))
W2_UNITS = ((0, 2), (2, 2), (4, 2), (6, 1), (7, 1))
ORDER = (
    ("norm", 0), ("pack", 0), ("pack", 1), ("norm", 1), ("norm", 2), ("ring", 1), ("ring", 0), ("pack", 2),
    ("pack", 3), ("N2", 1), ("pack", 4), ("N2", 0), ("route", 0), ("N2", 2), ("wi1", 0), ("across", 0),
    ("N3", 2), ("ring", 2), ("N3", 0), ("ring", 3), ("norm", 3), ("N3", 1), ("route", 1), ("arrive", 0),
    ("pack", 5), ("pack", 6), ("N4", 0), ("across", 1), ("N4", 2), ("arrive", 1), ("route", 3), ("wi2", 0),
    ("ring", 4), ("C1", 0), ("ring", 6), ("ring", 5), ("across", 3), ("C1", 10), ("route", 2), ("N2", 3),
    ("across", 2), ("N5", 1), ("pack", 7), ("C2", 0), ("route", 4), ("wi3", 0), ("N5", 0), ("C2", 10),
    ("across", 4), ("N3", 3), ("ring", 7), ("route", 6), ("arrive", 3), ("route", 5), ("arrive", 2),
    ("across", 5), ("C1", 11), ("C4", 10), ("C3", 0), ("across", 6), ("C4", 0), ("C1", 1), ("N5", 3),
    ("arrive", 4), ("arrive", 5), ("arrive", 6), ("C1", 2), ("C2", 11), ("route", 7), ("C3", 10), ("pre", 1),
    ("wi4", 0), ("pre", 3), ("pre", 0), ("N5", 2), ("pre", 2), ("C5", 0), ("C2", 1), ("C1", 12), ("hid", 0),
    ("C3", 1), ("act", 0), ("across", 7), ("C5", 10), ("hid", 10), ("C3", 11), ("C4", 1), ("w2", 0),
    ("arrive", 7), ("C1", 13), ("C2", 12), ("wi5", 0), ("C2", 2), ("C5", 11), ("C3", 12), ("C1", 14),
    ("w2a", 0), ("C5", 1), ("w2", 1), ("C1", 3), ("w2a", 1), ("w2b", 0), ("C3", 2), ("C4", 12), ("C2", 14),
    ("C2", 13), ("C2", 3), ("w2b", 1), ("C3", 14), ("C5", 12), ("w2c", 0), ("C5", 2), ("w2", 2), ("C4", 14),
    ("C3", 3), ("C3", 13), ("hid", 2), ("hid", 12), ("w2a", 2), ("C4", 3), ("w2c", 1), ("hid", 11),
    ("C5", 13), ("hid", 13), ("w2z", 0), ("C5", 14), ("hid", 14), ("gp", 1), ("hid", 1), ("w2b", 2),
    ("C5", 3), ("hid", 3), ("gp", 0), ("g1", 2), ("w2", 3), ("gy", 1), ("gn", 6), ("gn", 5), ("v0", 2),
    ("gn", 7), ("e1", 2), ("gn", 4), ("g1", 1), ("g2", 6), ("w2a", 3), ("f1", 0), ("w2c", 2), ("w2", 4),
    ("g2", 5), ("v0", 1), ("e1", 1), ("g2", 7), ("g1", 3), ("w2a", 4), ("gy", 0), ("gn", 1), ("g2", 4),
    ("e2", 2), ("w2s", 0), ("v0", 3), ("e1", 3), ("w2b", 3), ("g1", 0), ("gn", 3), ("w2b", 4), ("v0", 0),
    ("e1", 0), ("gn", 0), ("gn", 2), ("f2", 0), ("g2", 1), ("w2c", 3), ("g3", 6), ("g3", 5), ("w2z", 1),
    ("e2", 1), ("g3", 7), ("g2", 3), ("w2c", 4), ("e2", 3), ("w2z", 2), ("g2", 2), ("g2", 0), ("e3", 0),
    ("g3", 1), ("g3", 4), ("e2", 0), ("f3", 0), ("w2s", 1), ("g3", 2), ("g3", 3), ("w2s", 2), ("w2o", 0),
    ("e4", 0), ("g3", 0), ("w2f", 0), ("f4", 0),
)
MAX_COPIES = 256


def normal_cdf(value):
    return 0.5 * (1.0 + lax.erf(value * 0.7071067811865476))


def normal_pdf(value):
    return jnp.exp(-0.5 * value * value) * 0.3989422804014327


def dot(a, b):
    return jnp.dot(a, b, preferred_element_type=F32)


class Place:
    def __init__(self):
        d = lax.axis_index("dp")
        s = lax.axis_index("seq")
        self.seq = s
        self.x, self.zh = lax.div(d, 2), lax.rem(d, 2)
        self.zl, self.y, self.c = lax.div(s, 8), lax.rem(lax.div(s, 2), 4), lax.rem(s, 2)
        self.XP = self.dev(x=self.xs(1))
        self.XM = self.dev(x=self.xs(3))
        self.YP = self.dev(y=self.ys(1))
        self.YM = self.dev(y=self.ys(3))
        self.ZX = self.dev(zh=1 - self.zh, zl=1 - self.zl)
        self.ZL = self.dev(zl=1 - self.zl)
        self.CO = self.dev(c=1 - self.c)

    def xs(self, k):
        return lax.rem(self.x + k, 4)

    def ys(self, k):
        return lax.rem(self.y + k, 4)

    def dev(self, **kw):
        g = lambda n: kw.get(n, getattr(self, n))
        return (g("x") * 2 + g("zh"), g("zl") * 8 + g("y") * 2 + g("c"))

    def greet(self):
        for to in (self.XP, self.XM, self.YP, self.YM, self.ZX, self.ZL, self.CO):
            pl.semaphore_signal(pltpu.get_barrier_semaphore(), inc=1, device_id=to, device_id_type=MESH)

    def meet(self):
        pl.semaphore_wait(pltpu.get_barrier_semaphore(), 7)


class Copies:
    def __init__(self, send, recv):
        self.send, self.recv, self.all, self.sent = send, recv, [], set()

    def __call__(self, src, dst, to):
        i = len(self.all)
        cp = pltpu.make_async_remote_copy(
            src_ref=src, dst_ref=dst, send_sem=self.send.at[i], recv_sem=self.recv.at[i],
            device_id=to, device_id_type=MESH,
        )
        cp.start()
        self.all.append(cp)
        return cp

    def leave(self, copies):
        for cp in copies:
            if id(cp) not in self.sent:
                self.sent.add(id(cp))
                cp.wait_send()

    def finish(self):
        self.leave(self.all)


class Gather:
    def __init__(self, pc, copy, buf, row, rows, lo, w, z_first):
        self.pc, self.copy, self.buf, self.z_first = pc, copy, buf, z_first
        self.rows, self.lo, self.w, self.r = pl.ds(row, rows), lo, w, []

    def blk(self, k, z, part=0, parts=1):
        w = self.w // parts
        return self.buf.at[self.pc.xs(k) * 2 + z, self.rows, pl.ds(self.lo + part * w, w)]

    def to(self, ref, where):
        return self.copy(ref, ref, where)

    def s1(self):
        pc = self.pc
        own = self.blk(0, pc.zh)
        if self.z_first:
            self.z = self.to(own, pc.ZX)
        self.p, self.m = self.to(own, pc.XP), self.to(own, pc.XM)
        if not self.z_first:
            self.z = self.to(own, pc.ZX)

    def relay(self, z):
        pc = self.pc
        return [self.to(self.blk(3, z, 0, 2), pc.XP), self.to(self.blk(1, z, 1, 2), pc.XM)]

    def s2(self):
        pc = self.pc
        if self.z_first:
            self.z.wait_recv()
            other = self.blk(0, 1 - pc.zh)
            self.zp, self.zm = self.to(other, pc.XP), self.to(other, pc.XM)
        else:
            self.p.wait_recv()
            self.m.wait_recv()
            self.r += self.relay(pc.zh)
            self.f = [self.to(self.blk(3, pc.zh), pc.ZX), self.to(self.blk(1, pc.zh), pc.ZX)]

    def s3(self):
        pc = self.pc
        if self.z_first:
            self.p.wait_recv()
            self.m.wait_recv()
            self.r += self.relay(pc.zh)
        else:
            for cp in self.r:
                cp.wait_recv()
            self.f.append(self.to(self.blk(2, pc.zh), pc.ZX))

    def s4(self):
        self.zp.wait_recv()
        self.zm.wait_recv()
        self.r += self.relay(1 - self.pc.zh)

    def s5(self):
        for cp in self.r if self.z_first else [self.z] + self.f:
            cp.wait_recv()


def routing_tables(pc, cnt, own, st):
    iota = lambda shape, axis: lax.broadcasted_iota(I32, shape, axis)
    one = lambda m: jnp.where(m, 1.0, 0.0).astype(BF)
    i0, i1 = iota((64, 64), 0), iota((64, 64), 1)
    col = lambda r: jnp.sum(jnp.where(i0 == i1, r, 0), axis=1, keepdims=True)
    sh = lax.div(st, TOK)
    cnt_c, own_c, st_c, sh_c = col(cnt), col(own), col(st), col(sh)
    before_o = jnp.sum(jnp.where((own_c == own) & (i0 < i1), cnt_c, 0), axis=0, keepdims=True)
    before_h = jnp.sum(jnp.where((sh_c == sh) & (i1 < i0), cnt, 0), axis=1, keepdims=True)
    off = iota((64, TOK), 1) + pc.seq * TOK - st_c
    inside = (sh_c == pc.seq) & (off >= 0) & (off < cnt_c)
    rank = jnp.sum(jnp.where(inside, before_h + off + 1, 0), axis=0, keepdims=True) - 1
    pack = one(iota((64, TOK), 0) == rank)
    r = iota((256, 64), 0)
    q, k = lax.div(r, 64), lax.rem(r, 64)
    core = pc.c + lax.div(q, 2) * (1 - 2 * pc.c)
    zl = pc.zl + lax.rem(q, 2) * (1 - 2 * pc.zl)
    off = k - before_o
    inside = (own == zl * 8 + pc.y * 2 + core) & (off >= 0) & (off < cnt)
    want = jnp.sum(jnp.where(inside, st + off + 1, 0), axis=1, keepdims=True)
    r = iota((64, 256), 1)
    off = lax.rem(r, 64) - before_h
    inside = (sh_c == pc.zl * 8 + lax.div(r, 64) * 2 + pc.c) & (off >= 0) & (off < cnt_c)
    held = jnp.sum(jnp.where(inside, st_c + off + 1, 0), axis=0, keepdims=True)
    return pack, one((want == held) & (want > 0))


def merger_kernel(
    cnt_ref, own_ref, st_ref, gain_ref, b_ref, gs_hbm, feat_hbm, win_hbm, wout_hbm,
    mig_ref, gw1_ref, gw2_ref,
    pack_m, route_m, big, feat, win, win2, wout, g, hc, hz, rt, nt, pre, gh, act_t, gp, gp2,
    w2, cr2, ya2, yb2, ss, zr2, o2, xa, xb, cr1, ya1, yb1, zr1, eb1, ec1, ed1,
    send, recv, lsem,
):
    pc = Place()
    copy = Copies(send, recv)
    me = pc.x * 2 + pc.zh
    nc = D // CW
    cut = lambda i: pl.ds(i * CW, CW)
    loads = []

    def load(src, dst):
        cp = pltpu.make_async_copy(src, dst, lsem.at[len(loads)])
        cp.start()
        loads.append(cp)
        return cp

    def piece(p):
        return pl.ds(((p // 8) % 2 * 8 + p % 4 * 2 + p // 16) * BW + (p // 4) % 2 * UW, UW)

    pc.greet()
    lf = load(feat_hbm, feat)
    lg = [load(gs_hbm.at[:, :, :, piece(p)], big.at[0:2, :, :, pl.ds(p * UW, UW)]) for p in range(32)]
    gain = gain_ref[...].reshape(1, VW)
    pack_m[...], route_m[...] = routing_tables(pc, cnt_ref[...], own_ref[...], st_ref[...])
    lf.wait()
    lw = load(win_hbm, win)
    lo = [
        load(wout_hbm.at[:, piece(p)], wout.at[p // 16, p // 8 % 2, p // 2 % 4, :, pl.ds(p % 2 * UW, UW)])
        for p in range(32)
    ]
    pc.meet()

    yp, ym, rp, rm, co, zl = ({} for _ in range(6))

    def do_pack(i):
        for p in range(4 * i, 4 * i + 4):
            lg[p].wait()
        g[pc.y, :, cut(i)] = dot(pack_m[...], big[0:2, :, :, cut(i)].reshape(TOK, CW)).astype(BF)
        own = g.at[pc.y, :, cut(i)]
        yp[i] = copy(own, own, pc.YP)
        ym[i] = copy(own, own, pc.YM)

    def do_ring(i):
        yp[i].wait_recv()
        up = g.at[pc.ys(3), pl.ds(0, HALF), cut(i)]
        rp[i] = copy(up, up, pc.YP)
        ym[i].wait_recv()
        down = g.at[pc.ys(1), pl.ds(HALF, HALF), cut(i)]
        rm[i] = copy(down, down, pc.YM)

    def do_route(i):
        rp[i].wait_recv()
        rm[i].wait_recv()
        for j in range(CW // 512):
            cols = pl.ds(i * CW + j * 512, 512)
            big[2:4, :, :, cols] = (
                dot(route_m[...], g[:, :, cols].reshape(4 * SLOTS, 512)).astype(BF).reshape(2, 2, SLOTS, 512)
            )
        co[i] = copy(big.at[3, :, :, cut(i)], hc.at[:, :, cut(i)], pc.CO)

    def do_across(i):
        co[i].wait_recv()
        big[2, :, :, cut(i)] = big[2, :, :, cut(i)] + hc[:, :, cut(i)]
        zl[i] = copy(big.at[2, 1, :, cut(i)], hz.at[:, cut(i)], pc.ZL)

    cs = {
        b * 10 + k: Gather(pc, copy, rt, b * RB, RB, u * CW, n * CW, C_KINDS[b][k] == "A")
        for b in range(2) for k, (u, n) in enumerate(CHUNKS[b])
    }
    ns = [Gather(pc, copy, nt, 0, SLOTS, n * VW, VW, N_KINDS[n] == "A") for n in range(4)]

    def do_arrive(i):
        zl[i].wait_recv()
        rt[me, :, cut(i)] = big[2, 0, :, cut(i)] + hz[:, cut(i)]

    def standardized(n, row=0, rows=SLOTS):
        v = feat[row:row + rows, n * VW:(n + 1) * VW].astype(F32)
        d = v - jnp.mean(v, axis=1, keepdims=True)
        inv = lax.rsqrt(jnp.mean(d * d, axis=1, keepdims=True) + EPS)
        return d * inv, inv

    def do_norm(n):
        nt[me, :, n * VW:(n + 1) * VW] = (standardized(n)[0] * gain).astype(BF)
        ns[n].s1()

    def do_pre(n):
        if not started:
            lw.wait()
        part = dot(
            nt[:, :, n * VW:(n + 1) * VW].reshape(ROWS, VW), win[n * VW:(n + 1) * VW, :]
        ).reshape(8, SLOTS, HID)
        if started:
            pre[...] += part
        else:
            pre[...] = part + b_ref[...].reshape(1, 1, HID)
            started.append(n)

    started = []

    def do_act(_):
        def tile(k, _):
            at = pl.ds(k * 2, 2)
            v = pre[at].reshape(128, HID)
            cdf = normal_cdf(v)
            act_t[:, pl.ds(pl.multiple_of(k * 128, 128), 128)] = (v * cdf).T.astype(BF)
            pre[at] = (cdf + v * normal_pdf(v)).reshape(2, SLOTS, HID)
            return 0

        lax.fori_loop(0, 4, tile, 0)

    opened = set()

    def do_hid(i):
        b = i // 10
        u, n = CHUNKS[b][i % 10]
        part = None
        for q in range(2 * u, 2 * (u + n)):
            for p in (2 * q, 2 * q + 1):
                if p not in ready:
                    lo[p].wait()
                    ready.add(p)
            one = lax.dot_general(
                rt[:, b * RB:(b + 1) * RB, q * BW:(q + 1) * BW].reshape(8 * RB, BW),
                wout[q // 8, q // 4 % 2, q % 4], NT_DIMS, preferred_element_type=F32,
            )
            part = one if part is None else part + one
        if b in opened:
            gh[b] += part
        else:
            gh[b] = part
            opened.add(b)

    ready = set()

    mine = pl.ds(pl.multiple_of(pc.c * HH, HH), HH)
    theirs = pl.ds(pl.multiple_of((1 - pc.c) * HH, HH), HH)
    wc, wa, wb, wz, wo = ({} for _ in range(5))

    def part_rows(d):
        return pl.ds(pl.multiple_of(pc.c * HH + d * HH // 2, HH // 2), HH // 2)

    def do_w2(w):
        b, (u, n) = w % 2, W2_UNITS[w]
        if w >= 2:
            copy.leave([wc[w - 2]] + wa[w - 2] + wb[w - 2])
        for i in range(n):
            for y in (0, 2):
                lo_col = (u + i) * CW + y * UW
                part = dot(act_t[...], rt[:, :, lo_col:lo_col + BW].reshape(ROWS, BW)).astype(BF)
                w2[b, i, y] = part[:, 0:UW]
                w2[b, i, y + 1] = part[:, UW:BW]
        wc[w] = copy(w2.at[b, pl.ds(0, n), :, theirs], cr2.at[pl.ds(u, n)], pc.CO)

    def do_w2a(w):
        b, (u, n), y = w % 2, W2_UNITS[w], pc.ys(2)
        wc[w].wait_recv()
        for i in range(n):
            w2[b, i, y, mine] = w2[b, i, y, mine] + cr2[u + i, y]
        wa[w] = [
            copy(w2.at[b, pl.ds(0, n), y, part_rows(d)], ya2.at[d, pl.ds(u, n)], to)
            for d, to in enumerate((pc.YP, pc.YM))
        ]

    def do_w2b(w):
        b, (u, n) = w % 2, W2_UNITS[w]
        wb[w] = []
        for d, (r, to) in enumerate(((1, pc.YP), (3, pc.YM))):
            y = pc.ys(r)
            wa[w][d].wait_recv()
            for i in range(n):
                w2[b, i, y, mine] = w2[b, i, y, mine] + cr2[u + i, y]
                w2[b, i, y, part_rows(d)] = w2[b, i, y, part_rows(d)] + ya2[d, u + i]
            wb[w].append(copy(w2.at[b, pl.ds(0, n), y, mine], yb2.at[d, pl.ds(u, n)], to))

    def do_w2c(w):
        b, (u, n) = w % 2, W2_UNITS[w]
        for cp in wb[w]:
            cp.wait_recv()
        for i in range(n):
            ss[u + i] = (
                w2[b, i, pc.y, mine].astype(F32) + cr2[u + i, pc.y].astype(F32)
                + yb2[0, u + i].astype(F32) + yb2[1, u + i].astype(F32)
            ).astype(BF)

    z_parts = ((0, 0, 2), (1, 0, 1), (1, 1, 1))

    def unit(z, c, half=0):
        return (z + 2 * c) * 2 + half

    def do_w2z(q):
        c, half, n = z_parts[q]
        wz[q] = copy(ss.at[pl.ds(unit(1 - pc.zl, c, half), n)], zr2.at[c, pl.ds(half, n)], pc.ZL)

    def do_w2s(q):
        c, half, n = z_parts[q]
        wz[q].wait_recv()
        for h in range(half, half + n):
            ss[unit(pc.zl, c, h)] = ss[unit(pc.zl, c, h)] + zr2[c, h]

    def do_w2o(_):
        wo[0] = copy(ss.at[pl.ds(unit(pc.zl, 1 - pc.c), 2)], o2, pc.CO)

    def do_w2f(_):
        wo[0].wait_recv()
        for h in range(2):
            gw2_ref[mine, h * UW:(h + 1) * UW] = ss[unit(pc.zl, pc.c, h)]
            gw2_ref[theirs, h * UW:(h + 1) * UW] = o2[h]

    gx, ga, gb, wi = {}, {}, {}, {}

    def share(z, n=1):
        return pl.ds(pl.multiple_of((pc.c * 8 + pc.y * 2 + z) * 320, 320), n * 320)

    def do_wi1(_):
        wi[1] = [copy(win_hbm.at[share(1 - pc.zl)], win2.at[share(1 - pc.zl)], pc.ZX)]

    def pass_on(n, refs):
        for cp in wi[n - 1]:
            cp.wait_recv()
        wi[n] = [copy(win2.at[rows], win2.at[rows], to) for rows, to in refs]

    def do_wi2(_):
        pass_on(2, [(share(pc.zl), pc.ZL)])

    def do_wi3(_):
        pass_on(3, [(share(0, 2), pc.YP), (share(0, 2), pc.YM)])

    def do_wi4(_):
        at = lambda k, z: pl.ds(pl.multiple_of((pc.c * 8 + pc.ys(k) * 2 + z) * 320, 320), 320)
        pass_on(4, [(at(3, 0), pc.YP), (at(1, 1), pc.YM)])

    def do_wi5(_):
        pass_on(5, [(pl.ds(pl.multiple_of(pc.c * 2560, 2560), 2560), pc.CO)])

    def do_gp(b):
        rows = pl.ds(b * RB, RB)
        gp[:, :, rows, :] = (
            (gh[b].reshape(8, RB, HID) * pre[:, rows, :]).astype(BF).reshape(4, 2, RB, HID)
        )
        copy.leave(list(co.values()) + list(zl.values()))
        gx[b] = copy(gp.at[:, 1 - pc.zh, rows], gp2.at[:, rows], pc.ZX)

    def do_gy(b):
        for cp in wi.pop(5, []):
            cp.wait_recv()
        gx[b].wait_recv()

    def do_gn(i):
        b, j = i // 4, i % 4
        rows, at = pl.ds(b * RB, RB), slice(j * VW, (j + 1) * VW)
        part = lax.dot_general(
            gp[:, pc.zh, rows, :].reshape(4 * RB, HID), win[at, :], NT_DIMS, preferred_element_type=F32
        ) + lax.dot_general(
            gp2[:, rows, :].reshape(4 * RB, HID), win2[at, :], NT_DIMS, preferred_element_type=F32
        )
        big[:, 0, rows, at] = part.astype(BF).reshape(4, RB, VW)
        ga[i] = [
            copy(
                big.at[pc.xs(2), 0, rows, pl.ds(j * VW + d * VW // 2, VW // 2)],
                xa.at[d, rows, pl.ds(j * VW // 2, VW // 2)], to,
            )
            for d, to in enumerate((pc.XP, pc.XM))
        ]

    def do_g2(i):
        b, j = i // 4, i % 4
        rows, at = pl.ds(b * RB, RB), pl.ds(j * VW, VW)
        gb[i] = []
        for d, (k, to) in enumerate(((1, pc.XP), (3, pc.XM))):
            ga[i][d].wait_recv()
            half = pl.ds(j * VW + d * VW // 2, VW // 2)
            near = pc.xs(k)
            big[near, 0, rows, half] = big[near, 0, rows, half] + xa[d, rows, pl.ds(j * VW // 2, VW // 2)]
            gb[i].append(copy(big.at[near, 0, rows, at], xb.at[d, rows, at], to))

    def do_g3(i):
        b, j = i // 4, i % 4
        rows, at = pl.ds(b * RB, RB), pl.ds(j * VW, VW)
        for cp in gb[i]:
            cp.wait_recv()
        total = (
            big[pc.x, 0, rows, at].astype(F32) + xb[0, rows, at].astype(F32) + xb[1, rows, at].astype(F32)
        )
        xhat, inv = standardized(j, b * RB, RB)
        t = total * gain
        mig_ref[rows, at] = (
            (t - jnp.mean(t, axis=1, keepdims=True) - xhat * jnp.mean(t * xhat, axis=1, keepdims=True)) * inv
        ).astype(BF)

    vc, va, vb, vz, ve, vf, vg = {}, {}, {}, {}, {}, [], []
    col_a, col_b = [pl.ds(p * 128, 128) for p in range(CA // 128)], pl.ds(CA, HID - CA)

    def w1(z, y, cols, row=0, rows=320):
        return wout.at[pc.c, z, y, pl.ds(row, rows), cols]

    def do_g1(k):
        y = pc.ys(k)

        def tile(z, _):
            cols = pl.ds(pl.multiple_of((z * 4 + y) * 640, 128), 640)
            part = lax.dot_general(
                nt[:, :, cols].reshape(ROWS, 640), gp[...].reshape(ROWS, HID), TN_DIMS,
                preferred_element_type=F32,
            ).astype(BF)
            wout[0, z, y, 0:320, 0:HID] = part[0:320]
            wout[1, z, y, 0:320, 0:HID] = part[320:640]
            return 0

        lax.fori_loop(0, 2, tile, 0)
        vc[k] = copy(wout.at[1 - pc.c, :, y, pl.ds(0, 320), pl.ds(0, HID)], cr1.at[:, y], pc.CO)

    def do_v0(k):
        y = pc.ys(k)
        vc[k].wait_recv()
        for z in range(2):
            part = w1(z, y, pl.ds(0, HID))
            part[...] = part[...] + cr1[z, y]

    def do_f1(p):
        va[p] = [
            copy(w1(slice(None), pc.ys(2), col_a[p], d * 160, 160), ya1.at[p, d], to)
            for d, to in enumerate((pc.YP, pc.YM))
        ]

    def do_f2(p):
        vb[p] = []
        for d, (r, to) in enumerate(((1, pc.YP), (3, pc.YM))):
            y = pc.ys(r)
            va[p][d].wait_recv()
            for z in range(2):
                part = w1(z, y, col_a[p], d * 160, 160)
                part[...] = part[...] + ya1[p, d, z]
            vb[p].append(copy(w1(slice(None), y, col_a[p]), yb1.at[p, d], to))

    def total_a(p, z):
        return (
            w1(z, pc.y, col_a[p])[...].astype(F32) + yb1[p, 0, z].astype(F32) + yb1[p, 1, z].astype(F32)
        )

    def do_f3(p):
        for cp in vb[p]:
            cp.wait_recv()
        there = w1(1 - pc.zl, pc.y, col_a[p])
        there[...] = total_a(p, 1 - pc.zl).astype(BF)
        vz[p] = copy(there, zr1.at[p], pc.ZL)

    def do_f4(p):
        vz[p].wait_recv()
        gw1_ref[:, p * 128:(p + 1) * 128] = (total_a(p, pc.zl) + zr1[p].astype(F32)).astype(BF)

    def do_e1(k):
        y = pc.ys(k)
        ve[k] = copy(w1(1 - pc.zl, y, col_b), eb1.at[y], pc.ZL)

    def do_e2(k):
        y = pc.ys(k)
        ve[k].wait_recv()
        part = w1(pc.zl, y, col_b)
        part[...] = part[...] + eb1[y]
        if k == 2:
            for d, to in enumerate((pc.YP, pc.YM)):
                vf.append(copy(w1(pc.zl, y, col_b, d * 160, 160), ec1.at[d], to))

    def do_e3(_):
        for d, (r, to) in enumerate(((1, pc.YP), (3, pc.YM))):
            y = pc.ys(r)
            vf[d].wait_recv()
            part = w1(pc.zl, y, col_b, d * 160, 160)
            part[...] = part[...] + ec1[d]
            vg.append(copy(w1(pc.zl, y, col_b), ed1.at[d], to))

    def do_e4(_):
        for cp in vg:
            cp.wait_recv()
        gw1_ref[:, CA:HID] = (
            w1(pc.zl, pc.y, col_b)[...].astype(F32) + ed1[0].astype(F32) + ed1[1].astype(F32)
        ).astype(BF)

    stages = {
        "pack": do_pack, "ring": do_ring, "route": do_route, "across": do_across, "arrive": do_arrive,
        "norm": do_norm, "pre": do_pre, "act": do_act, "hid": do_hid, "gp": do_gp, "gy": do_gy, "gn": do_gn,
        "g2": do_g2, "g3": do_g3, "wi1": do_wi1, "wi2": do_wi2, "wi3": do_wi3, "wi4": do_wi4, "wi5": do_wi5,
        "w2": do_w2, "w2a": do_w2a, "w2b": do_w2b, "w2c": do_w2c, "w2z": do_w2z, "w2s": do_w2s,
        "w2o": do_w2o, "w2f": do_w2f, "g1": do_g1, "v0": do_v0, "f1": do_f1, "f2": do_f2, "f3": do_f3, "f4": do_f4,
        "e1": do_e1, "e2": do_e2, "e3": do_e3, "e4": do_e4,
    }
    for s in range(1, 6):
        stages["N%d" % s] = lambda i, s=s: getattr(ns[i], "s%d" % s)()
        stages["C%d" % s] = lambda i, s=s: getattr(cs[i], "s%d" % s)()
    for name, i in ORDER:
        stages[name](i)
    copy.finish()
    assert len(copy.all) <= MAX_COPIES


def merger_call(cnt, own, st, gain, bias, gs, feat, win, wout):
    vm = pl.BlockSpec(memory_space=pltpu.VMEM)
    hb = pl.BlockSpec(memory_space=pl.ANY)
    buf = lambda *shape: pltpu.VMEM(shape, BF)
    return pl.pallas_call(
        merger_kernel,
        out_shape=(
            jax.ShapeDtypeStruct((SLOTS, MW), BF),
            jax.ShapeDtypeStruct((320, HID), BF),
            jax.ShapeDtypeStruct((HID, BW), BF),
        ),
        in_specs=[vm, vm, vm, vm, vm, hb, hb, hb, hb],
        out_specs=(vm, vm, vm),
        scratch_shapes=[
            buf(SLOTS, TOK),
            buf(4 * SLOTS, 4 * SLOTS),
            buf(4, 2, SLOTS, D),
            buf(SLOTS, MW),
            buf(MW, HID),
            buf(MW, HID),
            buf(2, 2, 4, HID, BW),
            buf(4, SLOTS, D),
            buf(2, SLOTS, D),
            buf(SLOTS, D),
            buf(8, SLOTS, D),
            buf(8, SLOTS, MW),
            pltpu.VMEM((8, SLOTS, HID), F32),
            pltpu.VMEM((2, 8 * RB, HID), F32),
            buf(HID, ROWS),
            buf(4, 2, SLOTS, HID),
            buf(4, SLOTS, HID),
            buf(2, 2, 4, HID, UW),
            buf(8, 4, HH, UW),
            buf(2, 8, HH // 2, UW),
            buf(2, 8, HH, UW),
            buf(8, HH, UW),
            buf(2, 2, HH, UW),
            buf(2, HH, UW),
            buf(2, SLOTS, MW // 2),
            buf(2, SLOTS, MW),
            buf(2, 4, 320, HID),
            buf(CA // 128, 2, 2, 160, 128),
            buf(CA // 128, 2, 2, 320, 128),
            buf(CA // 128, 320, 128),
            buf(4, 320, HID - CA),
            buf(2, 160, HID - CA),
            buf(2, 320, HID - CA),
            pltpu.SemaphoreType.DMA((MAX_COPIES,)),
            pltpu.SemaphoreType.DMA((MAX_COPIES,)),
            pltpu.SemaphoreType.DMA((72,)),
        ],
        compiler_params=pltpu.CompilerParams(
            collective_id=0, has_side_effects=True, vmem_limit_bytes=63 * 2**20
        ),
        cost_estimate=pl.CostEstimate(
            flops=2 * 512 * 384 * 31744, bytes_accessed=16 * 2**20, transcendentals=400000
        ),
        name="merger_backward",
    )(cnt, own, st, gain, bias, gs, feat, win, wout)


def finish_kernel(a, b, c, ao, bo, co, av, bv, cv, sem):
    ways = [
        (src.at[rows], mid.at[rows], dst.at[rows])
        for src, mid, dst, rows in (
            (a, av, ao, pl.ds(0, 32)), (c, cv, co, pl.ds(0, 384)), (b, bv, bo, pl.ds(0, 320)), (a, av, ao, pl.ds(32, 32))
        )
    ]
    ins = [pltpu.make_async_copy(src, mid, sem.at[n]) for n, (src, mid, _) in enumerate(ways)]
    outs = [pltpu.make_async_copy(mid, dst, sem.at[n + 4]) for n, (_, mid, dst) in enumerate(ways)]
    for cp in ins:
        cp.start()
    for cp, out in zip(ins, outs):
        cp.wait()
        out.start()
    for out in outs:
        out.wait()


def finish_call(*arrays):
    hb = pl.BlockSpec(memory_space=pl.ANY)
    return pl.pallas_call(
        finish_kernel,
        out_shape=tuple(jax.ShapeDtypeStruct(a.shape, a.dtype) for a in arrays),
        in_specs=[hb] * 3,
        out_specs=(hb, hb, hb),
        scratch_shapes=[pltpu.VMEM(a.shape, a.dtype) for a in arrays] + [pltpu.SemaphoreType.DMA((8,))],
        compiler_params=pltpu.CompilerParams(vmem_limit_bytes=63 * 2**20),
        name="write_results",
    )(*arrays)


def local(
    grad_seq, features, merger_norm_gain, w_in, b_in, w_out, image_counts, sample_owner, image_starts
):
    mig, gw1, gw2 = merger_call(
        image_counts, sample_owner, image_starts, merger_norm_gain, b_in,
        grad_seq.reshape(2, 2, SLOTS, D), features[0], w_in, w_out,
    )
    mig, gw1, gw2 = finish_call(mig, gw1, gw2)
    return (mig[None], gw1, gw2)


def solution(mesh):
    in_specs = (
        P("dp", "seq", None),
        P("dp", "seq", None),
        P(),
        P(None, "dp"),
        P("dp"),
        P("dp", None),
        P("dp", None),
        P("dp", None),
        P("dp", None),
    )
    out_specs = (P("dp", "seq", None), P("seq", "dp"), P("dp", "seq"))
    return jax.shard_map(local, mesh=mesh, in_specs=in_specs, out_specs=out_specs, check_vma=False)
```

```python
import jax
import jax.numpy as jnp
from jax import lax
from jax.experimental import pallas as pl
from jax.experimental.pallas import tpu as pltpu
from jax.sharding import PartitionSpec as P

EPS = 1e-06
MESH = pl.DeviceIdType.MESH
BF = jnp.bfloat16
F32 = jnp.float32
I32 = jnp.int32
D = 8192
MW = 5120
VW = 1280
HID = 384
HH = HID // 2
SLOTS = 64
TOK = 256
ROWS = 512
HALF = 32
BW = 512
CW = 1024
UW = BW // 2
CA = 128
RB = 32
NT_DIMS = (((1,), (1,)), ((), ()))
TN_DIMS = (((0,), (0,)), ((), ()))
N_KINDS = "ABAB"
C_KINDS = ("AABA", "ABABA")
CHUNKS = (((0, 2), (2, 2), (4, 2), (6, 2)), ((0, 2), (2, 2), (4, 2), (6, 1), (7, 1)))
W2_UNITS = ((0, 2), (2, 2), (4, 2), (6, 1), (7, 1))
ORDER = (
    ("norm", 0), ("pack", 0), ("pack", 1), ("norm", 1), ("norm", 2), ("ring", 1), ("ring", 0), ("pack", 2),
    ("pack", 3), ("N2", 1), ("pack", 4), ("N2", 0), ("route", 0), ("N2", 2), ("wi1", 0), ("across", 0),
    ("N3", 2), ("ring", 2), ("N3", 0), ("ring", 3), ("norm", 3), ("N3", 1), ("route", 1), ("arrive", 0),
    ("pack", 5), ("pack", 6), ("N4", 0), ("across", 1), ("N4", 2), ("arrive", 1), ("route", 3), ("wi2", 0),
    ("ring", 4), ("C1", 0), ("ring", 6), ("ring", 5), ("across", 3), ("C1", 10), ("route", 2), ("N2", 3),
    ("across", 2), ("N5", 1), ("pack", 7), ("C2", 0), ("route", 4), ("wi3", 0), ("N5", 0), ("C2", 10),
    ("across", 4), ("N3", 3), ("ring", 7), ("route", 6), ("arrive", 3), ("route", 5), ("arrive", 2),
    ("across", 5), ("C1", 11), ("C4", 10), ("C3", 0), ("across", 6), ("C4", 0), ("C1", 1), ("N5", 3),
    ("arrive", 4), ("arrive", 5), ("arrive", 6), ("C1", 2), ("C2", 11), ("route", 7), ("C3", 10), ("pre", 1),
    ("wi4", 0), ("pre", 3), ("pre", 0), ("N5", 2), ("pre", 2), ("C5", 0), ("C2", 1), ("C1", 12), ("hid", 0),
    ("C3", 1), ("act", 0), ("across", 7), ("C5", 10), ("hid", 10), ("C3", 11), ("C4", 1), ("w2", 0),
    ("arrive", 7), ("C1", 13), ("C2", 12), ("wi5", 0), ("C2", 2), ("C5", 11), ("C3", 12), ("C1", 14),
    ("w2a", 0), ("C5", 1), ("w2", 1), ("C1", 3), ("w2a", 1), ("w2b", 0), ("C3", 2), ("C4", 12), ("C2", 14),
    ("C2", 13), ("C2", 3), ("w2b", 1), ("C3", 14), ("C5", 12), ("w2c", 0), ("C5", 2), ("w2", 2), ("C4", 14),
    ("C3", 3), ("C3", 13), ("hid", 2), ("hid", 12), ("w2a", 2), ("C4", 3), ("w2c", 1), ("hid", 11),
    ("C5", 13), ("hid", 13), ("w2z", 0), ("C5", 14), ("hid", 14), ("gp", 1), ("hid", 1), ("w2b", 2),
    ("C5", 3), ("hid", 3), ("gp", 0), ("g1", 2), ("w2", 3), ("gy", 1), ("gn", 6), ("gn", 5), ("v0", 2),
    ("gn", 7), ("e1", 2), ("gn", 4), ("g1", 1), ("g2", 6), ("w2a", 3), ("f1", 0), ("w2c", 2), ("w2", 4),
    ("g2", 5), ("v0", 1), ("e1", 1), ("g2", 7), ("g1", 3), ("w2a", 4), ("gy", 0), ("gn", 1), ("g2", 4),
    ("e2", 2), ("w2s", 0), ("v0", 3), ("e1", 3), ("w2b", 3), ("g1", 0), ("gn", 3), ("w2b", 4), ("v0", 0),
    ("e1", 0), ("gn", 0), ("gn", 2), ("f2", 0), ("g2", 1), ("w2c", 3), ("g3", 6), ("g3", 5), ("w2z", 1),
    ("e2", 1), ("g3", 7), ("g2", 3), ("w2c", 4), ("e2", 3), ("w2z", 2), ("g2", 2), ("g2", 0), ("e3", 0),
    ("g3", 1), ("g3", 4), ("e2", 0), ("f3", 0), ("w2s", 1), ("g3", 2), ("g3", 3), ("w2s", 2), ("w2o", 0),
    ("e4", 0), ("g3", 0), ("w2f", 0), ("f4", 0),
)
MAX_COPIES = 256


def normal_cdf(value):
    return 0.5 * (1.0 + lax.erf(value * 0.7071067811865476))


def normal_pdf(value):
    return jnp.exp(-0.5 * value * value) * 0.3989422804014327


def dot(a, b):
    return jnp.dot(a, b, preferred_element_type=F32)


class Place:
    def __init__(self):
        d = lax.axis_index("dp")
        s = lax.axis_index("seq")
        self.seq = s
        self.x, self.zh = lax.div(d, 2), lax.rem(d, 2)
        self.zl, self.y, self.c = lax.div(s, 8), lax.rem(lax.div(s, 2), 4), lax.rem(s, 2)
        self.XP = self.dev(x=self.xs(1))
        self.XM = self.dev(x=self.xs(3))
        self.YP = self.dev(y=self.ys(1))
        self.YM = self.dev(y=self.ys(3))
        self.ZX = self.dev(zh=1 - self.zh, zl=1 - self.zl)
        self.ZL = self.dev(zl=1 - self.zl)
        self.CO = self.dev(c=1 - self.c)

    def xs(self, k):
        return lax.rem(self.x + k, 4)

    def ys(self, k):
        return lax.rem(self.y + k, 4)

    def dev(self, **kw):
        g = lambda n: kw.get(n, getattr(self, n))
        return (g("x") * 2 + g("zh"), g("zl") * 8 + g("y") * 2 + g("c"))

    def greet(self):
        for to in (self.XP, self.XM, self.YP, self.YM, self.ZX, self.ZL, self.CO):
            pl.semaphore_signal(pltpu.get_barrier_semaphore(), inc=1, device_id=to, device_id_type=MESH)

    def meet(self):
        pl.semaphore_wait(pltpu.get_barrier_semaphore(), 7)


class Copies:
    def __init__(self, send, recv):
        self.send, self.recv, self.all, self.sent = send, recv, [], set()

    def __call__(self, src, dst, to):
        i = len(self.all)
        cp = pltpu.make_async_remote_copy(
            src_ref=src, dst_ref=dst, send_sem=self.send.at[i], recv_sem=self.recv.at[i],
            device_id=to, device_id_type=MESH,
        )
        cp.start()
        self.all.append(cp)
        return cp

    def leave(self, copies):
        for cp in copies:
            if id(cp) not in self.sent:
                self.sent.add(id(cp))
                cp.wait_send()

    def finish(self):
        self.leave(self.all)


class Gather:
    def __init__(self, pc, copy, buf, row, rows, lo, w, z_first):
        self.pc, self.copy, self.buf, self.z_first = pc, copy, buf, z_first
        self.rows, self.lo, self.w, self.r = pl.ds(row, rows), lo, w, []

    def blk(self, k, z, part=0, parts=1):
        w = self.w // parts
        return self.buf.at[self.pc.xs(k) * 2 + z, self.rows, pl.ds(self.lo + part * w, w)]

    def to(self, ref, where):
        return self.copy(ref, ref, where)

    def s1(self):
        pc = self.pc
        own = self.blk(0, pc.zh)
        if self.z_first:
            self.z = self.to(own, pc.ZX)
        self.p, self.m = self.to(own, pc.XP), self.to(own, pc.XM)
        if not self.z_first:
            self.z = self.to(own, pc.ZX)

    def relay(self, z):
        pc = self.pc
        return [self.to(self.blk(3, z, 0, 2), pc.XP), self.to(self.blk(1, z, 1, 2), pc.XM)]

    def s2(self):
        pc = self.pc
        if self.z_first:
            self.z.wait_recv()
            other = self.blk(0, 1 - pc.zh)
            self.zp, self.zm = self.to(other, pc.XP), self.to(other, pc.XM)
        else:
            self.p.wait_recv()
            self.m.wait_recv()
            self.r += self.relay(pc.zh)
            self.f = [self.to(self.blk(3, pc.zh), pc.ZX), self.to(self.blk(1, pc.zh), pc.ZX)]

    def s3(self):
        pc = self.pc
        if self.z_first:
            self.p.wait_recv()
            self.m.wait_recv()
            self.r += self.relay(pc.zh)
        else:
            for cp in self.r:
                cp.wait_recv()
            self.f.append(self.to(self.blk(2, pc.zh), pc.ZX))

    def s4(self):
        self.zp.wait_recv()
        self.zm.wait_recv()
        self.r += self.relay(1 - self.pc.zh)

    def s5(self):
        for cp in self.r if self.z_first else [self.z] + self.f:
            cp.wait_recv()


def routing_tables(pc, cnt, own, st):
    iota = lambda shape, axis: lax.broadcasted_iota(I32, shape, axis)
    one = lambda m: jnp.where(m, 1.0, 0.0).astype(BF)
    i0, i1 = iota((64, 64), 0), iota((64, 64), 1)
    col = lambda r: jnp.sum(jnp.where(i0 == i1, r, 0), axis=1, keepdims=True)
    sh = lax.div(st, TOK)
    cnt_c, own_c, st_c, sh_c = col(cnt), col(own), col(st), col(sh)
    before_o = jnp.sum(jnp.where((own_c == own) & (i0 < i1), cnt_c, 0), axis=0, keepdims=True)
    before_h = jnp.sum(jnp.where((sh_c == sh) & (i1 < i0), cnt, 0), axis=1, keepdims=True)
    off = iota((64, TOK), 1) + pc.seq * TOK - st_c
    inside = (sh_c == pc.seq) & (off >= 0) & (off < cnt_c)
    rank = jnp.sum(jnp.where(inside, before_h + off + 1, 0), axis=0, keepdims=True) - 1
    pack = one(iota((64, TOK), 0) == rank)
    r = iota((256, 64), 0)
    q, k = lax.div(r, 64), lax.rem(r, 64)
    core = pc.c + lax.div(q, 2) * (1 - 2 * pc.c)
    zl = pc.zl + lax.rem(q, 2) * (1 - 2 * pc.zl)
    off = k - before_o
    inside = (own == zl * 8 + pc.y * 2 + core) & (off >= 0) & (off < cnt)
    want = jnp.sum(jnp.where(inside, st + off + 1, 0), axis=1, keepdims=True)
    r = iota((64, 256), 1)
    off = lax.rem(r, 64) - before_h
    inside = (sh_c == pc.zl * 8 + lax.div(r, 64) * 2 + pc.c) & (off >= 0) & (off < cnt_c)
    held = jnp.sum(jnp.where(inside, st_c + off + 1, 0), axis=0, keepdims=True)
    return pack, one((want == held) & (want > 0))


def merger_kernel(
    cnt_ref, own_ref, st_ref, gain_ref, b_ref, gs_hbm, feat_hbm, win_hbm, wout_hbm,
    mig_ref, gw1_ref, gw2_ref,
    pack_m, route_m, big, feat, win, win2, wout, g, hc, hz, rt, nt, pre, gh, act_t, gp, gp2,
    w2, cr2, ya2, yb2, ss, zr2, o2, xa, xb, cr1, ya1, yb1, zr1, eb1, ec1, ed1,
    send, recv, lsem,
):
    pc = Place()
    copy = Copies(send, recv)
    me = pc.x * 2 + pc.zh
    nc = D // CW
    cut = lambda i: pl.ds(i * CW, CW)
    loads = []

    def load(src, dst):
        cp = pltpu.make_async_copy(src, dst, lsem.at[len(loads)])
        cp.start()
        loads.append(cp)
        return cp

    def piece(p):
        return pl.ds(((p // 8) % 2 * 8 + p % 4 * 2 + p // 16) * BW + (p // 4) % 2 * UW, UW)

    pc.greet()
    lf = [load(feat_hbm.at[:, pl.ds(n * VW, VW)], feat.at[:, pl.ds(n * VW, VW)]) for n in range(4)]
    lg = [load(gs_hbm.at[:, :, :, piece(p)], big.at[0:2, :, :, pl.ds(p * UW, UW)]) for p in range(32)]
    gain = gain_ref[...].reshape(1, VW)
    lw, lo = [], []

    def load_weights():
        lw.append(load(win_hbm, win))
        for p in range(32):
            to = wout.at[p // 16, p // 8 % 2, p // 2 % 4, :, pl.ds(p % 2 * UW, UW)]
            lo.append(load(wout_hbm.at[:, piece(p)], to))

    routed = []

    yp, ym, rp, rm, co, zl = ({} for _ in range(6))

    def do_pack(i):
        if not routed:
            pack_m[...], route_m[...] = routing_tables(pc, cnt_ref[...], own_ref[...], st_ref[...])
            routed.append(i)
        for p in range(4 * i, 4 * i + 4):
            lg[p].wait()
        g[pc.y, :, cut(i)] = dot(pack_m[...], big[0:2, :, :, cut(i)].reshape(TOK, CW)).astype(BF)
        own = g.at[pc.y, :, cut(i)]
        yp[i] = copy(own, own, pc.YP)
        ym[i] = copy(own, own, pc.YM)

    def do_ring(i):
        yp[i].wait_recv()
        up = g.at[pc.ys(3), pl.ds(0, HALF), cut(i)]
        rp[i] = copy(up, up, pc.YP)
        ym[i].wait_recv()
        down = g.at[pc.ys(1), pl.ds(HALF, HALF), cut(i)]
        rm[i] = copy(down, down, pc.YM)

    def do_route(i):
        rp[i].wait_recv()
        rm[i].wait_recv()
        for j in range(CW // 512):
            cols = pl.ds(i * CW + j * 512, 512)
            big[2:4, :, :, cols] = (
                dot(route_m[...], g[:, :, cols].reshape(4 * SLOTS, 512)).astype(BF).reshape(2, 2, SLOTS, 512)
            )
        co[i] = copy(big.at[3, :, :, cut(i)], hc.at[:, :, cut(i)], pc.CO)

    def do_across(i):
        co[i].wait_recv()
        big[2, :, :, cut(i)] = big[2, :, :, cut(i)] + hc[:, :, cut(i)]
        zl[i] = copy(big.at[2, 1, :, cut(i)], hz.at[:, cut(i)], pc.ZL)

    cs = {
        b * 10 + k: Gather(pc, copy, rt, b * RB, RB, u * CW, n * CW, C_KINDS[b][k] == "A")
        for b in range(2) for k, (u, n) in enumerate(CHUNKS[b])
    }
    ns = [Gather(pc, copy, nt, 0, SLOTS, n * VW, VW, N_KINDS[n] == "A") for n in range(4)]

    def do_arrive(i):
        zl[i].wait_recv()
        rt[me, :, cut(i)] = big[2, 0, :, cut(i)] + hz[:, cut(i)]

    def standardized(n, row=0, rows=SLOTS):
        v = feat[row:row + rows, n * VW:(n + 1) * VW].astype(F32)
        d = v - jnp.mean(v, axis=1, keepdims=True)
        inv = lax.rsqrt(jnp.mean(d * d, axis=1, keepdims=True) + EPS)
        return d * inv, inv

    def do_norm(n):
        lf[n].wait()
        nt[me, :, n * VW:(n + 1) * VW] = (standardized(n)[0] * gain).astype(BF)
        if n == 0:
            pc.meet()
        ns[n].s1()
        if n == 0:
            load_weights()

    def do_pre(n):
        if not started:
            lw[0].wait()
        part = dot(
            nt[:, :, n * VW:(n + 1) * VW].reshape(ROWS, VW), win[n * VW:(n + 1) * VW, :]
        ).reshape(8, SLOTS, HID)
        if started:
            pre[...] += part
        else:
            pre[...] = part + b_ref[...].reshape(1, 1, HID)
            started.append(n)

    started = []

    def do_act(_):
        def tile(k, _):
            at = pl.ds(k * 2, 2)
            v = pre[at].reshape(128, HID)
            cdf = normal_cdf(v)
            act_t[:, pl.ds(pl.multiple_of(k * 128, 128), 128)] = (v * cdf).T.astype(BF)
            pre[at] = (cdf + v * normal_pdf(v)).reshape(2, SLOTS, HID)
            return 0

        lax.fori_loop(0, 4, tile, 0)

    opened = set()

    def do_hid(i):
        b = i // 10
        u, n = CHUNKS[b][i % 10]
        part = None
        for q in range(2 * u, 2 * (u + n)):
            for p in (2 * q, 2 * q + 1):
                if p not in ready:
                    lo[p].wait()
                    ready.add(p)
            one = lax.dot_general(
                rt[:, b * RB:(b + 1) * RB, q * BW:(q + 1) * BW].reshape(8 * RB, BW),
                wout[q // 8, q // 4 % 2, q % 4], NT_DIMS, preferred_element_type=F32,
            )
            part = one if part is None else part + one
        if b in opened:
            gh[b] += part
        else:
            gh[b] = part
            opened.add(b)

    ready = set()

    mine = pl.ds(pl.multiple_of(pc.c * HH, HH), HH)
    theirs = pl.ds(pl.multiple_of((1 - pc.c) * HH, HH), HH)
    wc, wa, wb, wz, wo = ({} for _ in range(5))

    def part_rows(d):
        return pl.ds(pl.multiple_of(pc.c * HH + d * HH // 2, HH // 2), HH // 2)

    def do_w2(w):
        b, (u, n) = w % 2, W2_UNITS[w]
        if w >= 2:
            copy.leave([wc[w - 2]] + wa[w - 2] + wb[w - 2])
        for i in range(n):
            for y in (0, 2):
                lo_col = (u + i) * CW + y * UW
                part = dot(act_t[...], rt[:, :, lo_col:lo_col + BW].reshape(ROWS, BW)).astype(BF)
                w2[b, i, y] = part[:, 0:UW]
                w2[b, i, y + 1] = part[:, UW:BW]
        wc[w] = copy(w2.at[b, pl.ds(0, n), :, theirs], cr2.at[pl.ds(u, n)], pc.CO)

    def do_w2a(w):
        b, (u, n), y = w % 2, W2_UNITS[w], pc.ys(2)
        wc[w].wait_recv()
        for i in range(n):
            w2[b, i, y, mine] = w2[b, i, y, mine] + cr2[u + i, y]
        wa[w] = [
            copy(w2.at[b, pl.ds(0, n), y, part_rows(d)], ya2.at[d, pl.ds(u, n)], to)
            for d, to in enumerate((pc.YP, pc.YM))
        ]

    def do_w2b(w):
        b, (u, n) = w % 2, W2_UNITS[w]
        wb[w] = []
        for d, (r, to) in enumerate(((1, pc.YP), (3, pc.YM))):
            y = pc.ys(r)
            wa[w][d].wait_recv()
            for i in range(n):
                w2[b, i, y, mine] = w2[b, i, y, mine] + cr2[u + i, y]
                w2[b, i, y, part_rows(d)] = w2[b, i, y, part_rows(d)] + ya2[d, u + i]
            wb[w].append(copy(w2.at[b, pl.ds(0, n), y, mine], yb2.at[d, pl.ds(u, n)], to))

    def do_w2c(w):
        b, (u, n) = w % 2, W2_UNITS[w]
        for cp in wb[w]:
            cp.wait_recv()
        for i in range(n):
            ss[u + i] = (
                w2[b, i, pc.y, mine].astype(F32) + cr2[u + i, pc.y].astype(F32)
                + yb2[0, u + i].astype(F32) + yb2[1, u + i].astype(F32)
            ).astype(BF)

    z_parts = ((0, 0, 2), (1, 0, 1), (1, 1, 1))

    def unit(z, c, half=0):
        return (z + 2 * c) * 2 + half

    def do_w2z(q):
        c, half, n = z_parts[q]
        wz[q] = copy(ss.at[pl.ds(unit(1 - pc.zl, c, half), n)], zr2.at[c, pl.ds(half, n)], pc.ZL)

    def do_w2s(q):
        c, half, n = z_parts[q]
        wz[q].wait_recv()
        for h in range(half, half + n):
            ss[unit(pc.zl, c, h)] = ss[unit(pc.zl, c, h)] + zr2[c, h]

    def do_w2o(_):
        wo[0] = copy(ss.at[pl.ds(unit(pc.zl, 1 - pc.c), 2)], o2, pc.CO)

    def do_w2f(_):
        wo[0].wait_recv()
        for h in range(2):
            gw2_ref[mine, h * UW:(h + 1) * UW] = ss[unit(pc.zl, pc.c, h)]
            gw2_ref[theirs, h * UW:(h + 1) * UW] = o2[h]

    gx, ga, gb, wi = {}, {}, {}, {}

    def share(z, n=1):
        return pl.ds(pl.multiple_of((pc.c * 8 + pc.y * 2 + z) * 320, 320), n * 320)

    def do_wi1(_):
        wi[1] = [copy(win_hbm.at[share(1 - pc.zl)], win2.at[share(1 - pc.zl)], pc.ZX)]

    def pass_on(n, refs):
        for cp in wi[n - 1]:
            cp.wait_recv()
        wi[n] = [copy(win2.at[rows], win2.at[rows], to) for rows, to in refs]

    def do_wi2(_):
        pass_on(2, [(share(pc.zl), pc.ZL)])

    def do_wi3(_):
        pass_on(3, [(share(0, 2), pc.YP), (share(0, 2), pc.YM)])

    def do_wi4(_):
        at = lambda k, z: pl.ds(pl.multiple_of((pc.c * 8 + pc.ys(k) * 2 + z) * 320, 320), 320)
        pass_on(4, [(at(3, 0), pc.YP), (at(1, 1), pc.YM)])

    def do_wi5(_):
        pass_on(5, [(pl.ds(pl.multiple_of(pc.c * 2560, 2560), 2560), pc.CO)])

    def do_gp(b):
        rows = pl.ds(b * RB, RB)
        gp[:, :, rows, :] = (
            (gh[b].reshape(8, RB, HID) * pre[:, rows, :]).astype(BF).reshape(4, 2, RB, HID)
        )
        copy.leave(list(co.values()) + list(zl.values()))
        gx[b] = copy(gp.at[:, 1 - pc.zh, rows], gp2.at[:, rows], pc.ZX)

    def do_gy(b):
        for cp in wi.pop(5, []):
            cp.wait_recv()
        gx[b].wait_recv()

    def do_gn(i):
        b, j = i // 4, i % 4
        rows, at = pl.ds(b * RB, RB), slice(j * VW, (j + 1) * VW)
        part = lax.dot_general(
            gp[:, pc.zh, rows, :].reshape(4 * RB, HID), win[at, :], NT_DIMS, preferred_element_type=F32
        ) + lax.dot_general(
            gp2[:, rows, :].reshape(4 * RB, HID), win2[at, :], NT_DIMS, preferred_element_type=F32
        )
        big[:, 0, rows, at] = part.astype(BF).reshape(4, RB, VW)
        ga[i] = [
            copy(
                big.at[pc.xs(2), 0, rows, pl.ds(j * VW + d * VW // 2, VW // 2)],
                xa.at[d, rows, pl.ds(j * VW // 2, VW // 2)], to,
            )
            for d, to in enumerate((pc.XP, pc.XM))
        ]

    def do_g2(i):
        b, j = i // 4, i % 4
        rows, at = pl.ds(b * RB, RB), pl.ds(j * VW, VW)
        gb[i] = []
        for d, (k, to) in enumerate(((1, pc.XP), (3, pc.XM))):
            ga[i][d].wait_recv()
            half = pl.ds(j * VW + d * VW // 2, VW // 2)
            near = pc.xs(k)
            big[near, 0, rows, half] = big[near, 0, rows, half] + xa[d, rows, pl.ds(j * VW // 2, VW // 2)]
            gb[i].append(copy(big.at[near, 0, rows, at], xb.at[d, rows, at], to))

    def do_g3(i):
        b, j = i // 4, i % 4
        rows, at = pl.ds(b * RB, RB), pl.ds(j * VW, VW)
        for cp in gb[i]:
            cp.wait_recv()
        total = (
            big[pc.x, 0, rows, at].astype(F32) + xb[0, rows, at].astype(F32) + xb[1, rows, at].astype(F32)
        )
        xhat, inv = standardized(j, b * RB, RB)
        t = total * gain
        mig_ref[rows, at] = (
            (t - jnp.mean(t, axis=1, keepdims=True) - xhat * jnp.mean(t * xhat, axis=1, keepdims=True)) * inv
        ).astype(BF)

    vc, va, vb, vz, ve, vf, vg = {}, {}, {}, {}, {}, [], []
    col_a, col_b = [pl.ds(p * 128, 128) for p in range(CA // 128)], pl.ds(CA, HID - CA)

    def w1(z, y, cols, row=0, rows=320):
        return wout.at[pc.c, z, y, pl.ds(row, rows), cols]

    def do_g1(k):
        y = pc.ys(k)

        def tile(z, _):
            cols = pl.ds(pl.multiple_of((z * 4 + y) * 640, 128), 640)
            part = lax.dot_general(
                nt[:, :, cols].reshape(ROWS, 640), gp[...].reshape(ROWS, HID), TN_DIMS,
                preferred_element_type=F32,
            ).astype(BF)
            wout[0, z, y, 0:320, 0:HID] = part[0:320]
            wout[1, z, y, 0:320, 0:HID] = part[320:640]
            return 0

        lax.fori_loop(0, 2, tile, 0)
        vc[k] = copy(wout.at[1 - pc.c, :, y, pl.ds(0, 320), pl.ds(0, HID)], cr1.at[:, y], pc.CO)

    def do_v0(k):
        y = pc.ys(k)
        vc[k].wait_recv()
        for z in range(2):
            part = w1(z, y, pl.ds(0, HID))
            part[...] = part[...] + cr1[z, y]

    def do_f1(p):
        va[p] = [
            copy(w1(slice(None), pc.ys(2), col_a[p], d * 160, 160), ya1.at[p, d], to)
            for d, to in enumerate((pc.YP, pc.YM))
        ]

    def do_f2(p):
        vb[p] = []
        for d, (r, to) in enumerate(((1, pc.YP), (3, pc.YM))):
            y = pc.ys(r)
            va[p][d].wait_recv()
            for z in range(2):
                part = w1(z, y, col_a[p], d * 160, 160)
                part[...] = part[...] + ya1[p, d, z]
            vb[p].append(copy(w1(slice(None), y, col_a[p]), yb1.at[p, d], to))

    def total_a(p, z):
        return (
            w1(z, pc.y, col_a[p])[...].astype(F32) + yb1[p, 0, z].astype(F32) + yb1[p, 1, z].astype(F32)
        )

    def do_f3(p):
        for cp in vb[p]:
            cp.wait_recv()
        there = w1(1 - pc.zl, pc.y, col_a[p])
        there[...] = total_a(p, 1 - pc.zl).astype(BF)
        vz[p] = copy(there, zr1.at[p], pc.ZL)

    def do_f4(p):
        vz[p].wait_recv()
        gw1_ref[:, p * 128:(p + 1) * 128] = (total_a(p, pc.zl) + zr1[p].astype(F32)).astype(BF)

    def do_e1(k):
        y = pc.ys(k)
        ve[k] = copy(w1(1 - pc.zl, y, col_b), eb1.at[y], pc.ZL)

    def do_e2(k):
        y = pc.ys(k)
        ve[k].wait_recv()
        part = w1(pc.zl, y, col_b)
        part[...] = part[...] + eb1[y]
        if k == 2:
            for d, to in enumerate((pc.YP, pc.YM)):
                vf.append(copy(w1(pc.zl, y, col_b, d * 160, 160), ec1.at[d], to))

    def do_e3(_):
        for d, (r, to) in enumerate(((1, pc.YP), (3, pc.YM))):
            y = pc.ys(r)
            vf[d].wait_recv()
            part = w1(pc.zl, y, col_b, d * 160, 160)
            part[...] = part[...] + ec1[d]
            vg.append(copy(w1(pc.zl, y, col_b), ed1.at[d], to))

    def do_e4(_):
        for cp in vg:
            cp.wait_recv()
        gw1_ref[:, CA:HID] = (
            w1(pc.zl, pc.y, col_b)[...].astype(F32) + ed1[0].astype(F32) + ed1[1].astype(F32)
        ).astype(BF)

    stages = {
        "pack": do_pack, "ring": do_ring, "route": do_route, "across": do_across, "arrive": do_arrive,
        "norm": do_norm, "pre": do_pre, "act": do_act, "hid": do_hid, "gp": do_gp, "gy": do_gy, "gn": do_gn,
        "g2": do_g2, "g3": do_g3, "wi1": do_wi1, "wi2": do_wi2, "wi3": do_wi3, "wi4": do_wi4, "wi5": do_wi5,
        "w2": do_w2, "w2a": do_w2a, "w2b": do_w2b, "w2c": do_w2c, "w2z": do_w2z, "w2s": do_w2s,
        "w2o": do_w2o, "w2f": do_w2f, "g1": do_g1, "v0": do_v0, "f1": do_f1, "f2": do_f2, "f3": do_f3, "f4": do_f4,
        "e1": do_e1, "e2": do_e2, "e3": do_e3, "e4": do_e4,
    }
    for s in range(1, 6):
        stages["N%d" % s] = lambda i, s=s: getattr(ns[i], "s%d" % s)()
        stages["C%d" % s] = lambda i, s=s: getattr(cs[i], "s%d" % s)()
    for name, i in ORDER:
        stages[name](i)
    copy.finish()
    assert len(copy.all) <= MAX_COPIES


def merger_call(cnt, own, st, gain, bias, gs, feat, win, wout):
    vm = pl.BlockSpec(memory_space=pltpu.VMEM)
    hb = pl.BlockSpec(memory_space=pl.ANY)
    buf = lambda *shape: pltpu.VMEM(shape, BF)
    return pl.pallas_call(
        merger_kernel,
        out_shape=(
            jax.ShapeDtypeStruct((SLOTS, MW), BF),
            jax.ShapeDtypeStruct((320, HID), BF),
            jax.ShapeDtypeStruct((HID, BW), BF),
        ),
        in_specs=[vm, vm, vm, vm, vm, hb, hb, hb, hb],
        out_specs=(vm, vm, vm),
        scratch_shapes=[
            buf(SLOTS, TOK),
            buf(4 * SLOTS, 4 * SLOTS),
            buf(4, 2, SLOTS, D),
            buf(SLOTS, MW),
            buf(MW, HID),
            buf(MW, HID),
            buf(2, 2, 4, HID, BW),
            buf(4, SLOTS, D),
            buf(2, SLOTS, D),
            buf(SLOTS, D),
            buf(8, SLOTS, D),
            buf(8, SLOTS, MW),
            pltpu.VMEM((8, SLOTS, HID), F32),
            pltpu.VMEM((2, 8 * RB, HID), F32),
            buf(HID, ROWS),
            buf(4, 2, SLOTS, HID),
            buf(4, SLOTS, HID),
            buf(2, 2, 4, HID, UW),
            buf(8, 4, HH, UW),
            buf(2, 8, HH // 2, UW),
            buf(2, 8, HH, UW),
            buf(8, HH, UW),
            buf(2, 2, HH, UW),
            buf(2, HH, UW),
            buf(2, SLOTS, MW // 2),
            buf(2, SLOTS, MW),
            buf(2, 4, 320, HID),
            buf(CA // 128, 2, 2, 160, 128),
            buf(CA // 128, 2, 2, 320, 128),
            buf(CA // 128, 320, 128),
            buf(4, 320, HID - CA),
            buf(2, 160, HID - CA),
            buf(2, 320, HID - CA),
            pltpu.SemaphoreType.DMA((MAX_COPIES,)),
            pltpu.SemaphoreType.DMA((MAX_COPIES,)),
            pltpu.SemaphoreType.DMA((72,)),
        ],
        compiler_params=pltpu.CompilerParams(
            collective_id=0, has_side_effects=True, vmem_limit_bytes=63 * 2**20
        ),
        cost_estimate=pl.CostEstimate(
            flops=2 * 512 * 384 * 31744, bytes_accessed=16 * 2**20, transcendentals=400000
        ),
        name="merger_backward",
    )(cnt, own, st, gain, bias, gs, feat, win, wout)


def finish_kernel(a, b, c, ao, bo, co, av, bv, cv, sem):
    ways = [
        (src.at[rows], mid.at[rows], dst.at[rows])
        for src, mid, dst, rows in (
            (a, av, ao, pl.ds(0, 32)), (c, cv, co, pl.ds(0, 384)), (b, bv, bo, pl.ds(0, 320)), (a, av, ao, pl.ds(32, 32))
        )
    ]
    ins = [pltpu.make_async_copy(src, mid, sem.at[n]) for n, (src, mid, _) in enumerate(ways)]
    outs = [pltpu.make_async_copy(mid, dst, sem.at[n + 4]) for n, (_, mid, dst) in enumerate(ways)]
    for cp in ins:
        cp.start()
    for cp, out in zip(ins, outs):
        cp.wait()
        out.start()
    for out in outs:
        out.wait()


def finish_call(*arrays):
    hb = pl.BlockSpec(memory_space=pl.ANY)
    return pl.pallas_call(
        finish_kernel,
        out_shape=tuple(jax.ShapeDtypeStruct(a.shape, a.dtype) for a in arrays),
        in_specs=[hb] * 3,
        out_specs=(hb, hb, hb),
        scratch_shapes=[pltpu.VMEM(a.shape, a.dtype) for a in arrays] + [pltpu.SemaphoreType.DMA((8,))],
        compiler_params=pltpu.CompilerParams(vmem_limit_bytes=63 * 2**20),
        name="write_results",
    )(*arrays)


def local(
    grad_seq, features, merger_norm_gain, w_in, b_in, w_out, image_counts, sample_owner, image_starts
):
    mig, gw1, gw2 = merger_call(
        image_counts, sample_owner, image_starts, merger_norm_gain, b_in,
        grad_seq.reshape(2, 2, SLOTS, D), features[0], w_in, w_out,
    )
    mig, gw1, gw2 = finish_call(mig, gw1, gw2)
    return (mig[None], gw1, gw2)


def solution(mesh):
    in_specs = (
        P("dp", "seq", None),
        P("dp", "seq", None),
        P(),
        P(None, "dp"),
        P("dp"),
        P("dp", None),
        P("dp", None),
        P("dp", None),
        P("dp", None),
    )
    out_specs = (P("dp", "seq", None), P("seq", "dp"), P("dp", "seq"))
    return jax.shard_map(local, mesh=mesh, in_specs=in_specs, out_specs=out_specs, check_vma=False)
```

```python
import jax
import jax.numpy as jnp
from jax import lax
from jax.experimental import pallas as pl
from jax.experimental.pallas import tpu as pltpu
from jax.sharding import PartitionSpec as P

EPS = 1e-06
MESH = pl.DeviceIdType.MESH
BF = jnp.bfloat16
F32 = jnp.float32
I32 = jnp.int32
D = 8192
MW = 5120
VW = 1280
HID = 384
HH = HID // 2
SLOTS = 64
TOK = 256
ROWS = 512
HALF = 32
BW = 512
CW = 1024
UW = BW // 2
CA = 128
RB = 32
NT_DIMS = (((1,), (1,)), ((), ()))
TN_DIMS = (((0,), (0,)), ((), ()))
N_KINDS = "ABAB"
C_KINDS = ("AABA", "ABABA")
CHUNKS = (((0, 2), (2, 2), (4, 2), (6, 2)), ((0, 2), (2, 2), (4, 2), (6, 1), (7, 1)))
W2_UNITS = ((0, 2), (2, 2), (4, 2), (6, 1), (7, 1))
ORDER = (
    ("norm", 0), ("pack", 0), ("pack", 1), ("norm", 1), ("norm", 2), ("ring", 1), ("ring", 0), ("pack", 2),
    ("pack", 3), ("N2", 1), ("pack", 4), ("N2", 0), ("route", 0), ("N2", 2), ("wi1", 0), ("across", 0),
    ("N3", 2), ("ring", 2), ("N3", 0), ("ring", 3), ("norm", 3), ("N3", 1), ("route", 1), ("arrive", 0),
    ("pack", 5), ("pack", 6), ("N4", 0), ("across", 1), ("N4", 2), ("arrive", 1), ("route", 3), ("wi2", 0),
    ("ring", 4), ("C1", 0), ("ring", 6), ("ring", 5), ("across", 3), ("C1", 10), ("route", 2), ("N2", 3),
    ("across", 2), ("N5", 1), ("pack", 7), ("C2", 0), ("route", 4), ("wi3", 0), ("N5", 0), ("C2", 10),
    ("across", 4), ("N3", 3), ("ring", 7), ("route", 6), ("arrive", 3), ("route", 5), ("arrive", 2),
    ("across", 5), ("C1", 11), ("C4", 10), ("C3", 0), ("across", 6), ("C4", 0), ("C1", 1), ("N5", 3),
    ("arrive", 4), ("arrive", 5), ("arrive", 6), ("C1", 2), ("C2", 11), ("route", 7), ("C3", 10), ("pre", 1),
    ("wi4", 0), ("pre", 3), ("pre", 0), ("N5", 2), ("pre", 2), ("C5", 0), ("C2", 1), ("C1", 12), ("hid", 0),
    ("C3", 1), ("act", 0), ("across", 7), ("C5", 10), ("hid", 10), ("C3", 11), ("C4", 1), ("w2", 0),
    ("arrive", 7), ("C1", 13), ("C2", 12), ("wi5", 0), ("C2", 2), ("C5", 11), ("C3", 12), ("C1", 14),
    ("w2a", 0), ("C5", 1), ("w2", 1), ("C1", 3), ("w2a", 1), ("w2b", 0), ("C3", 2), ("C4", 12), ("C2", 14),
    ("C2", 13), ("C2", 3), ("w2b", 1), ("C3", 14), ("C5", 12), ("w2c", 0), ("C5", 2), ("w2", 2), ("C4", 14),
    ("C3", 3), ("C3", 13), ("hid", 2), ("hid", 12), ("w2a", 2), ("C4", 3), ("w2c", 1), ("hid", 11),
    ("C5", 13), ("hid", 13), ("w2z", 0), ("C5", 14), ("hid", 14), ("gp", 1), ("hid", 1), ("w2b", 2),
    ("C5", 3), ("hid", 3), ("gp", 0), ("g1", 2), ("w2", 3), ("gy", 1), ("gn", 6), ("gn", 5), ("v0", 2),
    ("gn", 7), ("e1", 2), ("gn", 4), ("g1", 1), ("g2", 6), ("w2a", 3), ("f1", 0), ("w2c", 2), ("w2", 4),
    ("g2", 5), ("v0", 1), ("e1", 1), ("g2", 7), ("g1", 3), ("w2a", 4), ("gy", 0), ("gn", 1), ("g2", 4),
    ("e2", 2), ("w2s", 0), ("v0", 3), ("e1", 3), ("w2b", 3), ("g1", 0), ("gn", 3), ("w2b", 4), ("v0", 0),
    ("e1", 0), ("gn", 0), ("gn", 2), ("f2", 0), ("g2", 1), ("w2c", 3), ("g3", 6), ("g3", 5), ("w2z", 1),
    ("e2", 1), ("g3", 7), ("g2", 3), ("w2c", 4), ("e2", 3), ("w2z", 2), ("g2", 2), ("g2", 0), ("e3", 0),
    ("g3", 1), ("g3", 4), ("e2", 0), ("f3", 0), ("w2s", 1), ("g3", 2), ("g3", 3), ("w2s", 2), ("w2o", 0),
    ("e4", 0), ("g3", 0), ("w2f", 0), ("f4", 0),
)
MAX_COPIES = 256


def normal_cdf(value):
    return 0.5 * (1.0 + lax.erf(value * 0.7071067811865476))


def normal_pdf(value):
    return jnp.exp(-0.5 * value * value) * 0.3989422804014327


def dot(a, b):
    return jnp.dot(a, b, preferred_element_type=F32)


class Place:
    def __init__(self):
        d = lax.axis_index("dp")
        s = lax.axis_index("seq")
        self.seq = s
        self.x, self.zh = lax.div(d, 2), lax.rem(d, 2)
        self.zl, self.y, self.c = lax.div(s, 8), lax.rem(lax.div(s, 2), 4), lax.rem(s, 2)
        self.XP = self.dev(x=self.xs(1))
        self.XM = self.dev(x=self.xs(3))
        self.YP = self.dev(y=self.ys(1))
        self.YM = self.dev(y=self.ys(3))
        self.ZX = self.dev(zh=1 - self.zh, zl=1 - self.zl)
        self.ZL = self.dev(zl=1 - self.zl)
        self.CO = self.dev(c=1 - self.c)

    def xs(self, k):
        return lax.rem(self.x + k, 4)

    def ys(self, k):
        return lax.rem(self.y + k, 4)

    def dev(self, **kw):
        g = lambda n: kw.get(n, getattr(self, n))
        return (g("x") * 2 + g("zh"), g("zl") * 8 + g("y") * 2 + g("c"))

    def greet(self):
        for to in (self.XP, self.XM, self.YP, self.YM, self.ZX, self.ZL, self.CO):
            pl.semaphore_signal(pltpu.get_barrier_semaphore(), inc=1, device_id=to, device_id_type=MESH)

    def meet(self):
        pl.semaphore_wait(pltpu.get_barrier_semaphore(), 7)


class Copies:
    def __init__(self, send, recv):
        self.send, self.recv, self.all, self.sent = send, recv, [], set()

    def __call__(self, src, dst, to):
        i = len(self.all)
        cp = pltpu.make_async_remote_copy(
            src_ref=src, dst_ref=dst, send_sem=self.send.at[i], recv_sem=self.recv.at[i],
            device_id=to, device_id_type=MESH,
        )
        cp.start()
        self.all.append(cp)
        return cp

    def leave(self, copies):
        for cp in copies:
            if id(cp) not in self.sent:
                self.sent.add(id(cp))
                cp.wait_send()

    def finish(self):
        self.leave(self.all)


class Gather:
    def __init__(self, pc, copy, buf, row, rows, lo, w, z_first):
        self.pc, self.copy, self.buf, self.z_first = pc, copy, buf, z_first
        self.rows, self.lo, self.w, self.r = pl.ds(row, rows), lo, w, []

    def blk(self, k, z, part=0, parts=1):
        w = self.w // parts
        return self.buf.at[self.pc.xs(k) * 2 + z, self.rows, pl.ds(self.lo + part * w, w)]

    def to(self, ref, where):
        return self.copy(ref, ref, where)

    def s1(self):
        pc = self.pc
        own = self.blk(0, pc.zh)
        if self.z_first:
            self.z = self.to(own, pc.ZX)
        self.p, self.m = self.to(own, pc.XP), self.to(own, pc.XM)
        if not self.z_first:
            self.z = self.to(own, pc.ZX)

    def relay(self, z):
        pc = self.pc
        return [self.to(self.blk(3, z, 0, 2), pc.XP), self.to(self.blk(1, z, 1, 2), pc.XM)]

    def s2(self):
        pc = self.pc
        if self.z_first:
            self.z.wait_recv()
            other = self.blk(0, 1 - pc.zh)
            self.zp, self.zm = self.to(other, pc.XP), self.to(other, pc.XM)
        else:
            self.p.wait_recv()
            self.m.wait_recv()
            self.r += self.relay(pc.zh)
            self.f = [self.to(self.blk(3, pc.zh), pc.ZX), self.to(self.blk(1, pc.zh), pc.ZX)]

    def s3(self):
        pc = self.pc
        if self.z_first:
            self.p.wait_recv()
            self.m.wait_recv()
            self.r += self.relay(pc.zh)
        else:
            for cp in self.r:
                cp.wait_recv()
            self.f.append(self.to(self.blk(2, pc.zh), pc.ZX))

    def s4(self):
        self.zp.wait_recv()
        self.zm.wait_recv()
        self.r += self.relay(1 - self.pc.zh)

    def s5(self):
        for cp in self.r if self.z_first else [self.z] + self.f:
            cp.wait_recv()


def routing_tables(pc, cnt, own, st):
    iota = lambda shape, axis: lax.broadcasted_iota(I32, shape, axis)
    one = lambda m: jnp.where(m, 1.0, 0.0).astype(BF)
    i0, i1 = iota((64, 64), 0), iota((64, 64), 1)
    col = lambda r: jnp.sum(jnp.where(i0 == i1, r, 0), axis=1, keepdims=True)
    sh = lax.div(st, TOK)
    cnt_c, own_c, st_c, sh_c = col(cnt), col(own), col(st), col(sh)
    before_o = jnp.sum(jnp.where((own_c == own) & (i0 < i1), cnt_c, 0), axis=0, keepdims=True)
    before_h = jnp.sum(jnp.where((sh_c == sh) & (i1 < i0), cnt, 0), axis=1, keepdims=True)
    off = iota((64, TOK), 1) + pc.seq * TOK - st_c
    inside = (sh_c == pc.seq) & (off >= 0) & (off < cnt_c)
    rank = jnp.sum(jnp.where(inside, before_h + off + 1, 0), axis=0, keepdims=True) - 1
    pack = one(iota((64, TOK), 0) == rank)
    r = iota((256, 64), 0)
    q, k = lax.div(r, 64), lax.rem(r, 64)
    core = pc.c + lax.div(q, 2) * (1 - 2 * pc.c)
    zl = pc.zl + lax.rem(q, 2) * (1 - 2 * pc.zl)
    off = k - before_o
    inside = (own == zl * 8 + pc.y * 2 + core) & (off >= 0) & (off < cnt)
    want = jnp.sum(jnp.where(inside, st + off + 1, 0), axis=1, keepdims=True)
    r = iota((64, 256), 1)
    off = lax.rem(r, 64) - before_h
    inside = (sh_c == pc.zl * 8 + lax.div(r, 64) * 2 + pc.c) & (off >= 0) & (off < cnt_c)
    held = jnp.sum(jnp.where(inside, st_c + off + 1, 0), axis=0, keepdims=True)
    return pack, one((want == held) & (want > 0))


def merger_kernel(
    cnt_ref, own_ref, st_ref, gain_ref, b_ref, gs_hbm, feat_hbm, win_hbm, wout_hbm,
    mig_hbm, gw1_hbm, gw2_hbm, mig_ref, gw1_ref, gw2_ref,
    pack_m, route_m, big, feat, win, win2, wout, g, hc, hz, rt, nt, pre, gh, act_t, gp, gp2,
    w2, cr2, ya2, yb2, ss, zr2, o2, xa, xb, cr1, ya1, yb1, zr1, eb1, ec1, ed1,
    send, recv, lsem,
):
    pc = Place()
    copy = Copies(send, recv)
    me = pc.x * 2 + pc.zh
    nc = D // CW
    cut = lambda i: pl.ds(i * CW, CW)
    loads = []

    def load(src, dst):
        cp = pltpu.make_async_copy(src, dst, lsem.at[len(loads)])
        cp.start()
        loads.append(cp)
        return cp

    def piece(p):
        return pl.ds(((p // 8) % 2 * 8 + p % 4 * 2 + p // 16) * BW + (p // 4) % 2 * UW, UW)

    pc.greet()
    lf = [load(feat_hbm.at[:, pl.ds(n * VW, VW)], feat.at[:, pl.ds(n * VW, VW)]) for n in range(4)]
    lg = [load(gs_hbm.at[:, :, :, piece(p)], big.at[0:2, :, :, pl.ds(p * UW, UW)]) for p in range(32)]
    gain = gain_ref[...].reshape(1, VW)
    lw, lo = [], []

    def load_weights():
        lw.append(load(win_hbm, win))
        for p in range(32):
            to = wout.at[p // 16, p // 8 % 2, p // 2 % 4, :, pl.ds(p % 2 * UW, UW)]
            lo.append(load(wout_hbm.at[:, piece(p)], to))

    routed, results = [], []

    yp, ym, rp, rm, co, zl = ({} for _ in range(6))

    def do_pack(i):
        if not routed:
            pack_m[...], route_m[...] = routing_tables(pc, cnt_ref[...], own_ref[...], st_ref[...])
            routed.append(i)
        for p in range(4 * i, 4 * i + 4):
            lg[p].wait()
        g[pc.y, :, cut(i)] = dot(pack_m[...], big[0:2, :, :, cut(i)].reshape(TOK, CW)).astype(BF)
        own = g.at[pc.y, :, cut(i)]
        yp[i] = copy(own, own, pc.YP)
        ym[i] = copy(own, own, pc.YM)

    def do_ring(i):
        yp[i].wait_recv()
        up = g.at[pc.ys(3), pl.ds(0, HALF), cut(i)]
        rp[i] = copy(up, up, pc.YP)
        ym[i].wait_recv()
        down = g.at[pc.ys(1), pl.ds(HALF, HALF), cut(i)]
        rm[i] = copy(down, down, pc.YM)

    def do_route(i):
        rp[i].wait_recv()
        rm[i].wait_recv()
        for j in range(CW // 512):
            cols = pl.ds(i * CW + j * 512, 512)
            big[2:4, :, :, cols] = (
                dot(route_m[...], g[:, :, cols].reshape(4 * SLOTS, 512)).astype(BF).reshape(2, 2, SLOTS, 512)
            )
        co[i] = copy(big.at[3, :, :, cut(i)], hc.at[:, :, cut(i)], pc.CO)

    def do_across(i):
        co[i].wait_recv()
        big[2, :, :, cut(i)] = big[2, :, :, cut(i)] + hc[:, :, cut(i)]
        zl[i] = copy(big.at[2, 1, :, cut(i)], hz.at[:, cut(i)], pc.ZL)

    cs = {
        b * 10 + k: Gather(pc, copy, rt, b * RB, RB, u * CW, n * CW, C_KINDS[b][k] == "A")
        for b in range(2) for k, (u, n) in enumerate(CHUNKS[b])
    }
    ns = [Gather(pc, copy, nt, 0, SLOTS, n * VW, VW, N_KINDS[n] == "A") for n in range(4)]

    def do_arrive(i):
        zl[i].wait_recv()
        rt[me, :, cut(i)] = big[2, 0, :, cut(i)] + hz[:, cut(i)]

    def standardized(n, row=0, rows=SLOTS):
        v = feat[row:row + rows, n * VW:(n + 1) * VW].astype(F32)
        d = v - jnp.mean(v, axis=1, keepdims=True)
        inv = lax.rsqrt(jnp.mean(d * d, axis=1, keepdims=True) + EPS)
        return d * inv, inv

    def do_norm(n):
        lf[n].wait()
        nt[me, :, n * VW:(n + 1) * VW] = (standardized(n)[0] * gain).astype(BF)
        if n == 0:
            pc.meet()
        ns[n].s1()
        if n == 0:
            load_weights()

    def do_pre(n):
        if not started:
            lw[0].wait()
        part = dot(
            nt[:, :, n * VW:(n + 1) * VW].reshape(ROWS, VW), win[n * VW:(n + 1) * VW, :]
        ).reshape(8, SLOTS, HID)
        if started:
            pre[...] += part
        else:
            pre[...] = part + b_ref[...].reshape(1, 1, HID)
            started.append(n)

    started = []

    def do_act(_):
        def tile(k, _):
            at = pl.ds(k * 2, 2)
            v = pre[at].reshape(128, HID)
            cdf = normal_cdf(v)
            act_t[:, pl.ds(pl.multiple_of(k * 128, 128), 128)] = (v * cdf).T.astype(BF)
            pre[at] = (cdf + v * normal_pdf(v)).reshape(2, SLOTS, HID)
            return 0

        lax.fori_loop(0, 4, tile, 0)

    opened = set()

    def do_hid(i):
        b = i // 10
        u, n = CHUNKS[b][i % 10]
        part = None
        for q in range(2 * u, 2 * (u + n)):
            for p in (2 * q, 2 * q + 1):
                if p not in ready:
                    lo[p].wait()
                    ready.add(p)
            one = lax.dot_general(
                rt[:, b * RB:(b + 1) * RB, q * BW:(q + 1) * BW].reshape(8 * RB, BW),
                wout[q // 8, q // 4 % 2, q % 4], NT_DIMS, preferred_element_type=F32,
            )
            part = one if part is None else part + one
        if b in opened:
            gh[b] += part
        else:
            gh[b] = part
            opened.add(b)

    ready = set()

    mine = pl.ds(pl.multiple_of(pc.c * HH, HH), HH)
    theirs = pl.ds(pl.multiple_of((1 - pc.c) * HH, HH), HH)
    wc, wa, wb, wz, wo = ({} for _ in range(5))

    def part_rows(d):
        return pl.ds(pl.multiple_of(pc.c * HH + d * HH // 2, HH // 2), HH // 2)

    def do_w2(w):
        b, (u, n) = w % 2, W2_UNITS[w]
        if w >= 2:
            copy.leave([wc[w - 2]] + wa[w - 2] + wb[w - 2])
        for i in range(n):
            for y in (0, 2):
                lo_col = (u + i) * CW + y * UW
                part = dot(act_t[...], rt[:, :, lo_col:lo_col + BW].reshape(ROWS, BW)).astype(BF)
                w2[b, i, y] = part[:, 0:UW]
                w2[b, i, y + 1] = part[:, UW:BW]
        wc[w] = copy(w2.at[b, pl.ds(0, n), :, theirs], cr2.at[pl.ds(u, n)], pc.CO)

    def do_w2a(w):
        b, (u, n), y = w % 2, W2_UNITS[w], pc.ys(2)
        wc[w].wait_recv()
        for i in range(n):
            w2[b, i, y, mine] = w2[b, i, y, mine] + cr2[u + i, y]
        wa[w] = [
            copy(w2.at[b, pl.ds(0, n), y, part_rows(d)], ya2.at[d, pl.ds(u, n)], to)
            for d, to in enumerate((pc.YP, pc.YM))
        ]

    def do_w2b(w):
        b, (u, n) = w % 2, W2_UNITS[w]
        wb[w] = []
        for d, (r, to) in enumerate(((1, pc.YP), (3, pc.YM))):
            y = pc.ys(r)
            wa[w][d].wait_recv()
            for i in range(n):
                w2[b, i, y, mine] = w2[b, i, y, mine] + cr2[u + i, y]
                w2[b, i, y, part_rows(d)] = w2[b, i, y, part_rows(d)] + ya2[d, u + i]
            wb[w].append(copy(w2.at[b, pl.ds(0, n), y, mine], yb2.at[d, pl.ds(u, n)], to))

    def do_w2c(w):
        b, (u, n) = w % 2, W2_UNITS[w]
        for cp in wb[w]:
            cp.wait_recv()
        for i in range(n):
            ss[u + i] = (
                w2[b, i, pc.y, mine].astype(F32) + cr2[u + i, pc.y].astype(F32)
                + yb2[0, u + i].astype(F32) + yb2[1, u + i].astype(F32)
            ).astype(BF)

    z_parts = ((0, 0, 2), (1, 0, 1), (1, 1, 1))

    def unit(z, c, half=0):
        return (z + 2 * c) * 2 + half

    def do_w2z(q):
        c, half, n = z_parts[q]
        wz[q] = copy(ss.at[pl.ds(unit(1 - pc.zl, c, half), n)], zr2.at[c, pl.ds(half, n)], pc.ZL)

    def do_w2s(q):
        c, half, n = z_parts[q]
        wz[q].wait_recv()
        for h in range(half, half + n):
            ss[unit(pc.zl, c, h)] = ss[unit(pc.zl, c, h)] + zr2[c, h]

    def do_w2o(_):
        wo[0] = copy(ss.at[pl.ds(unit(pc.zl, 1 - pc.c), 2)], o2, pc.CO)

    def do_w2f(_):
        wo[0].wait_recv()
        for h in range(2):
            gw2_ref[mine, h * UW:(h + 1) * UW] = ss[unit(pc.zl, pc.c, h)]
            gw2_ref[theirs, h * UW:(h + 1) * UW] = o2[h]
        results.append(load(gw2_ref, gw2_hbm))

    gx, ga, gb, wi = {}, {}, {}, {}

    def share(z, n=1):
        return pl.ds(pl.multiple_of((pc.c * 8 + pc.y * 2 + z) * 320, 320), n * 320)

    def do_wi1(_):
        wi[1] = [copy(win_hbm.at[share(1 - pc.zl)], win2.at[share(1 - pc.zl)], pc.ZX)]

    def pass_on(n, refs):
        for cp in wi[n - 1]:
            cp.wait_recv()
        wi[n] = [copy(win2.at[rows], win2.at[rows], to) for rows, to in refs]

    def do_wi2(_):
        pass_on(2, [(share(pc.zl), pc.ZL)])

    def do_wi3(_):
        pass_on(3, [(share(0, 2), pc.YP), (share(0, 2), pc.YM)])

    def do_wi4(_):
        at = lambda k, z: pl.ds(pl.multiple_of((pc.c * 8 + pc.ys(k) * 2 + z) * 320, 320), 320)
        pass_on(4, [(at(3, 0), pc.YP), (at(1, 1), pc.YM)])

    def do_wi5(_):
        pass_on(5, [(pl.ds(pl.multiple_of(pc.c * 2560, 2560), 2560), pc.CO)])

    def do_gp(b):
        rows = pl.ds(b * RB, RB)
        gp[:, :, rows, :] = (
            (gh[b].reshape(8, RB, HID) * pre[:, rows, :]).astype(BF).reshape(4, 2, RB, HID)
        )
        copy.leave(list(co.values()) + list(zl.values()))
        gx[b] = copy(gp.at[:, 1 - pc.zh, rows], gp2.at[:, rows], pc.ZX)

    def do_gy(b):
        for cp in wi.pop(5, []):
            cp.wait_recv()
        gx[b].wait_recv()

    def do_gn(i):
        b, j = i // 4, i % 4
        rows, at = pl.ds(b * RB, RB), slice(j * VW, (j + 1) * VW)
        part = lax.dot_general(
            gp[:, pc.zh, rows, :].reshape(4 * RB, HID), win[at, :], NT_DIMS, preferred_element_type=F32
        ) + lax.dot_general(
            gp2[:, rows, :].reshape(4 * RB, HID), win2[at, :], NT_DIMS, preferred_element_type=F32
        )
        big[:, 0, rows, at] = part.astype(BF).reshape(4, RB, VW)
        ga[i] = [
            copy(
                big.at[pc.xs(2), 0, rows, pl.ds(j * VW + d * VW // 2, VW // 2)],
                xa.at[d, rows, pl.ds(j * VW // 2, VW // 2)], to,
            )
            for d, to in enumerate((pc.XP, pc.XM))
        ]

    def do_g2(i):
        b, j = i // 4, i % 4
        rows, at = pl.ds(b * RB, RB), pl.ds(j * VW, VW)
        gb[i] = []
        for d, (k, to) in enumerate(((1, pc.XP), (3, pc.XM))):
            ga[i][d].wait_recv()
            half = pl.ds(j * VW + d * VW // 2, VW // 2)
            near = pc.xs(k)
            big[near, 0, rows, half] = big[near, 0, rows, half] + xa[d, rows, pl.ds(j * VW // 2, VW // 2)]
            gb[i].append(copy(big.at[near, 0, rows, at], xb.at[d, rows, at], to))

    def do_g3(i):
        b, j = i // 4, i % 4
        rows, at = pl.ds(b * RB, RB), pl.ds(j * VW, VW)
        for cp in gb[i]:
            cp.wait_recv()
        total = (
            big[pc.x, 0, rows, at].astype(F32) + xb[0, rows, at].astype(F32) + xb[1, rows, at].astype(F32)
        )
        xhat, inv = standardized(j, b * RB, RB)
        t = total * gain
        mig_ref[rows, at] = (
            (t - jnp.mean(t, axis=1, keepdims=True) - xhat * jnp.mean(t * xhat, axis=1, keepdims=True)) * inv
        ).astype(BF)
        results.append(load(mig_ref.at[rows, at], mig_hbm.at[rows, at]))

    vc, va, vb, vz, ve, vf, vg = {}, {}, {}, {}, {}, [], []
    col_a, col_b = [pl.ds(p * 128, 128) for p in range(CA // 128)], pl.ds(CA, HID - CA)

    def w1(z, y, cols, row=0, rows=320):
        return wout.at[pc.c, z, y, pl.ds(row, rows), cols]

    def do_g1(k):
        y = pc.ys(k)

        def tile(z, _):
            cols = pl.ds(pl.multiple_of((z * 4 + y) * 640, 128), 640)
            part = lax.dot_general(
                nt[:, :, cols].reshape(ROWS, 640), gp[...].reshape(ROWS, HID), TN_DIMS,
                preferred_element_type=F32,
            ).astype(BF)
            wout[0, z, y, 0:320, 0:HID] = part[0:320]
            wout[1, z, y, 0:320, 0:HID] = part[320:640]
            return 0

        lax.fori_loop(0, 2, tile, 0)
        vc[k] = copy(wout.at[1 - pc.c, :, y, pl.ds(0, 320), pl.ds(0, HID)], cr1.at[:, y], pc.CO)

    def do_v0(k):
        y = pc.ys(k)
        vc[k].wait_recv()
        for z in range(2):
            part = w1(z, y, pl.ds(0, HID))
            part[...] = part[...] + cr1[z, y]

    def do_f1(p):
        va[p] = [
            copy(w1(slice(None), pc.ys(2), col_a[p], d * 160, 160), ya1.at[p, d], to)
            for d, to in enumerate((pc.YP, pc.YM))
        ]

    def do_f2(p):
        vb[p] = []
        for d, (r, to) in enumerate(((1, pc.YP), (3, pc.YM))):
            y = pc.ys(r)
            va[p][d].wait_recv()
            for z in range(2):
                part = w1(z, y, col_a[p], d * 160, 160)
                part[...] = part[...] + ya1[p, d, z]
            vb[p].append(copy(w1(slice(None), y, col_a[p]), yb1.at[p, d], to))

    def total_a(p, z):
        return (
            w1(z, pc.y, col_a[p])[...].astype(F32) + yb1[p, 0, z].astype(F32) + yb1[p, 1, z].astype(F32)
        )

    def do_f3(p):
        for cp in vb[p]:
            cp.wait_recv()
        there = w1(1 - pc.zl, pc.y, col_a[p])
        there[...] = total_a(p, 1 - pc.zl).astype(BF)
        vz[p] = copy(there, zr1.at[p], pc.ZL)

    def do_f4(p):
        vz[p].wait_recv()
        gw1_ref[:, p * 128:(p + 1) * 128] = (total_a(p, pc.zl) + zr1[p].astype(F32)).astype(BF)
        cols = pl.ds(p * 128, 128)
        results.append(load(gw1_ref.at[:, cols], gw1_hbm.at[:, cols]))

    def do_e1(k):
        y = pc.ys(k)
        ve[k] = copy(w1(1 - pc.zl, y, col_b), eb1.at[y], pc.ZL)

    def do_e2(k):
        y = pc.ys(k)
        ve[k].wait_recv()
        part = w1(pc.zl, y, col_b)
        part[...] = part[...] + eb1[y]
        if k == 2:
            for d, to in enumerate((pc.YP, pc.YM)):
                vf.append(copy(w1(pc.zl, y, col_b, d * 160, 160), ec1.at[d], to))

    def do_e3(_):
        for d, (r, to) in enumerate(((1, pc.YP), (3, pc.YM))):
            y = pc.ys(r)
            vf[d].wait_recv()
            part = w1(pc.zl, y, col_b, d * 160, 160)
            part[...] = part[...] + ec1[d]
            vg.append(copy(w1(pc.zl, y, col_b), ed1.at[d], to))

    def do_e4(_):
        for cp in vg:
            cp.wait_recv()
        gw1_ref[:, CA:HID] = (
            w1(pc.zl, pc.y, col_b)[...].astype(F32) + ed1[0].astype(F32) + ed1[1].astype(F32)
        ).astype(BF)
        results.append(load(gw1_ref.at[:, col_b], gw1_hbm.at[:, col_b]))

    stages = {
        "pack": do_pack, "ring": do_ring, "route": do_route, "across": do_across, "arrive": do_arrive,
        "norm": do_norm, "pre": do_pre, "act": do_act, "hid": do_hid, "gp": do_gp, "gy": do_gy, "gn": do_gn,
        "g2": do_g2, "g3": do_g3, "wi1": do_wi1, "wi2": do_wi2, "wi3": do_wi3, "wi4": do_wi4, "wi5": do_wi5,
        "w2": do_w2, "w2a": do_w2a, "w2b": do_w2b, "w2c": do_w2c, "w2z": do_w2z, "w2s": do_w2s,
        "w2o": do_w2o, "w2f": do_w2f, "g1": do_g1, "v0": do_v0, "f1": do_f1, "f2": do_f2, "f3": do_f3, "f4": do_f4,
        "e1": do_e1, "e2": do_e2, "e3": do_e3, "e4": do_e4,
    }
    for s in range(1, 6):
        stages["N%d" % s] = lambda i, s=s: getattr(ns[i], "s%d" % s)()
        stages["C%d" % s] = lambda i, s=s: getattr(cs[i], "s%d" % s)()
    for name, i in ORDER:
        stages[name](i)
    copy.finish()
    for cp in results:
        cp.wait()
    assert len(copy.all) <= MAX_COPIES


def merger_call(cnt, own, st, gain, bias, gs, feat, win, wout):
    vm = pl.BlockSpec(memory_space=pltpu.VMEM)
    hb = pl.BlockSpec(memory_space=pl.ANY)
    buf = lambda *shape: pltpu.VMEM(shape, BF)
    return pl.pallas_call(
        merger_kernel,
        out_shape=(
            jax.ShapeDtypeStruct((SLOTS, MW), BF),
            jax.ShapeDtypeStruct((320, HID), BF),
            jax.ShapeDtypeStruct((HID, BW), BF),
        ),
        in_specs=[vm, vm, vm, vm, vm, hb, hb, hb, hb],
        out_specs=(hb, hb, hb),
        scratch_shapes=[
            buf(SLOTS, MW),
            buf(320, HID),
            buf(HID, BW),
            buf(SLOTS, TOK),
            buf(4 * SLOTS, 4 * SLOTS),
            buf(4, 2, SLOTS, D),
            buf(SLOTS, MW),
            buf(MW, HID),
            buf(MW, HID),
            buf(2, 2, 4, HID, BW),
            buf(4, SLOTS, D),
            buf(2, SLOTS, D),
            buf(SLOTS, D),
            buf(8, SLOTS, D),
            buf(8, SLOTS, MW),
            pltpu.VMEM((8, SLOTS, HID), F32),
            pltpu.VMEM((2, 8 * RB, HID), F32),
            buf(HID, ROWS),
            buf(4, 2, SLOTS, HID),
            buf(4, SLOTS, HID),
            buf(2, 2, 4, HID, UW),
            buf(8, 4, HH, UW),
            buf(2, 8, HH // 2, UW),
            buf(2, 8, HH, UW),
            buf(8, HH, UW),
            buf(2, 2, HH, UW),
            buf(2, HH, UW),
            buf(2, SLOTS, MW // 2),
            buf(2, SLOTS, MW),
            buf(2, 4, 320, HID),
            buf(CA // 128, 2, 2, 160, 128),
            buf(CA // 128, 2, 2, 320, 128),
            buf(CA // 128, 320, 128),
            buf(4, 320, HID - CA),
            buf(2, 160, HID - CA),
            buf(2, 320, HID - CA),
            pltpu.SemaphoreType.DMA((MAX_COPIES,)),
            pltpu.SemaphoreType.DMA((MAX_COPIES,)),
            pltpu.SemaphoreType.DMA((88,)),
        ],
        compiler_params=pltpu.CompilerParams(
            collective_id=0, has_side_effects=True, vmem_limit_bytes=63 * 2**20
        ),
        cost_estimate=pl.CostEstimate(
            flops=2 * 512 * 384 * 31744, bytes_accessed=16 * 2**20, transcendentals=400000
        ),
        name="merger_backward",
    )(cnt, own, st, gain, bias, gs, feat, win, wout)


def finish_kernel(a, b, c, ao, bo, co, av, bv, cv, sem):
    ways = [
        (src.at[rows], mid.at[rows], dst.at[rows])
        for src, mid, dst, rows in (
            (a, av, ao, pl.ds(0, 32)), (c, cv, co, pl.ds(0, 384)), (b, bv, bo, pl.ds(0, 320)), (a, av, ao, pl.ds(32, 32))
        )
    ]
    ins = [pltpu.make_async_copy(src, mid, sem.at[n]) for n, (src, mid, _) in enumerate(ways)]
    outs = [pltpu.make_async_copy(mid, dst, sem.at[n + 4]) for n, (_, mid, dst) in enumerate(ways)]
    for cp in ins:
        cp.start()
    for cp, out in zip(ins, outs):
        cp.wait()
        out.start()
    for out in outs:
        out.wait()


def finish_call(*arrays):
    hb = pl.BlockSpec(memory_space=pl.ANY)
    return pl.pallas_call(
        finish_kernel,
        out_shape=tuple(jax.ShapeDtypeStruct(a.shape, a.dtype) for a in arrays),
        in_specs=[hb] * 3,
        out_specs=(hb, hb, hb),
        scratch_shapes=[pltpu.VMEM(a.shape, a.dtype) for a in arrays] + [pltpu.SemaphoreType.DMA((8,))],
        compiler_params=pltpu.CompilerParams(vmem_limit_bytes=63 * 2**20),
        name="write_results",
    )(*arrays)


def local(
    grad_seq, features, merger_norm_gain, w_in, b_in, w_out, image_counts, sample_owner, image_starts
):
    mig, gw1, gw2 = merger_call(
        image_counts, sample_owner, image_starts, merger_norm_gain, b_in,
        grad_seq.reshape(2, 2, SLOTS, D), features[0], w_in, w_out,
    )
    mig, gw1, gw2 = finish_call(mig, gw1, gw2)
    return (mig[None], gw1, gw2)


def solution(mesh):
    in_specs = (
        P("dp", "seq", None),
        P("dp", "seq", None),
        P(),
        P(None, "dp"),
        P("dp"),
        P("dp", None),
        P("dp", None),
        P("dp", None),
        P("dp", None),
    )
    out_specs = (P("dp", "seq", None), P("seq", "dp"), P("dp", "seq"))
    return jax.shard_map(local, mesh=mesh, in_specs=in_specs, out_specs=out_specs, check_vma=False)
```
